512 devices in a mesh: resp: 128 (over z_hi, x, y), tp: 4 (over z_lo, core).
Axes of the slice: x: 4, y: 8, z: 8 (z_hi: 4, z_lo: 2; z = z_hi * 2 + z_lo), core: 2. Of those that a mesh axis runs over, the one named last changes fastest.
Arguments:
- response_queries: bfloat16 [256, 128, 4096], P('resp', None, 'tp'), may hold values from -1000 to 1000
- response_kv: bfloat16 [2, 256, 128, 2048], P(None, 'resp', None, 'tp'), may hold values from -6 to 6
- prompt_kv: bfloat16 [2, 16, 512, 2048], P(None, None, 'resp', 'tp'), may hold values from -16 to 16
- response_lengths: int32 [256], P('resp'), may hold values from 1 to 128, as said below
- device_prompt: int32 [128], replicated, may hold values from 0 to 15, as said below
- probe_weight: float32 [4096], P('tp'), may hold values from -0.5 to 0.5
Outputs:
- context: bfloat16 [256, 128, 4096], P('resp', None, 'tp')
- advantage: float32 [256], P('resp')
The draws below stay inside these ranges and needn't reach their ends.
Inputs may be any that keep to these rules, and one draw needn't show every extreme that they name: `response_lengths`: at least one response has exactly 128 live tokens. `device_prompt`: each prompt index is named by exactly 8 entries.
All inputs are finite; a program needn't handle non-finite values.
Results may differ from the reference program's by a relative error of at most 0.0055.
Values may be sent and summed in bfloat16 or wider, within the bound.
A program may use at most 64 MiB of HBM per device.

```python
import math
import jax
import jax.numpy as jnp
from jax import lax

HEADS = 32
KV_HEADS = 16
HEAD_DIM = 128
SCALAR = 144
BEST = 16
RD = 2
LR = 128
LP = 512
RESPONSES = 256
PROMPTS = 16
N_RESP = 128


def prompt_helper(key):
    key = jax.random.fold_in(key, 11)
    base = jax.random.normal(key, (2, PROMPTS, LP, KV_HEADS * HEAD_DIM), jnp.float32)
    base = base.at[0, :, 1].set(base[0, :, 0])
    return base


def owner_helper(key):
    key = jax.random.fold_in(key, 12)
    order = jax.random.permutation(key, N_RESP)
    return (order // (BEST // RD)).astype(jnp.int32)


def draw_prompt_kv(key, part):
    shared = prompt_helper(key)
    return shared.astype(jnp.bfloat16)


def draw_device_prompt(key, part):
    return owner_helper(key)


def draw_response_queries(key, part):
    key = jax.random.fold_in(key, 5)
    return jax.random.normal(key, (RESPONSES, LR, HEADS * HEAD_DIM), jnp.float32).astype(jnp.bfloat16)


def draw_response_lengths(key, part):
    key = jax.random.fold_in(key, 7)
    lengths = jax.random.randint(key, (RESPONSES,), 1, LR + 1)
    chosen = jax.random.randint(jax.random.fold_in(key, 1), (), 0, RESPONSES)
    return lengths.at[chosen].set(LR).astype(jnp.int32)


def steps_of(own_key, shape, cuts, least, high):
    loudness = 1.0
    for axis_at, shards_of in cuts:
        draws = jax.random.uniform(jax.random.fold_in(jax.random.fold_in(own_key, 6), axis_at), (shards_of,), jnp.float32, least / len(cuts), high / len(cuts))
        loudness = loudness * jnp.repeat(jnp.exp(draws), shape[axis_at] // shards_of).reshape((-1,) + (1,) * (len(shape) - 1 - axis_at))
    return loudness


def scatter_about(rng, dims, width, bound, split=(), kind=jnp.bfloat16):
    result = jax.random.normal(rng, dims, jnp.float32) * width
    if len(split) > 0:
        result = steps_of(rng, dims, split, -0.22, 0.18) * result
    return jnp.clip(result, min=-bound, max=bound).astype(kind)


def setup_inputs(seed: int = 0) -> dict:
    splits = jax.random.split(jax.random.key(seed), 7)
    return {
        "response_queries": draw_response_queries(jax.random.fold_in(splits[6], 71), 0),
        "response_kv": scatter_about(splits[1], (2, RESPONSES, LR, KV_HEADS * HEAD_DIM), 1.0, 6.0, ((1, 128), (3, 4))),
        "prompt_kv": draw_prompt_kv(jax.random.fold_in(splits[6], 71), 0),
        "response_lengths": draw_response_lengths(jax.random.fold_in(splits[6], 71), 0),
        "device_prompt": draw_device_prompt(jax.random.fold_in(splits[6], 71), 0),
        "probe_weight": scatter_about(splits[5], (HEADS * HEAD_DIM,), HEAD_DIM ** -0.5, 0.5, ((0, 4),), jnp.float32),
    }


def reference(response_queries, response_kv, prompt_kv, response_lengths, device_prompt, probe_weight):
    group_size = HEADS // KV_HEADS
    score_scale = 1.0 / math.sqrt(SCALAR)
    prompt_of = jnp.repeat(device_prompt, RD)
    positions = jnp.arange(LR, dtype=jnp.int32)
    causal = positions[None, :] <= positions[:, None]

    def single(operands):
        queries, self_keys, self_values, length, prompt = operands
        prefix = jnp.take(prompt_kv, prompt, axis=1).astype(jnp.float32)
        query_f = queries.astype(jnp.float32).reshape(LR, KV_HEADS, group_size, HEAD_DIM)
        prefix_keys = prefix[0].reshape(LP, KV_HEADS, HEAD_DIM)
        prefix_values = prefix[1].reshape(LP, KV_HEADS, HEAD_DIM)
        keys_f = self_keys.astype(jnp.float32).reshape(LR, KV_HEADS, HEAD_DIM)
        values_f = self_values.astype(jnp.float32).reshape(LR, KV_HEADS, HEAD_DIM)
        prompt_scores = jnp.einsum('tkgd,pkd->tkgp', query_f, prefix_keys) * score_scale
        self_scores = jnp.einsum('tkgd,ukd->tkgu', query_f, keys_f) * score_scale
        visible = causal & (positions[None, :] < length)
        mask = visible[:, None, None, :]
        self_scores = jnp.where(mask, self_scores, -1e+30)
        row_max = jnp.maximum(prompt_scores.max(-1), self_scores.max(-1))
        prompt_exp = jnp.exp(prompt_scores - row_max[..., None])
        self_exp = jnp.where(mask, jnp.exp(self_scores - row_max[..., None]), 0.0)
        denominator = prompt_exp.sum(-1) + self_exp.sum(-1)
        prompt_w = prompt_exp.astype(jnp.bfloat16).astype(jnp.float32)
        self_w = self_exp.astype(jnp.bfloat16).astype(jnp.float32)
        mixed = jnp.einsum('tkgp,pkd->tkgd', prompt_w, prefix_values)
        mixed = mixed + jnp.einsum('tkgu,ukd->tkgd', self_w, values_f)
        mixed = mixed / denominator[..., None]
        mixed = jnp.where(positions[:, None, None, None] < length, mixed, 0.0)
        rounded = mixed.reshape(LR, HEADS * HEAD_DIM).astype(jnp.bfloat16)
        end_row = lax.dynamic_index_in_dim(rounded, (length - 1).astype(jnp.int32), 0, keepdims=False)
        reward = jnp.sum(end_row.astype(jnp.float32) * probe_weight)
        return (rounded, reward)
    context, rewards = lax.map(single, (response_queries, response_kv[0], response_kv[1], response_lengths, prompt_of))
    same_prompt = (prompt_of[:, None] == prompt_of[None, :]).astype(jnp.float32)
    group_mean = lax.optimization_barrier(jnp.sum(same_prompt * rewards[None, :], axis=1)) / BEST
    advantage = rewards - group_mean
    return (context, advantage)
```

```python
import functools
import math

import jax
import jax.numpy as jnp
from jax import lax
from jax.experimental import pallas as pl
from jax.experimental.pallas import tpu as pltpu
from jax.sharding import PartitionSpec as P

HEAD_DIM = 128
SCALAR = 144
BEST = 16
MESH = pl.DeviceIdType.MESH

NZ, NX, NY, NT = 4, 4, 8, 4
NXY, NZX, NZT = NX * NY, NZ * NX, NZ * NT
PROMPTS = 16
TOKENS = 4
PIECES = 4
ROWS = PIECES * TOKENS


def attention(scores_parts, values, scale2):
    top = functools.reduce(jnp.maximum, [jnp.max(s, axis=1, keepdims=True) for s in scores_parts])
    weights = [jnp.exp2((s - top) * scale2) for s in scores_parts]
    total = functools.reduce(jnp.add, [jnp.sum(w, axis=1, keepdims=True) for w in weights])
    mixed = functools.reduce(
        jnp.add,
        [
            jnp.dot(w.astype(jnp.bfloat16), v, preferred_element_type=jnp.float32)
            for w, v in zip(weights, values)
        ],
    )
    return mixed * (1.0 / total)


def scores_of(q, k):
    return lax.dot_general(q, k, (((1,), (1,)), ((), ())), preferred_element_type=jnp.float32)


def kernel(
    lengths,
    prompts,
    probe,
    q_hbm,
    kv_hbm,
    raw_hbm,
    context,
    advantage,
    q,
    kv,
    raw,
    own_a,
    own_b,
    got_a,
    got_b,
    out_a,
    out_b,
    all_a,
    all_b,
    row_1,
    row_2,
    load_sem,
    ring_send,
    ring_recv,
    send_sem,
    recv_sem,
):
    me = lax.axis_index("resp")
    tp = lax.axis_index("tp")
    zh = lax.div(me, NXY)
    xy = lax.rem(me, NXY)
    x = lax.div(xy, NY)
    y = lax.rem(xy, NY)
    zx = zh * NX + x

    def at_xy(j):
        return zh * NXY + j

    def at_zx(j):
        return j * NY + y

    def at_z(step):
        return lax.rem(zh + step, NZ) * NXY + xy

    def at_y(step):
        return zh * NXY + x * NY + lax.rem(y + step, NY)

    load_raw = pltpu.make_async_copy(raw_hbm, raw, load_sem.at[0])
    load_q = pltpu.make_async_copy(q_hbm, q, load_sem.at[1])
    load_kv = pltpu.make_async_copy(kv_hbm, kv, load_sem.at[2])
    load_raw.start()
    load_q.start()
    load_kv.start()

    barrier = pltpu.get_barrier_semaphore()

    def greet(device, tp_index):
        pl.semaphore_signal(barrier, inc=1, device_id=(device, tp_index), device_id_type=MESH)

    def greet_xy(i, c):
        greet(at_xy(lax.rem(xy + i, NXY)), tp)
        return c

    lax.fori_loop(1, NXY, greet_xy, 0)

    def greet_zx(i, c):
        greet(at_zx(lax.rem(zh + 1 + lax.div(i, NX), NZ) * NX + lax.rem(i, NX)), tp)
        return c

    lax.fori_loop(0, (NZ - 1) * NX, greet_zx, 0)

    def greet_tp(i, c):
        greet(lax.div(i, NT - 1) * NXY + xy, lax.rem(tp + 1 + lax.rem(i, NT - 1), NT))
        return c

    lax.fori_loop(0, NZ * (NT - 1), greet_tp, 0)

    load_raw.wait()

    def split(p, c):
        k = raw[0, p].astype(jnp.float32)
        v = raw[1, p].astype(jnp.float32)
        for plan, dst in enumerate((own_a, own_b)):
            parts = [
                part[:, (2 * plan + h) * HEAD_DIM : (2 * plan + h + 1) * HEAD_DIM]
                for part in (k, v)
                for h in range(2)
            ]
            dst[p] = jnp.concatenate(parts, axis=0).astype(jnp.bfloat16)
        return c

    lax.fori_loop(0, PROMPTS, split, 0)

    pl.semaphore_wait(barrier, (NXY - 1) + (NZ - 1) * NX + NZ * (NT - 1))

    half = PROMPTS // 2
    lo, hi = pl.ds(0, half), pl.ds(half, half)

    def ring(index, src, dst, device):
        return pltpu.make_async_remote_copy(
            src_ref=src,
            dst_ref=dst,
            send_sem=ring_send.at[index],
            recv_sem=ring_recv.at[index],
            device_id=(device, tp),
            device_id_type=MESH,
        )

    first = [
        ring(0, own_a, got_a.at[0], at_z(1)),
        ring(1, own_a, got_a.at[1], at_z(NZ - 1)),
        ring(2, own_b, got_b.at[2], at_y(2)),
        ring(3, own_b, got_b.at[3], at_y(NY - 2)),
        ring(4, own_b, got_b.at[0], at_y(1)),
        ring(5, own_b, got_b.at[1], at_y(NY - 1)),
    ]
    second = [
        ring(6, got_a.at[0, lo], got_a.at[2, lo], at_z(1)),
        ring(7, got_a.at[1, hi], got_a.at[2, hi], at_z(NZ - 1)),
        ring(8, got_b.at[2, lo], got_b.at[6, lo], at_y(2)),
        ring(9, got_b.at[2], got_b.at[4], at_y(1)),
        ring(10, got_b.at[3, hi], got_b.at[6, hi], at_y(NY - 2)),
        ring(11, got_b.at[3], got_b.at[5], at_y(NY - 1)),
    ]
    for copy in first:
        copy.start()
    first[0].wait_recv()
    second[0].start()
    first[1].wait_recv()
    second[1].start()
    first[2].wait_recv()
    second[2].start()
    second[3].start()
    first[3].wait_recv()
    second[4].start()
    second[5].start()
    second[0].wait_recv()
    second[1].wait_recv()

    def regroup(tiles):
        tiles = [t.astype(jnp.float32) for t in tiles]
        return [
            jnp.concatenate([t[TOKENS * g : TOKENS * (g + 1)] for t in tiles], axis=0).astype(jnp.bfloat16)
            for g in range(PIECES)
        ]

    def fill_a(dst, slot, p):
        for g, piece in enumerate(regroup([own_a[p]] + [got_a[s, p] for s in range(3)])):
            dst[slot, g] = piece

    def fill_b(dst, slot, p):
        for g, piece in enumerate(regroup([own_b[p]] + [got_b[s, p] for s in range(7)])):
            dst[slot, g] = piece

    def send_a(i, c):
        j = lax.rem(xy + i, NXY)
        fill_a(out_a, i, prompts[at_xy(j)])
        pltpu.make_async_remote_copy(
            src_ref=out_a.at[i],
            dst_ref=all_a.at[xy],
            send_sem=send_sem.at[0],
            recv_sem=recv_sem.at[0],
            device_id=(at_xy(j), tp),
            device_id_type=MESH,
        ).start()
        return c

    def send_b(i, c):
        j = lax.rem(zx + i, NZX)
        fill_b(out_b, i, prompts[at_zx(j)])
        pltpu.make_async_remote_copy(
            src_ref=out_b.at[i],
            dst_ref=all_b.at[zx],
            send_sem=send_sem.at[1],
            recv_sem=recv_sem.at[1],
            device_id=(at_zx(j), tp),
            device_id_type=MESH,
        ).start()
        return c

    lax.fori_loop(1, NXY // 2, send_a, 0)
    first[4].wait_recv()
    first[5].wait_recv()
    for copy in second[2:]:
        copy.wait_recv()

    def send_both(i, c):
        send_b(i, c)
        return send_a(i + NXY // 2 - 1, c)

    lax.fori_loop(1, NZX, send_both, 0)
    send_a(NXY - 1, 0)

    mine = prompts[me]
    fill_a(all_a, xy, mine)
    fill_b(all_b, zx, mine)

    load_q.wait()
    load_kv.wait()
    responses, steps, width = q.shape
    scale2 = math.log2(math.e) / math.sqrt(SCALAR)
    kv_heads = kv.shape[3] // HEAD_DIM
    column = lax.broadcasted_iota(jnp.int32, (8, steps), 1)
    last_q = []
    for r in range(responses):
        pick = (column == lengths[r] - 1).astype(jnp.bfloat16)
        last_q.append(jnp.dot(pick, q[r], preferred_element_type=jnp.float32).astype(jnp.bfloat16))

    def keys_values(g):
        ref = (all_a, all_b)[g // 2]
        h = g % 2
        return (
            ref[:, h].reshape(-1, HEAD_DIM),
            ref[:, 2 + h].reshape(-1, HEAD_DIM),
        )

    def own_keys_values(r, g):
        columns = slice(g * HEAD_DIM, (g + 1) * HEAD_DIM)
        return kv[0, r, :, columns], kv[1, r, :, columns]

    def wait_bytes(ref, sem):
        pltpu.make_async_copy(ref, ref, sem).wait()

    wait_bytes(all_a.at[pl.ds(0, NXY - 1)], recv_sem.at[0])
    wait_bytes(all_b.at[pl.ds(0, NZX - 1)], recv_sem.at[1])

    partial = [jnp.zeros((8, HEAD_DIM), jnp.float32) for _ in range(responses)]
    for g in range(kv_heads):
        k, v = keys_values(g)
        heads = (2 * g, 2 * g + 1)
        for r in range(responses):
            rows = jnp.concatenate(
                [last_q[r][:, h * HEAD_DIM : (h + 1) * HEAD_DIM] for h in heads], axis=0
            )
            own_k, own_v = own_keys_values(r, g)
            own = scores_of(rows, own_k)
            seen = lax.broadcasted_iota(jnp.int32, own.shape, 1) < lengths[r]
            own = jnp.where(seen, own, -1e30)
            mixed = attention([scores_of(rows, k), own], [v, own_v], scale2)
            mixed = mixed.astype(jnp.bfloat16).astype(jnp.float32)
            for n, h in enumerate(heads):
                partial[r] = partial[r] + mixed[8 * n : 8 * n + 8] * probe[h : h + 1, :]

    lane = lax.broadcasted_iota(jnp.int32, (1, HEAD_DIM), 1)
    sums = [jnp.sum(part[0:1], axis=1, keepdims=True) for part in partial]
    row = jnp.where(lane == mine, sums[0] + sums[1], 0.0)
    for r in range(responses):
        row = jnp.where(lane == PROMPTS + r, sums[r], row)

    zt = zh * NT + tp
    row_1[zt] = row

    def send_1(i, c):
        j = lax.rem(zt + i, NZT)
        pltpu.make_async_remote_copy(
            src_ref=row_1.at[zt],
            dst_ref=row_1.at[zt],
            send_sem=send_sem.at[2],
            recv_sem=recv_sem.at[2],
            device_id=(lax.div(j, NT) * NXY + xy, lax.rem(j, NT)),
            device_id_type=MESH,
        ).start()
        return c

    lax.fori_loop(1, NZT, send_1, 0)

    def attend(r, g):
        k, v = keys_values(g)
        own_k, own_v = own_keys_values(r, g)
        low = 2 * g * HEAD_DIM
        rows = jnp.concatenate(
            [q[r, :, low : low + HEAD_DIM], q[r, :, low + HEAD_DIM : low + 2 * HEAD_DIM]], axis=0
        )
        own = scores_of(rows, own_k)
        t = lax.broadcasted_iota(jnp.int32, own.shape, 0)
        t = jnp.where(t >= steps, t - steps, t)
        u = lax.broadcasted_iota(jnp.int32, own.shape, 1)
        own = jnp.where(u <= t, own, -1e30)
        mixed = attention([scores_of(rows, k), own], [v, own_v], scale2)
        live = lax.broadcasted_iota(jnp.int32, (steps, HEAD_DIM), 0) < lengths[r]
        for n in range(2):
            part = jnp.where(live, mixed[n * steps : (n + 1) * steps], 0.0)
            context[r, :, low + n * HEAD_DIM : low + (n + 1) * HEAD_DIM] = part.astype(jnp.bfloat16)

    for g in range(kv_heads // 2):
        for r in range(responses):
            attend(r, g)

    wait_bytes(row_1.at[pl.ds(0, NZT - 1)], recv_sem.at[2])
    line = jnp.sum(row_1[...], axis=0)
    rewards = jnp.sum(row_1[pl.ds(zh * NT, NT)], axis=0)
    row_2[xy] = line

    def send_2(i, c):
        j = lax.rem(xy + i, NXY)
        pltpu.make_async_remote_copy(
            src_ref=row_2.at[xy],
            dst_ref=row_2.at[xy],
            send_sem=send_sem.at[3],
            recv_sem=recv_sem.at[3],
            device_id=(at_xy(j), tp),
            device_id_type=MESH,
        ).start()
        return c

    lax.fori_loop(1, NXY, send_2, 0)

    for g in range(kv_heads // 2, kv_heads):
        for r in range(responses):
            attend(r, g)

    wait_bytes(row_2.at[pl.ds(0, NXY - 1)], recv_sem.at[3])
    table = jnp.sum(row_2[...], axis=0)
    group = jnp.sum(jnp.where(lane == mine, table, 0.0), axis=1, keepdims=True) / BEST
    result = rewards - group
    for r in range(responses):
        advantage[r] = jnp.sum(jnp.where(lane == PROMPTS + r, result, 0.0))

    for copy in first:
        copy.wait_send()
    for copy in second:
        copy.wait_send()
    wait_bytes(out_a.at[pl.ds(1, NXY - 1)], send_sem.at[0])
    wait_bytes(out_b.at[pl.ds(1, NZX - 1)], send_sem.at[1])
    wait_bytes(row_1.at[pl.ds(0, NZT - 1)], send_sem.at[2])
    wait_bytes(row_2.at[pl.ds(0, NXY - 1)], send_sem.at[3])


def shards(response_queries, response_kv, prompt_kv, response_lengths, device_prompt, probe_weight):
    bf16 = jnp.bfloat16
    smem = pl.BlockSpec(memory_space=pltpu.SMEM)
    vmem = pl.BlockSpec(memory_space=pltpu.VMEM)
    anywhere = pl.BlockSpec(memory_space=pl.ANY)
    block = (PROMPTS, ROWS, HEAD_DIM)
    context, advantage = pl.pallas_call(
        kernel,
        out_shape=(
            jax.ShapeDtypeStruct(response_queries.shape, bf16),
            jax.ShapeDtypeStruct(response_lengths.shape, jnp.float32),
        ),
        in_specs=[smem, smem, vmem, anywhere, anywhere, anywhere],
        out_specs=(vmem, smem),
        scratch_shapes=[
            pltpu.VMEM(response_queries.shape, bf16),
            pltpu.VMEM(response_kv.shape, bf16),
            pltpu.VMEM(prompt_kv.shape, bf16),
            pltpu.VMEM(block, bf16),
            pltpu.VMEM(block, bf16),
            pltpu.VMEM((NZ - 1,) + block, bf16),
            pltpu.VMEM((NY - 1,) + block, bf16),
            pltpu.VMEM((NXY, PIECES, NZ * TOKENS, HEAD_DIM), bf16),
            pltpu.VMEM((NZX, PIECES, NY * TOKENS, HEAD_DIM), bf16),
            pltpu.VMEM((NXY, PIECES, NZ * TOKENS, HEAD_DIM), bf16),
            pltpu.VMEM((NZX, PIECES, NY * TOKENS, HEAD_DIM), bf16),
            pltpu.VMEM((NZT, 1, HEAD_DIM), jnp.float32),
            pltpu.VMEM((NXY, 1, HEAD_DIM), jnp.float32),
            pltpu.SemaphoreType.DMA((3,)),
            pltpu.SemaphoreType.DMA((12,)),
            pltpu.SemaphoreType.DMA((12,)),
            pltpu.SemaphoreType.DMA((4,)),
            pltpu.SemaphoreType.DMA((4,)),
        ],
        compiler_params=pltpu.CompilerParams(
            collective_id=0, has_side_effects=True, vmem_limit_bytes=60 * 1024 * 1024
        ),
        cost_estimate=pl.CostEstimate(
            flops=700_000_000, bytes_accessed=2_000_000, transcendentals=1_400_000
        ),
    )(
        response_lengths,
        device_prompt,
        probe_weight.reshape(-1, HEAD_DIM),
        response_queries,
        response_kv,
        prompt_kv,
    )
    return context, advantage


def solution(mesh):
    placed = (
        P("resp", None, "tp"),
        P(None, "resp", None, "tp"),
        P(None, None, "resp", "tp"),
        P("resp"),
        P(),
        P("tp"),
    )
    return jax.shard_map(
        shards,
        mesh=mesh,
        in_specs=placed,
        out_specs=(P("resp", None, "tp"), P("resp")),
        check_vma=False,
    )
```

```python
import functools
import math

import jax
import jax.numpy as jnp
from jax import lax
from jax.experimental import pallas as pl
from jax.experimental.pallas import tpu as pltpu
from jax.sharding import PartitionSpec as P

HEAD_DIM = 128
SCALAR = 144
BEST = 16
MESH = pl.DeviceIdType.MESH

NZ, NX, NY, NT = 4, 4, 8, 4
NXY, NZX, NZT = NX * NY, NZ * NX, NZ * NT
PROMPTS = 16
TOKENS = 4
PIECES = 4
ROWS = PIECES * TOKENS


def attention(scores_parts, values, scale2):
    top = functools.reduce(jnp.maximum, [jnp.max(s, axis=1, keepdims=True) for s in scores_parts])
    weights = [jnp.exp2((s - top) * scale2) for s in scores_parts]
    total = functools.reduce(jnp.add, [jnp.sum(w, axis=1, keepdims=True) for w in weights])
    mixed = functools.reduce(
        jnp.add,
        [
            jnp.dot(w.astype(jnp.bfloat16), v, preferred_element_type=jnp.float32)
            for w, v in zip(weights, values)
        ],
    )
    return mixed * (1.0 / total)


def scores_of(q, k):
    return lax.dot_general(q, k, (((1,), (1,)), ((), ())), preferred_element_type=jnp.float32)


def kernel(
    lengths,
    prompts,
    probe,
    q_hbm,
    kv_hbm,
    raw_hbm,
    context,
    advantage,
    q,
    kv,
    raw,
    own_a,
    own_b,
    got_a,
    got_b,
    by_prompt_a,
    by_prompt_b,
    out_a,
    out_b,
    all_a,
    all_b,
    row_1,
    row_2,
    load_sem,
    ring_send,
    ring_recv,
    send_sem,
    recv_sem,
):
    me = lax.axis_index("resp")
    tp = lax.axis_index("tp")
    zh = lax.div(me, NXY)
    xy = lax.rem(me, NXY)
    x = lax.div(xy, NY)
    y = lax.rem(xy, NY)
    zx = zh * NX + x

    def at_xy(j):
        return zh * NXY + j

    def at_zx(j):
        return j * NY + y

    def at_z(step):
        return lax.rem(zh + step, NZ) * NXY + xy

    def at_y(step):
        return zh * NXY + x * NY + lax.rem(y + step, NY)

    load_raw = pltpu.make_async_copy(raw_hbm, raw, load_sem.at[0])
    load_q = pltpu.make_async_copy(q_hbm, q, load_sem.at[1])
    load_kv = pltpu.make_async_copy(kv_hbm, kv, load_sem.at[2])
    load_raw.start()
    load_q.start()
    load_kv.start()

    barrier = pltpu.get_barrier_semaphore()

    def greet(device, tp_index):
        pl.semaphore_signal(barrier, inc=1, device_id=(device, tp_index), device_id_type=MESH)

    def greet_xy(i, c):
        greet(at_xy(lax.rem(xy + i, NXY)), tp)
        return c

    lax.fori_loop(1, NXY, greet_xy, 0)

    def greet_zx(i, c):
        greet(at_zx(lax.rem(zh + 1 + lax.div(i, NX), NZ) * NX + lax.rem(i, NX)), tp)
        return c

    lax.fori_loop(0, (NZ - 1) * NX, greet_zx, 0)

    def greet_tp(i, c):
        greet(lax.div(i, NT - 1) * NXY + xy, lax.rem(tp + 1 + lax.rem(i, NT - 1), NT))
        return c

    lax.fori_loop(0, NZ * (NT - 1), greet_tp, 0)

    load_raw.wait()

    def split(p, c):
        k = raw[0, p].astype(jnp.float32)
        v = raw[1, p].astype(jnp.float32)
        for plan, dst in enumerate((own_a, own_b)):
            parts = [
                part[:, (2 * plan + h) * HEAD_DIM : (2 * plan + h + 1) * HEAD_DIM]
                for part in (k, v)
                for h in range(2)
            ]
            dst[p] = jnp.concatenate(parts, axis=0).astype(jnp.bfloat16)
        return c

    lax.fori_loop(0, PROMPTS, split, 0)

    pl.semaphore_wait(barrier, (NXY - 1) + (NZ - 1) * NX + NZ * (NT - 1))

    half = PROMPTS // 2
    lo, hi = pl.ds(0, half), pl.ds(half, half)

    def ring(index, src, dst, device):
        return pltpu.make_async_remote_copy(
            src_ref=src,
            dst_ref=dst,
            send_sem=ring_send.at[index],
            recv_sem=ring_recv.at[index],
            device_id=(device, tp),
            device_id_type=MESH,
        )

    first = [
        ring(0, own_a, got_a.at[0], at_z(1)),
        ring(1, own_a, got_a.at[1], at_z(NZ - 1)),
        ring(2, own_b, got_b.at[2], at_y(2)),
        ring(3, own_b, got_b.at[3], at_y(NY - 2)),
        ring(4, own_b, got_b.at[0], at_y(1)),
        ring(5, own_b, got_b.at[1], at_y(NY - 1)),
    ]
    second = [
        ring(6, got_a.at[0, lo], got_a.at[2, lo], at_z(1)),
        ring(7, got_a.at[1, hi], got_a.at[2, hi], at_z(NZ - 1)),
        ring(8, got_b.at[2, lo], got_b.at[6, lo], at_y(2)),
        ring(9, got_b.at[2], got_b.at[4], at_y(1)),
        ring(10, got_b.at[3, hi], got_b.at[6, hi], at_y(NY - 2)),
        ring(11, got_b.at[3], got_b.at[5], at_y(NY - 1)),
    ]
    for copy in first:
        copy.start()
    first[0].wait_recv()
    second[0].start()
    first[1].wait_recv()
    second[1].start()
    first[2].wait_recv()
    second[2].start()
    second[3].start()
    first[3].wait_recv()
    second[4].start()
    second[5].start()
    second[0].wait_recv()
    second[1].wait_recv()

    def regroup(own, got, slots, dst):
        def one(p, c):
            tiles = [own[p]] + [got[s, p] for s in range(slots)]
            tiles = [t.astype(jnp.float32) for t in tiles]
            for g in range(PIECES):
                rows = [t[TOKENS * g : TOKENS * (g + 1)] for t in tiles]
                dst[p, g] = jnp.concatenate(rows, axis=0).astype(jnp.bfloat16)
            return c

        def four(i, c):
            for n in range(4):
                one(4 * i + n, c)
            return c

        lax.fori_loop(0, PROMPTS // 4, four, 0)

    def send(offsets_a, offsets_b):
        places_a = [lax.rem(xy + i, NXY) for i in offsets_a]
        places_b = [lax.rem(zx + i, NZX) for i in offsets_b]
        blocks_b = [by_prompt_b[prompts[at_zx(j)]] for j in places_b]
        blocks_a = [by_prompt_a[prompts[at_xy(j)]] for j in places_a]
        for i, block in zip(offsets_b, blocks_b):
            out_b[i] = block
        for i, block in zip(offsets_a, blocks_a):
            out_a[i] = block
        for i, j in zip(offsets_b, places_b):
            pltpu.make_async_remote_copy(
                src_ref=out_b.at[i],
                dst_ref=all_b.at[zx],
                send_sem=send_sem.at[1],
                recv_sem=recv_sem.at[1],
                device_id=(at_zx(j), tp),
                device_id_type=MESH,
            ).start()
        for i, j in zip(offsets_a, places_a):
            pltpu.make_async_remote_copy(
                src_ref=out_a.at[i],
                dst_ref=all_a.at[xy],
                send_sem=send_sem.at[0],
                recv_sem=recv_sem.at[0],
                device_id=(at_xy(j), tp),
                device_id_type=MESH,
            ).start()

    regroup(own_a, got_a, NZ - 1, by_prompt_a)

    def send_all_a(i, c):
        send([6 * i + 1 + n for n in range(6)], [])
        return c

    lax.fori_loop(0, 5, send_all_a, 0)
    send([NXY - 1], [])
    first[4].wait_recv()
    first[5].wait_recv()
    for copy in second[2:]:
        copy.wait_recv()
    regroup(own_b, got_b, NY - 1, by_prompt_b)

    def send_all_b(i, c):
        send([], [5 * i + 1 + n for n in range(5)])
        return c

    lax.fori_loop(0, 3, send_all_b, 0)

    mine = prompts[me]
    all_a[xy] = by_prompt_a[mine]
    all_b[zx] = by_prompt_b[mine]

    load_q.wait()
    load_kv.wait()
    responses, steps, width = q.shape
    scale2 = math.log2(math.e) / math.sqrt(SCALAR)
    kv_heads = kv.shape[3] // HEAD_DIM
    column = lax.broadcasted_iota(jnp.int32, (8, steps), 1)
    last_q = []
    for r in range(responses):
        pick = (column == lengths[r] - 1).astype(jnp.bfloat16)
        last_q.append(jnp.dot(pick, q[r], preferred_element_type=jnp.float32).astype(jnp.bfloat16))

    def keys_values(g):
        ref = (all_a, all_b)[g // 2]
        h = g % 2
        return (
            ref[:, h].reshape(-1, HEAD_DIM),
            ref[:, 2 + h].reshape(-1, HEAD_DIM),
        )

    def own_keys_values(r, g):
        columns = slice(g * HEAD_DIM, (g + 1) * HEAD_DIM)
        return kv[0, r, :, columns], kv[1, r, :, columns]

    def wait_bytes(ref, sem):
        pltpu.make_async_copy(ref, ref, sem).wait()

    partial = [jnp.zeros((8, HEAD_DIM), jnp.float32) for _ in range(responses)]

    def reward_of(g):
        k, v = keys_values(g)
        heads = (2 * g, 2 * g + 1)
        for r in range(responses):
            rows = jnp.concatenate(
                [last_q[r][:, h * HEAD_DIM : (h + 1) * HEAD_DIM] for h in heads], axis=0
            )
            own_k, own_v = own_keys_values(r, g)
            own = scores_of(rows, own_k)
            seen = lax.broadcasted_iota(jnp.int32, own.shape, 1) < lengths[r]
            own = jnp.where(seen, own, -1e30)
            mixed = attention([scores_of(rows, k), own], [v, own_v], scale2)
            mixed = mixed.astype(jnp.bfloat16).astype(jnp.float32)
            for n, h in enumerate(heads):
                partial[r] = partial[r] + mixed[8 * n : 8 * n + 8] * probe[h : h + 1, :]

    def attend(r, g):
        k, v = keys_values(g)
        own_k, own_v = own_keys_values(r, g)
        low = 2 * g * HEAD_DIM
        rows = jnp.concatenate(
            [q[r, :, low : low + HEAD_DIM], q[r, :, low + HEAD_DIM : low + 2 * HEAD_DIM]], axis=0
        )
        own = scores_of(rows, own_k)
        t = lax.broadcasted_iota(jnp.int32, own.shape, 0)
        t = jnp.where(t >= steps, t - steps, t)
        u = lax.broadcasted_iota(jnp.int32, own.shape, 1)
        own = jnp.where(u <= t, own, -1e30)
        mixed = attention([scores_of(rows, k), own], [v, own_v], scale2)
        live = lax.broadcasted_iota(jnp.int32, (steps, HEAD_DIM), 0) < lengths[r]
        for n in range(2):
            part = jnp.where(live, mixed[n * steps : (n + 1) * steps], 0.0)
            context[r, :, low + n * HEAD_DIM : low + (n + 1) * HEAD_DIM] = part.astype(jnp.bfloat16)

    wait_bytes(all_a.at[pl.ds(0, NXY - 1)], recv_sem.at[0])
    for g in range(2):
        reward_of(g)
    for g in range(2):
        for r in range(responses):
            attend(r, g)

    wait_bytes(all_b.at[pl.ds(0, NZX - 1)], recv_sem.at[1])
    for g in range(2, kv_heads):
        reward_of(g)

    lane = lax.broadcasted_iota(jnp.int32, (1, HEAD_DIM), 1)
    sums = [jnp.sum(part[0:1], axis=1, keepdims=True) for part in partial]
    row = jnp.where(lane == mine, sums[0] + sums[1], 0.0)
    for r in range(responses):
        row = jnp.where(lane == PROMPTS + r, sums[r], row)

    zt = zh * NT + tp
    row_1[zt] = row

    for i in range(1, NZT):
        j = lax.rem(zt + i, NZT)
        pltpu.make_async_remote_copy(
            src_ref=row_1.at[zt],
            dst_ref=row_1.at[zt],
            send_sem=send_sem.at[2],
            recv_sem=recv_sem.at[2],
            device_id=(lax.div(j, NT) * NXY + xy, lax.rem(j, NT)),
            device_id_type=MESH,
        ).start()

    for r in range(responses):
        attend(r, 2)

    wait_bytes(row_1.at[pl.ds(0, NZT - 1)], recv_sem.at[2])
    line = jnp.sum(row_1[...], axis=0)
    rewards = jnp.sum(row_1[pl.ds(zh * NT, NT)], axis=0)
    row_2[xy] = line

    for i in range(1, NXY):
        j = lax.rem(xy + i, NXY)
        pltpu.make_async_remote_copy(
            src_ref=row_2.at[xy],
            dst_ref=row_2.at[xy],
            send_sem=send_sem.at[3],
            recv_sem=recv_sem.at[3],
            device_id=(at_xy(j), tp),
            device_id_type=MESH,
        ).start()

    for r in range(responses):
        attend(r, 3)

    wait_bytes(row_2.at[pl.ds(0, NXY - 1)], recv_sem.at[3])
    table = jnp.sum(row_2[...], axis=0)
    group = jnp.sum(jnp.where(lane == mine, table, 0.0), axis=1, keepdims=True) / BEST
    result = rewards - group
    for r in range(responses):
        advantage[r] = jnp.sum(jnp.where(lane == PROMPTS + r, result, 0.0))

    for copy in first:
        copy.wait_send()
    for copy in second:
        copy.wait_send()
    wait_bytes(out_a.at[pl.ds(1, NXY - 1)], send_sem.at[0])
    wait_bytes(out_b.at[pl.ds(1, NZX - 1)], send_sem.at[1])
    wait_bytes(row_1.at[pl.ds(0, NZT - 1)], send_sem.at[2])
    wait_bytes(row_2.at[pl.ds(0, NXY - 1)], send_sem.at[3])


def shards(response_queries, response_kv, prompt_kv, response_lengths, device_prompt, probe_weight):
    bf16 = jnp.bfloat16
    smem = pl.BlockSpec(memory_space=pltpu.SMEM)
    vmem = pl.BlockSpec(memory_space=pltpu.VMEM)
    anywhere = pl.BlockSpec(memory_space=pl.ANY)
    in_hbm = functools.partial(pltpu.with_memory_space_constraint, memory_space=pltpu.HBM)
    block = (PROMPTS, ROWS, HEAD_DIM)
    context, advantage = pl.pallas_call(
        kernel,
        out_shape=(
            pltpu.VMEM(response_queries.shape, bf16),
            jax.ShapeDtypeStruct(response_lengths.shape, jnp.float32),
        ),
        in_specs=[smem, smem, vmem, anywhere, anywhere, anywhere],
        out_specs=(vmem, smem),
        scratch_shapes=[
            pltpu.VMEM(response_queries.shape, bf16),
            pltpu.VMEM(response_kv.shape, bf16),
            pltpu.VMEM(prompt_kv.shape, bf16),
            pltpu.VMEM(block, bf16),
            pltpu.VMEM(block, bf16),
            pltpu.VMEM((NZ - 1,) + block, bf16),
            pltpu.VMEM((NY - 1,) + block, bf16),
            pltpu.VMEM((PROMPTS, PIECES, NZ * TOKENS, HEAD_DIM), bf16),
            pltpu.VMEM((PROMPTS, PIECES, NY * TOKENS, HEAD_DIM), bf16),
            pltpu.VMEM((NXY, PIECES, NZ * TOKENS, HEAD_DIM), bf16),
            pltpu.VMEM((NZX, PIECES, NY * TOKENS, HEAD_DIM), bf16),
            pltpu.VMEM((NXY, PIECES, NZ * TOKENS, HEAD_DIM), bf16),
            pltpu.VMEM((NZX, PIECES, NY * TOKENS, HEAD_DIM), bf16),
            pltpu.VMEM((NZT, 1, HEAD_DIM), jnp.float32),
            pltpu.VMEM((NXY, 1, HEAD_DIM), jnp.float32),
            pltpu.SemaphoreType.DMA((3,)),
            pltpu.SemaphoreType.DMA((12,)),
            pltpu.SemaphoreType.DMA((12,)),
            pltpu.SemaphoreType.DMA((4,)),
            pltpu.SemaphoreType.DMA((4,)),
        ],
        compiler_params=pltpu.CompilerParams(
            collective_id=0, has_side_effects=True, vmem_limit_bytes=48 * 1024 * 1024
        ),
        cost_estimate=pl.CostEstimate(
            flops=700_000_000, bytes_accessed=2_000_000, transcendentals=1_400_000
        ),
    )(
        in_hbm(response_lengths),
        in_hbm(device_prompt),
        in_hbm(probe_weight.reshape(-1, HEAD_DIM)),
        in_hbm(response_queries),
        in_hbm(response_kv),
        in_hbm(prompt_kv),
    )
    return context, advantage


def solution(mesh):
    placed = (
        P("resp", None, "tp"),
        P(None, "resp", None, "tp"),
        P(None, None, "resp", "tp"),
        P("resp"),
        P(),
        P("tp"),
    )
    return jax.shard_map(
        shards,
        mesh=mesh,
        in_specs=placed,
        out_specs=(P("resp", None, "tp"), P("resp")),
        check_vma=False,
    )
```

```python
import functools
import math

import jax
import jax.numpy as jnp
from jax import lax
from jax.experimental import pallas as pl
from jax.experimental.pallas import tpu as pltpu
from jax.sharding import PartitionSpec as P

HEAD_DIM = 128
SCALAR = 144
BEST = 16
MESH = pl.DeviceIdType.MESH

NZ, NX, NY, NT = 4, 4, 8, 4
NXY, NZX, NZT = NX * NY, NZ * NX, NZ * NT
PROMPTS = 16
TOKENS = 4
PIECES = 4
ROWS = PIECES * TOKENS


def attention(scores_parts, values, scale2):
    top = functools.reduce(jnp.maximum, [jnp.max(s, axis=1, keepdims=True) for s in scores_parts])
    weights = [jnp.exp2((s - top) * scale2) for s in scores_parts]
    total = functools.reduce(jnp.add, [jnp.sum(w, axis=1, keepdims=True) for w in weights])
    mixed = functools.reduce(
        jnp.add,
        [
            jnp.dot(w.astype(jnp.bfloat16), v, preferred_element_type=jnp.float32)
            for w, v in zip(weights, values)
        ],
    )
    return mixed * (1.0 / total)


def wait_bytes(ref, sem):
    pltpu.make_async_copy(ref, ref, sem).wait()


def scores_of(q, k):
    return lax.dot_general(q, k, (((1,), (1,)), ((), ())), preferred_element_type=jnp.float32)


def gather_kernel(
    prompts,
    raw_hbm,
    all_a,
    all_b,
    raw,
    own_a,
    own_b,
    got_a,
    got_b,
    by_prompt_a,
    by_prompt_b,
    out_a,
    out_b,
    load_sem,
    ring_send,
    ring_recv,
    send_sem,
    recv_sem,
):
    me = lax.axis_index("resp")
    tp = lax.axis_index("tp")
    zh = lax.div(me, NXY)
    xy = lax.rem(me, NXY)
    x = lax.div(xy, NY)
    y = lax.rem(xy, NY)
    zx = zh * NX + x

    def at_xy(j):
        return zh * NXY + j

    def at_zx(j):
        return j * NY + y

    def at_z(step):
        return lax.rem(zh + step, NZ) * NXY + xy

    def at_y(step):
        return zh * NXY + x * NY + lax.rem(y + step, NY)

    load_raw = pltpu.make_async_copy(raw_hbm, raw, load_sem.at[0])
    load_raw.start()

    barrier = pltpu.get_barrier_semaphore()

    def greet(device, tp_index):
        pl.semaphore_signal(barrier, inc=1, device_id=(device, tp_index), device_id_type=MESH)

    def greet_xy(i, c):
        greet(at_xy(lax.rem(xy + i, NXY)), tp)
        return c

    lax.fori_loop(1, NXY, greet_xy, 0)

    def greet_zx(i, c):
        greet(at_zx(lax.rem(zh + 1 + lax.div(i, NX), NZ) * NX + lax.rem(i, NX)), tp)
        return c

    lax.fori_loop(0, (NZ - 1) * NX, greet_zx, 0)

    load_raw.wait()

    def split(p, c):
        k = raw[0, p].astype(jnp.float32)
        v = raw[1, p].astype(jnp.float32)
        for plan, dst in enumerate((own_a, own_b)):
            parts = [
                part[:, (2 * plan + h) * HEAD_DIM : (2 * plan + h + 1) * HEAD_DIM]
                for part in (k, v)
                for h in range(2)
            ]
            dst[p] = jnp.concatenate(parts, axis=0).astype(jnp.bfloat16)
        return c

    lax.fori_loop(0, PROMPTS, split, 0)

    pl.semaphore_wait(barrier, (NXY - 1) + (NZ - 1) * NX)

    half = PROMPTS // 2
    lo, hi = pl.ds(0, half), pl.ds(half, half)

    def ring(index, src, dst, device):
        return pltpu.make_async_remote_copy(
            src_ref=src,
            dst_ref=dst,
            send_sem=ring_send.at[index],
            recv_sem=ring_recv.at[index],
            device_id=(device, tp),
            device_id_type=MESH,
        )

    first = [
        ring(0, own_a, got_a.at[0], at_z(1)),
        ring(1, own_a, got_a.at[1], at_z(NZ - 1)),
        ring(2, own_b, got_b.at[2], at_y(2)),
        ring(3, own_b, got_b.at[3], at_y(NY - 2)),
        ring(4, own_b, got_b.at[0], at_y(1)),
        ring(5, own_b, got_b.at[1], at_y(NY - 1)),
    ]
    second = [
        ring(6, got_a.at[0, lo], got_a.at[2, lo], at_z(1)),
        ring(7, got_a.at[1, hi], got_a.at[2, hi], at_z(NZ - 1)),
        ring(8, got_b.at[2, lo], got_b.at[6, lo], at_y(2)),
        ring(9, got_b.at[2], got_b.at[4], at_y(1)),
        ring(10, got_b.at[3, hi], got_b.at[6, hi], at_y(NY - 2)),
        ring(11, got_b.at[3], got_b.at[5], at_y(NY - 1)),
    ]
    for copy in first:
        copy.start()
    first[0].wait_recv()
    second[0].start()
    first[1].wait_recv()
    second[1].start()
    first[2].wait_recv()
    second[2].start()
    second[3].start()
    first[3].wait_recv()
    second[4].start()
    second[5].start()
    second[0].wait_recv()
    second[1].wait_recv()

    def regroup(own, got, slots, dst):
        def one(p, c):
            tiles = [own[p]] + [got[s, p] for s in range(slots)]
            tiles = [t.astype(jnp.float32) for t in tiles]
            for g in range(PIECES):
                rows = [t[TOKENS * g : TOKENS * (g + 1)] for t in tiles]
                dst[p, g] = jnp.concatenate(rows, axis=0).astype(jnp.bfloat16)
            return c

        def four(i, c):
            for n in range(4):
                one(4 * i + n, c)
            return c

        lax.fori_loop(0, PROMPTS // 4, four, 0)

    def send(offsets_a, offsets_b):
        places_a = [lax.rem(xy + i, NXY) for i in offsets_a]
        places_b = [lax.rem(zx + i, NZX) for i in offsets_b]
        blocks_b = [by_prompt_b[prompts[at_zx(j)]] for j in places_b]
        blocks_a = [by_prompt_a[prompts[at_xy(j)]] for j in places_a]
        for i, block in zip(offsets_b, blocks_b):
            out_b[i] = block
        for i, block in zip(offsets_a, blocks_a):
            out_a[i] = block
        for i, j in zip(offsets_b, places_b):
            pltpu.make_async_remote_copy(
                src_ref=out_b.at[i],
                dst_ref=all_b.at[zx],
                send_sem=send_sem.at[1],
                recv_sem=recv_sem.at[1],
                device_id=(at_zx(j), tp),
                device_id_type=MESH,
            ).start()
        for i, j in zip(offsets_a, places_a):
            pltpu.make_async_remote_copy(
                src_ref=out_a.at[i],
                dst_ref=all_a.at[xy],
                send_sem=send_sem.at[0],
                recv_sem=recv_sem.at[0],
                device_id=(at_xy(j), tp),
                device_id_type=MESH,
            ).start()

    regroup(own_a, got_a, NZ - 1, by_prompt_a)

    def send_all_a(i, c):
        send([6 * i + 1 + n for n in range(6)], [])
        return c

    lax.fori_loop(0, 5, send_all_a, 0)
    send([NXY - 1], [])
    first[4].wait_recv()
    first[5].wait_recv()
    for copy in second[2:]:
        copy.wait_recv()
    regroup(own_b, got_b, NY - 1, by_prompt_b)

    def send_all_b(i, c):
        send([], [5 * i + 1 + n for n in range(5)])
        return c

    lax.fori_loop(0, 3, send_all_b, 0)

    mine = prompts[me]
    all_a[xy] = by_prompt_a[mine]
    all_b[zx] = by_prompt_b[mine]

    wait_bytes(all_a.at[pl.ds(0, NXY - 1)], recv_sem.at[0])
    wait_bytes(all_b.at[pl.ds(0, NZX - 1)], recv_sem.at[1])
    for copy in first:
        copy.wait_send()
    for copy in second:
        copy.wait_send()
    wait_bytes(out_a.at[pl.ds(1, NXY - 1)], send_sem.at[0])
    wait_bytes(out_b.at[pl.ds(1, NZX - 1)], send_sem.at[1])


def attention_kernel(lengths, probe, q, kv, all_a, all_b, context, reward):
    responses, steps, width = q.shape
    scale2 = math.log2(math.e) / math.sqrt(SCALAR)
    kv_heads = kv.shape[3] // HEAD_DIM
    place = lax.broadcasted_iota(jnp.int32, (steps, HEAD_DIM), 0)
    sums = [jnp.zeros((1, HEAD_DIM), jnp.float32) for _ in range(responses)]
    for g in range(kv_heads):
        blocks, h = (all_a, all_b)[g // 2], g % 2
        k = blocks[:, h].reshape(-1, HEAD_DIM)
        v = blocks[:, 2 + h].reshape(-1, HEAD_DIM)
        columns = slice(g * HEAD_DIM, (g + 1) * HEAD_DIM)
        for r in range(responses):
            low = 2 * g * HEAD_DIM
            rows = jnp.concatenate(
                [q[r, :, low : low + HEAD_DIM], q[r, :, low + HEAD_DIM : low + 2 * HEAD_DIM]], axis=0
            )
            own = scores_of(rows, kv[0, r, :, columns])
            t = lax.broadcasted_iota(jnp.int32, own.shape, 0)
            t = jnp.where(t >= steps, t - steps, t)
            u = lax.broadcasted_iota(jnp.int32, own.shape, 1)
            own = jnp.where(u <= t, own, -1e30)
            mixed = attention([scores_of(rows, k), own], [v, kv[1, r, :, columns]], scale2)
            for n in range(2):
                part = mixed[n * steps : (n + 1) * steps]
                part = jnp.where(place < lengths[r], part, 0.0).astype(jnp.bfloat16)
                context[r, :, low + n * HEAD_DIM : low + (n + 1) * HEAD_DIM] = part
                last = jnp.where(place == lengths[r] - 1, part.astype(jnp.float32), 0.0)
                last = jnp.sum(last, axis=0, keepdims=True)
                sums[r] = sums[r] + last * probe[2 * g + n : 2 * g + n + 1, :]
    for r in range(responses):
        reward[r] = sums[r]


def reward_kernel(prompts, reward, advantage, row_1, row_2, send_sem, recv_sem):
    responses = reward.shape[0]
    me = lax.axis_index("resp")
    tp = lax.axis_index("tp")
    zh = lax.div(me, NXY)
    xy = lax.rem(me, NXY)
    zt = zh * NT + tp
    mine = prompts[me]

    def at_xy(j):
        return zh * NXY + j

    def at_zt(j):
        return (lax.div(j, NT) * NXY + xy, lax.rem(j, NT))

    barrier = pltpu.get_barrier_semaphore()
    for i in range(1, NZT):
        device = at_zt(lax.rem(zt + i, NZT))
        pl.semaphore_signal(barrier, inc=1, device_id=device, device_id_type=MESH)
    for i in range(1, NXY):
        device = (at_xy(lax.rem(xy + i, NXY)), tp)
        pl.semaphore_signal(barrier, inc=1, device_id=device, device_id_type=MESH)

    lane = lax.broadcasted_iota(jnp.int32, (1, HEAD_DIM), 1)
    sums = [jnp.sum(reward[r], axis=1, keepdims=True) for r in range(responses)]
    row = jnp.where(lane == mine, sums[0] + sums[1], 0.0)
    for r in range(responses):
        row = jnp.where(lane == PROMPTS + r, sums[r], row)

    row_1[zt] = row
    pl.semaphore_wait(barrier, (NZT - 1) + (NXY - 1))

    for i in range(1, NZT):
        pltpu.make_async_remote_copy(
            src_ref=row_1.at[zt],
            dst_ref=row_1.at[zt],
            send_sem=send_sem.at[0],
            recv_sem=recv_sem.at[0],
            device_id=at_zt(lax.rem(zt + i, NZT)),
            device_id_type=MESH,
        ).start()

    wait_bytes(row_1.at[pl.ds(0, NZT - 1)], recv_sem.at[0])
    line = jnp.sum(row_1[...], axis=0)
    rewards = jnp.sum(row_1[pl.ds(zh * NT, NT)], axis=0)
    row_2[xy] = line

    for i in range(1, NXY):
        j = lax.rem(xy + i, NXY)
        pltpu.make_async_remote_copy(
            src_ref=row_2.at[xy],
            dst_ref=row_2.at[xy],
            send_sem=send_sem.at[1],
            recv_sem=recv_sem.at[1],
            device_id=(at_xy(j), tp),
            device_id_type=MESH,
        ).start()

    wait_bytes(row_2.at[pl.ds(0, NXY - 1)], recv_sem.at[1])
    table = jnp.sum(row_2[...], axis=0)
    group = jnp.sum(jnp.where(lane == mine, table, 0.0), axis=1, keepdims=True) / BEST
    result = rewards - group
    for r in range(responses):
        advantage[r] = jnp.sum(jnp.where(lane == PROMPTS + r, result, 0.0))

    wait_bytes(row_1.at[pl.ds(0, NZT - 1)], send_sem.at[0])
    wait_bytes(row_2.at[pl.ds(0, NXY - 1)], send_sem.at[1])


def shards(response_queries, response_kv, prompt_kv, response_lengths, device_prompt, probe_weight):
    bf16 = jnp.bfloat16
    smem = pl.BlockSpec(memory_space=pltpu.SMEM)
    vmem = pl.BlockSpec(memory_space=pltpu.VMEM)
    anywhere = pl.BlockSpec(memory_space=pl.ANY)
    in_hbm = functools.partial(pltpu.with_memory_space_constraint, memory_space=pltpu.HBM)
    in_vmem = functools.partial(pltpu.with_memory_space_constraint, memory_space=pltpu.VMEM)
    block = (PROMPTS, ROWS, HEAD_DIM)
    blocks_a = (NXY, PIECES, NZ * TOKENS, HEAD_DIM)
    blocks_b = (NZX, PIECES, NY * TOKENS, HEAD_DIM)
    all_a, all_b = pl.pallas_call(
        gather_kernel,
        out_shape=(pltpu.VMEM(blocks_a, bf16), pltpu.VMEM(blocks_b, bf16)),
        in_specs=[smem, anywhere],
        out_specs=(vmem, vmem),
        scratch_shapes=[
            pltpu.VMEM(prompt_kv.shape, bf16),
            pltpu.VMEM(block, bf16),
            pltpu.VMEM(block, bf16),
            pltpu.VMEM((NZ - 1,) + block, bf16),
            pltpu.VMEM((NY - 1,) + block, bf16),
            pltpu.VMEM((PROMPTS,) + blocks_a[1:], bf16),
            pltpu.VMEM((PROMPTS,) + blocks_b[1:], bf16),
            pltpu.VMEM(blocks_a, bf16),
            pltpu.VMEM(blocks_b, bf16),
            pltpu.SemaphoreType.DMA((1,)),
            pltpu.SemaphoreType.DMA((12,)),
            pltpu.SemaphoreType.DMA((12,)),
            pltpu.SemaphoreType.DMA((2,)),
            pltpu.SemaphoreType.DMA((2,)),
        ],
        compiler_params=pltpu.CompilerParams(
            collective_id=0, has_side_effects=True, vmem_limit_bytes=32 * 1024 * 1024
        ),
        cost_estimate=pl.CostEstimate(flops=1_000_000, bytes_accessed=2_000_000, transcendentals=0),
    )(in_hbm(device_prompt), in_hbm(prompt_kv))
    context, reward = pl.pallas_call(
        attention_kernel,
        out_shape=(
            jax.ShapeDtypeStruct(response_queries.shape, bf16),
            jax.ShapeDtypeStruct((response_lengths.shape[0], 1, HEAD_DIM), jnp.float32),
        ),
        in_specs=[smem, vmem, vmem, vmem, vmem, vmem],
        out_specs=(vmem, vmem),
        compiler_params=pltpu.CompilerParams(vmem_limit_bytes=32 * 1024 * 1024),
        cost_estimate=pl.CostEstimate(
            flops=700_000_000, bytes_accessed=2_000_000, transcendentals=1_400_000
        ),
    )(
        response_lengths,
        probe_weight.reshape(-1, HEAD_DIM),
        response_queries,
        response_kv,
        in_vmem(all_a),
        in_vmem(all_b),
    )
    advantage = pl.pallas_call(
        reward_kernel,
        out_shape=jax.ShapeDtypeStruct(response_lengths.shape, jnp.float32),
        in_specs=[smem, vmem],
        out_specs=smem,
        scratch_shapes=[
            pltpu.VMEM((NZT, 1, HEAD_DIM), jnp.float32),
            pltpu.VMEM((NXY, 1, HEAD_DIM), jnp.float32),
            pltpu.SemaphoreType.DMA((2,)),
            pltpu.SemaphoreType.DMA((2,)),
        ],
        compiler_params=pltpu.CompilerParams(collective_id=1, has_side_effects=True),
        cost_estimate=pl.CostEstimate(flops=10_000, bytes_accessed=10_000, transcendentals=0),
    )(device_prompt, reward)
    return context, advantage


def solution(mesh):
    placed = (
        P("resp", None, "tp"),
        P(None, "resp", None, "tp"),
        P(None, None, "resp", "tp"),
        P("resp"),
        P(),
        P("tp"),
    )
    return jax.shard_map(
        shards,
        mesh=mesh,
        in_specs=placed,
        out_specs=(P("resp", None, "tp"), P("resp")),
        check_vma=False,
    )
```

```python
import functools
import math

import jax
import jax.numpy as jnp
from jax import lax
from jax.experimental import pallas as pl
from jax.experimental.pallas import tpu as pltpu
from jax.sharding import PartitionSpec as P

HEAD_DIM = 128
SCALAR = 144
BEST = 16
MESH = pl.DeviceIdType.MESH

NZ, NX, NY, NT = 4, 4, 8, 4
NXY, NZX = NX * NY, NZ * NX
PROMPTS = 16
TOKENS = 4
PIECES = 4
ROWS = PIECES * TOKENS


def far_first(first, second):
    places = [(a, b) for a in range(first[0]) for b in range(second[0]) if (a, b) != (0, 0)]
    hops = lambda n, step: min(n[0] - step, step) * n[1]
    return sorted(places, key=lambda p: (-hops(first, p[0]) - hops(second, p[1]), p))


FAR_XY = far_first((NX, 1), (NY, 1))
FAR_ZX = far_first((NZ, 2), (NX, 1))
FAR_ZT = far_first((NZ, 2), (NT, 1))


def attention(scores_parts, values, scale2):
    top = functools.reduce(jnp.maximum, [jnp.max(s, axis=1, keepdims=True) for s in scores_parts])
    weights = [jnp.exp2((s - top) * scale2) for s in scores_parts]
    total = functools.reduce(jnp.add, [jnp.sum(w, axis=1, keepdims=True) for w in weights])
    mixed = functools.reduce(
        jnp.add,
        [
            jnp.dot(w.astype(jnp.bfloat16), v, preferred_element_type=jnp.float32)
            for w, v in zip(weights, values)
        ],
    )
    return mixed * (1.0 / total)


def scores_of(q, k):
    return lax.dot_general(q, k, (((1,), (1,)), ((), ())), preferred_element_type=jnp.float32)


def kernel(
    lengths,
    prompts,
    probe,
    q_hbm,
    kv_hbm,
    raw_hbm,
    context,
    advantage,
    q,
    kv,
    raw,
    own_a,
    own_b,
    got_a,
    got_b,
    by_prompt_a,
    by_prompt_b,
    out_a,
    out_b,
    all_a,
    all_b,
    row_1,
    row_2,
    lines,
    load_sem,
    ring_send,
    ring_recv,
    send_sem,
    recv_sem,
):
    me = lax.axis_index("resp")
    tp = lax.axis_index("tp")
    zh = lax.div(me, NXY)
    xy = lax.rem(me, NXY)
    x = lax.div(xy, NY)
    y = lax.rem(xy, NY)
    zx = zh * NX + x

    def at_z(step):
        return lax.rem(zh + step, NZ) * NXY + xy

    def at_y(step):
        return zh * NXY + x * NY + lax.rem(y + step, NY)

    def at_x(step):
        return zh * NXY + lax.rem(x + step, NX) * NY + y

    def at_tp(step):
        return lax.rem(tp + step, NT)

    load_raw = pltpu.make_async_copy(raw_hbm, raw, load_sem.at[0])
    load_q = pltpu.make_async_copy(q_hbm, q, load_sem.at[1])
    load_kv = pltpu.make_async_copy(kv_hbm, kv, load_sem.at[2])
    load_raw.start()
    load_q.start()
    load_kv.start()

    barrier = pltpu.get_barrier_semaphore()

    def greet(device, tp_index):
        pl.semaphore_signal(barrier, inc=1, device_id=(device, tp_index), device_id_type=MESH)

    for i in range(1, NY):
        greet(at_y(i), tp)
    for i in range(1, NZ):
        greet(at_z(i), tp)
    for i in range(1, NX):
        greet(at_x(i), tp)
    for i in range(1, NT):
        greet(me, at_tp(i))

    load_raw.wait()

    def split(p, c):
        k = raw[0, p].astype(jnp.float32)
        v = raw[1, p].astype(jnp.float32)
        for plan, dst in enumerate((own_a, own_b)):
            parts = [
                part[:, (2 * plan + h) * HEAD_DIM : (2 * plan + h + 1) * HEAD_DIM]
                for part in (k, v)
                for h in range(2)
            ]
            dst[p] = jnp.concatenate(parts, axis=0).astype(jnp.bfloat16)
        return c

    lax.fori_loop(0, PROMPTS, split, 0)

    pl.semaphore_wait(barrier, (NY - 1) + (NZ - 1) + (NX - 1) + (NT - 1))

    half = PROMPTS // 2
    lo, hi = pl.ds(0, half), pl.ds(half, half)

    def ring(index, src, dst, device):
        return pltpu.make_async_remote_copy(
            src_ref=src,
            dst_ref=dst,
            send_sem=ring_send.at[index],
            recv_sem=ring_recv.at[index],
            device_id=(device, tp),
            device_id_type=MESH,
        )

    first = [
        ring(0, own_a, got_a.at[0], at_z(1)),
        ring(1, own_a, got_a.at[1], at_z(NZ - 1)),
        ring(2, own_b, got_b.at[2], at_y(2)),
        ring(3, own_b, got_b.at[3], at_y(NY - 2)),
        ring(4, own_b, got_b.at[0], at_y(1)),
        ring(5, own_b, got_b.at[1], at_y(NY - 1)),
    ]
    second = [
        ring(6, got_a.at[0, lo], got_a.at[2, lo], at_z(1)),
        ring(7, got_a.at[1, hi], got_a.at[2, hi], at_z(NZ - 1)),
        ring(8, got_b.at[2, lo], got_b.at[6, lo], at_y(2)),
        ring(9, got_b.at[2], got_b.at[4], at_y(1)),
        ring(10, got_b.at[3, hi], got_b.at[6, hi], at_y(NY - 2)),
        ring(11, got_b.at[3], got_b.at[5], at_y(NY - 1)),
    ]
    for copy in first:
        copy.start()
    for i in range(1, NX):
        pl.semaphore_signal(lines.at[0], inc=1, device_id=(at_x(i), tp), device_id_type=MESH)
    for i in range(1, NZ):
        pl.semaphore_signal(lines.at[1], inc=1, device_id=(at_z(i), tp), device_id_type=MESH)
    first[0].wait_recv()
    second[0].start()
    first[1].wait_recv()
    second[1].start()
    first[2].wait_recv()
    second[2].start()
    second[3].start()
    first[3].wait_recv()
    second[4].start()
    second[5].start()
    second[0].wait_recv()
    second[1].wait_recv()

    def regroup(own, got, slots, dst):
        def one(p, c):
            tiles = [own[p]] + [got[s, p] for s in range(slots)]
            tiles = [t.astype(jnp.float32) for t in tiles]
            for g in range(PIECES):
                rows = [t[TOKENS * g : TOKENS * (g + 1)] for t in tiles]
                dst[p, g] = jnp.concatenate(rows, axis=0).astype(jnp.bfloat16)
            return c

        def four(i, c):
            for n in range(4):
                one(4 * i + n, c)
            return c

        lax.fori_loop(0, PROMPTS // 4, four, 0)

    def beside_xy(dx, dy):
        return zh * NXY + lax.rem(x + dx, NX) * NY + lax.rem(y + dy, NY)

    def beside_zx(dz, dx):
        return lax.rem(zh + dz, NZ) * NXY + lax.rem(x + dx, NX) * NY + y

    def send(plan, slots, places, by_prompt, out, everyone, mine_at):
        blocks = [by_prompt[prompts[j]] for j in places]
        for i, block in zip(slots, blocks):
            out[i] = block
        for i, j in zip(slots, places):
            pltpu.make_async_remote_copy(
                src_ref=out.at[i],
                dst_ref=everyone.at[mine_at],
                send_sem=send_sem.at[plan],
                recv_sem=recv_sem.at[plan],
                device_id=(j, tp),
                device_id_type=MESH,
            ).start()

    def send_a(low, high):
        places = [beside_xy(*offset) for offset in FAR_XY[low:high]]
        send(0, range(low, high), places, by_prompt_a, out_a, all_a, xy)

    def send_b(low, high):
        places = [beside_zx(*offset) for offset in FAR_ZX[low:high]]
        send(1, range(low, high), places, by_prompt_b, out_b, all_b, zx)

    regroup(own_a, got_a, NZ - 1, by_prompt_a)
    pl.semaphore_wait(lines.at[0], NX - 1)
    pl.semaphore_wait(lines.at[1], NZ - 1)

    for low in range(0, NXY - 1, 6):
        send_a(low, min(low + 6, NXY - 1))
    first[4].wait_recv()
    first[5].wait_recv()
    for copy in second[2:]:
        copy.wait_recv()
    regroup(own_b, got_b, NY - 1, by_prompt_b)

    for low in range(0, NZX - 1, 5):
        send_b(low, low + 5)

    mine = prompts[me]
    all_a[xy] = by_prompt_a[mine]
    all_b[zx] = by_prompt_b[mine]

    load_q.wait()
    load_kv.wait()
    responses, steps, width = q.shape
    scale2 = math.log2(math.e) / math.sqrt(SCALAR)
    kv_heads = kv.shape[3] // HEAD_DIM
    column = lax.broadcasted_iota(jnp.int32, (8, steps), 1)
    last_q = []
    for r in range(responses):
        pick = (column == lengths[r] - 1).astype(jnp.bfloat16)
        last_q.append(jnp.dot(pick, q[r], preferred_element_type=jnp.float32).astype(jnp.bfloat16))

    def keys_values(g):
        ref = (all_a, all_b)[g // 2]
        h = g % 2
        return (
            ref[:, h].reshape(-1, HEAD_DIM),
            ref[:, 2 + h].reshape(-1, HEAD_DIM),
        )

    def own_keys_values(r, g):
        columns = slice(g * HEAD_DIM, (g + 1) * HEAD_DIM)
        return kv[0, r, :, columns], kv[1, r, :, columns]

    def wait_bytes(ref, sem):
        pltpu.make_async_copy(ref, ref, sem).wait()

    partial = [jnp.zeros((8, HEAD_DIM), jnp.float32) for _ in range(responses)]

    def reward_of(g):
        k, v = keys_values(g)
        heads = (2 * g, 2 * g + 1)
        rows = [
            jnp.concatenate([last[:, h * HEAD_DIM : (h + 1) * HEAD_DIM] for h in heads], axis=0)
            for last in last_q
        ]
        own, own_v = [], []
        for r in range(responses):
            its_k, its_v = own_keys_values(r, g)
            scores = scores_of(rows[r], its_k)
            seen = lax.broadcasted_iota(jnp.int32, scores.shape, 1) < lengths[r]
            own.append(jnp.where(seen, scores, -1e30))
            own_v.append(its_v)
        shared = scores_of(jnp.concatenate(rows, axis=0), k)
        own = jnp.concatenate(own, axis=0)
        top = jnp.maximum(
            jnp.max(shared, axis=1, keepdims=True), jnp.max(own, axis=1, keepdims=True)
        )
        shared = jnp.exp2((shared - top) * scale2)
        own = jnp.exp2((own - top) * scale2)
        total = jnp.sum(shared, axis=1, keepdims=True) + jnp.sum(own, axis=1, keepdims=True)
        own = own.astype(jnp.bfloat16)
        mixed = jnp.dot(shared.astype(jnp.bfloat16), v, preferred_element_type=jnp.float32)
        for r in range(responses):
            low = 16 * r
            part = mixed[low : low + 16] + jnp.dot(
                own[low : low + 16], own_v[r], preferred_element_type=jnp.float32
            )
            part = part * (1.0 / total[low : low + 16])
            part = part.astype(jnp.bfloat16).astype(jnp.float32)
            for n, h in enumerate(heads):
                partial[r] = partial[r] + part[8 * n : 8 * n + 8] * probe[h : h + 1, :]

    def attend(r, g):
        k, v = keys_values(g)
        own_k, own_v = own_keys_values(r, g)
        low = 2 * g * HEAD_DIM
        rows = jnp.concatenate(
            [q[r, :, low : low + HEAD_DIM], q[r, :, low + HEAD_DIM : low + 2 * HEAD_DIM]], axis=0
        )
        own = scores_of(rows, own_k)
        t = lax.broadcasted_iota(jnp.int32, own.shape, 0)
        t = jnp.where(t >= steps, t - steps, t)
        u = lax.broadcasted_iota(jnp.int32, own.shape, 1)
        own = jnp.where(u <= t, own, -1e30)
        mixed = attention([scores_of(rows, k), own], [v, own_v], scale2)
        live = lax.broadcasted_iota(jnp.int32, (steps, HEAD_DIM), 0) < lengths[r]
        for n in range(2):
            part = jnp.where(live, mixed[n * steps : (n + 1) * steps], 0.0)
            context[r, :, low + n * HEAD_DIM : low + (n + 1) * HEAD_DIM] = part.astype(jnp.bfloat16)

    wait_bytes(all_a.at[pl.ds(0, NXY - 1)], recv_sem.at[0])
    for g in range(2):
        reward_of(g)
    for g in range(2):
        for r in range(responses):
            attend(r, g)

    wait_bytes(all_b.at[pl.ds(0, NZX - 1)], recv_sem.at[1])
    for g in range(2, kv_heads):
        reward_of(g)

    lane = lax.broadcasted_iota(jnp.int32, (1, HEAD_DIM), 1)
    sums = [jnp.sum(part[0:1], axis=1, keepdims=True) for part in partial]
    row = jnp.where(lane == mine, sums[0] + sums[1], 0.0)
    for r in range(responses):
        row = jnp.where(lane == PROMPTS + r, sums[r], row)

    zt = zh * NT + tp
    rounds = (
        (row_1, zt, [(at_z(dz), at_tp(dt)) for dz, dt in FAR_ZT]),
        (row_2, xy, [(beside_xy(*offset), tp) for offset in FAR_XY]),
    )

    def send_row(n, row):
        ref, slot, devices = rounds[n]
        ref[slot] = row
        for device in devices:
            pltpu.make_async_remote_copy(
                src_ref=ref.at[slot],
                dst_ref=ref.at[slot],
                send_sem=send_sem.at[2 + n],
                recv_sem=recv_sem.at[2 + n],
                device_id=device,
                device_id_type=MESH,
            ).start()

    def wait_rows(n):
        ref, _, devices = rounds[n]
        wait_bytes(ref.at[pl.ds(0, len(devices))], recv_sem.at[2 + n])

    send_row(0, row)
    attend(0, 2)
    attend(1, 2)
    wait_rows(0)
    rewards = jnp.sum(row_1[pl.ds(zh * NT, NT)], axis=0)
    send_row(1, jnp.sum(row_1[...], axis=0))
    attend(0, 3)
    attend(1, 3)
    wait_rows(1)
    table = jnp.sum(row_2[...], axis=0)
    group = jnp.sum(jnp.where(lane == mine, table, 0.0), axis=1, keepdims=True) / BEST
    result = rewards - group
    for r in range(responses):
        advantage[r] = jnp.sum(jnp.where(lane == PROMPTS + r, result, 0.0))

    for copy in first:
        copy.wait_send()
    for copy in second:
        copy.wait_send()
    wait_bytes(out_a.at[pl.ds(0, NXY - 1)], send_sem.at[0])
    wait_bytes(out_b.at[pl.ds(0, NZX - 1)], send_sem.at[1])
    for n, (ref, _, devices) in enumerate(rounds):
        wait_bytes(ref.at[pl.ds(0, len(devices))], send_sem.at[2 + n])


def shards(response_queries, response_kv, prompt_kv, response_lengths, device_prompt, probe_weight):
    bf16 = jnp.bfloat16
    smem = pl.BlockSpec(memory_space=pltpu.SMEM)
    vmem = pl.BlockSpec(memory_space=pltpu.VMEM)
    anywhere = pl.BlockSpec(memory_space=pl.ANY)
    in_hbm = functools.partial(pltpu.with_memory_space_constraint, memory_space=pltpu.HBM)
    block = (PROMPTS, ROWS, HEAD_DIM)
    context, advantage = pl.pallas_call(
        kernel,
        out_shape=(
            pltpu.VMEM(response_queries.shape, bf16),
            jax.ShapeDtypeStruct(response_lengths.shape, jnp.float32),
        ),
        in_specs=[smem, smem, vmem, anywhere, anywhere, anywhere],
        out_specs=(vmem, smem),
        scratch_shapes=[
            pltpu.VMEM(response_queries.shape, bf16),
            pltpu.VMEM(response_kv.shape, bf16),
            pltpu.VMEM(prompt_kv.shape, bf16),
            pltpu.VMEM(block, bf16),
            pltpu.VMEM(block, bf16),
            pltpu.VMEM((NZ - 1,) + block, bf16),
            pltpu.VMEM((NY - 1,) + block, bf16),
            pltpu.VMEM((PROMPTS, PIECES, NZ * TOKENS, HEAD_DIM), bf16),
            pltpu.VMEM((PROMPTS, PIECES, NY * TOKENS, HEAD_DIM), bf16),
            pltpu.VMEM((NXY, PIECES, NZ * TOKENS, HEAD_DIM), bf16),
            pltpu.VMEM((NZX, PIECES, NY * TOKENS, HEAD_DIM), bf16),
            pltpu.VMEM((NXY, PIECES, NZ * TOKENS, HEAD_DIM), bf16),
            pltpu.VMEM((NZX, PIECES, NY * TOKENS, HEAD_DIM), bf16),
            pltpu.VMEM((NZ * NT, 1, HEAD_DIM), jnp.float32),
            pltpu.VMEM((NXY, 1, HEAD_DIM), jnp.float32),
            pltpu.SemaphoreType.REGULAR((2,)),
            pltpu.SemaphoreType.DMA((3,)),
            pltpu.SemaphoreType.DMA((12,)),
            pltpu.SemaphoreType.DMA((12,)),
            pltpu.SemaphoreType.DMA((4,)),
            pltpu.SemaphoreType.DMA((4,)),
        ],
        compiler_params=pltpu.CompilerParams(
            collective_id=0, has_side_effects=True, vmem_limit_bytes=48 * 1024 * 1024
        ),
        cost_estimate=pl.CostEstimate(
            flops=700_000_000, bytes_accessed=2_000_000, transcendentals=1_400_000
        ),
    )(
        in_hbm(response_lengths),
        in_hbm(device_prompt),
        in_hbm(probe_weight.reshape(-1, HEAD_DIM)),
        in_hbm(response_queries),
        in_hbm(response_kv),
        in_hbm(prompt_kv),
    )
    return context, advantage


def solution(mesh):
    placed = (
        P("resp", None, "tp"),
        P(None, "resp", None, "tp"),
        P(None, None, "resp", "tp"),
        P("resp"),
        P(),
        P("tp"),
    )
    return jax.shard_map(
        shards,
        mesh=mesh,
        in_specs=placed,
        out_specs=(P("resp", None, "tp"), P("resp")),
        check_vma=False,
    )
```

```python
import functools
import math

import jax
import jax.numpy as jnp
from jax import lax
from jax.experimental import pallas as pl
from jax.experimental.pallas import tpu as pltpu
from jax.sharding import PartitionSpec as P

HEAD_DIM = 128
SCALAR = 144
BEST = 16
MESH = pl.DeviceIdType.MESH

NZ, NX, NY, NT = 4, 4, 8, 4
NXY, NZX = NX * NY, NZ * NX
PROMPTS = 16
TOKENS = 4
PIECES = 4
ROWS = PIECES * TOKENS


def far_first(first, second):
    places = [(a, b) for a in range(first[0]) for b in range(second[0]) if (a, b) != (0, 0)]
    hops = lambda n, step: min(n[0] - step, step) * n[1]
    return sorted(places, key=lambda p: (-hops(first, p[0]) - hops(second, p[1]), p))


FAR_XY = far_first((NX, 1), (NY, 1))
FAR_ZX = far_first((NZ, 2), (NX, 1))
FAR_ZT = far_first((NZ, 2), (NT, 1))


def attention(scores_parts, values, scale2):
    top = functools.reduce(jnp.maximum, [jnp.max(s, axis=1, keepdims=True) for s in scores_parts])
    weights = [jnp.exp2((s - top) * scale2) for s in scores_parts]
    total = functools.reduce(jnp.add, [jnp.sum(w, axis=1, keepdims=True) for w in weights])
    mixed = functools.reduce(
        jnp.add,
        [
            jnp.dot(w.astype(jnp.bfloat16), v, preferred_element_type=jnp.float32)
            for w, v in zip(weights, values)
        ],
    )
    return mixed * (1.0 / total)


def scores_of(q, k):
    return lax.dot_general(q, k, (((1,), (1,)), ((), ())), preferred_element_type=jnp.float32)


def kernel(
    lengths,
    prompts,
    probe,
    q_hbm,
    kv_hbm,
    raw_hbm,
    context,
    advantage,
    q,
    kv,
    raw,
    own_a,
    own_b,
    got_a,
    got_b,
    by_prompt_a,
    by_prompt_b,
    out_a,
    out_b,
    all_a,
    all_b,
    row_1,
    row_2,
    lines,
    load_sem,
    ring_send,
    ring_recv,
    send_sem,
    recv_sem,
):
    me = lax.axis_index("resp")
    tp = lax.axis_index("tp")
    zh = lax.div(me, NXY)
    xy = lax.rem(me, NXY)
    x = lax.div(xy, NY)
    y = lax.rem(xy, NY)
    zx = zh * NX + x

    def at_z(step):
        return lax.rem(zh + step, NZ) * NXY + xy

    def at_y(step):
        return zh * NXY + x * NY + lax.rem(y + step, NY)

    def at_x(step):
        return zh * NXY + lax.rem(x + step, NX) * NY + y

    def at_tp(step):
        return lax.rem(tp + step, NT)

    load_raw = pltpu.make_async_copy(raw_hbm, raw, load_sem.at[0])
    load_q = pltpu.make_async_copy(q_hbm, q, load_sem.at[1])
    load_kv = pltpu.make_async_copy(kv_hbm, kv, load_sem.at[2])
    load_raw.start()
    load_q.start()
    load_kv.start()

    barrier = pltpu.get_barrier_semaphore()

    def greet(device, tp_index):
        pl.semaphore_signal(barrier, inc=1, device_id=(device, tp_index), device_id_type=MESH)

    for i in (4, 3, 5, 2, 6, 1, 7):
        greet(at_y(i), tp)
    for i in (2, 1, 3):
        greet(at_z(i), tp)
    for i in (2, 1, 3):
        greet(at_x(i), tp)
    for i in (2, 3, 1):
        greet(me, at_tp(i))

    load_raw.wait()

    def split(p, c):
        k = raw[0, p].astype(jnp.float32)
        v = raw[1, p].astype(jnp.float32)
        for plan, dst in enumerate((own_a, own_b)):
            parts = [
                part[:, (2 * plan + h) * HEAD_DIM : (2 * plan + h + 1) * HEAD_DIM]
                for part in (k, v)
                for h in range(2)
            ]
            dst[p] = jnp.concatenate(parts, axis=0).astype(jnp.bfloat16)
        return c

    lax.fori_loop(0, PROMPTS, split, 0)

    pl.semaphore_wait(barrier, (NY - 1) + (NZ - 1) + (NX - 1) + (NT - 1))

    half = PROMPTS // 2
    lo, hi = pl.ds(0, half), pl.ds(half, half)

    def ring(index, src, dst, device):
        return pltpu.make_async_remote_copy(
            src_ref=src,
            dst_ref=dst,
            send_sem=ring_send.at[index],
            recv_sem=ring_recv.at[index],
            device_id=(device, tp),
            device_id_type=MESH,
        )

    first = [
        ring(0, own_a, got_a.at[0], at_z(1)),
        ring(1, own_a, got_a.at[1], at_z(NZ - 1)),
        ring(2, own_b, got_b.at[2], at_y(2)),
        ring(3, own_b, got_b.at[3], at_y(NY - 2)),
        ring(4, own_b, got_b.at[0], at_y(1)),
        ring(5, own_b, got_b.at[1], at_y(NY - 1)),
    ]
    second = [
        ring(6, got_a.at[0, lo], got_a.at[2, lo], at_z(1)),
        ring(7, got_a.at[1, hi], got_a.at[2, hi], at_z(NZ - 1)),
        ring(8, got_b.at[2, lo], got_b.at[6, lo], at_y(2)),
        ring(9, got_b.at[2], got_b.at[4], at_y(1)),
        ring(10, got_b.at[3, hi], got_b.at[6, hi], at_y(NY - 2)),
        ring(11, got_b.at[3], got_b.at[5], at_y(NY - 1)),
    ]
    for n in (2, 3, 0, 1, 4, 5):
        first[n].start()
    for i in range(1, NX):
        pl.semaphore_signal(lines.at[0], inc=1, device_id=(at_x(i), tp), device_id_type=MESH)
    for i in range(1, NZ):
        pl.semaphore_signal(lines.at[1], inc=1, device_id=(at_z(i), tp), device_id_type=MESH)
    first[2].wait_recv()
    second[2].start()
    second[3].start()
    first[3].wait_recv()
    second[4].start()
    second[5].start()
    first[0].wait_recv()
    second[0].start()
    first[1].wait_recv()
    second[1].start()
    second[0].wait_recv()
    second[1].wait_recv()

    def regroup(own, got, slots, dst):
        def one(p, c):
            tiles = [own[p]] + [got[s, p] for s in range(slots)]
            tiles = [t.astype(jnp.float32) for t in tiles]
            for g in range(PIECES):
                rows = [t[TOKENS * g : TOKENS * (g + 1)] for t in tiles]
                dst[p, g] = jnp.concatenate(rows, axis=0).astype(jnp.bfloat16)
            return c

        def four(i, c):
            for n in range(4):
                one(4 * i + n, c)
            return c

        lax.fori_loop(0, PROMPTS // 4, four, 0)

    def beside_xy(dx, dy):
        return zh * NXY + lax.rem(x + dx, NX) * NY + lax.rem(y + dy, NY)

    def beside_zx(dz, dx):
        return lax.rem(zh + dz, NZ) * NXY + lax.rem(x + dx, NX) * NY + y

    def send(plan, slots, places, by_prompt, out, everyone, mine_at):
        blocks = [by_prompt[prompts[j]] for j in places]
        for i, block in zip(slots, blocks):
            out[i] = block
        for i, j in zip(slots, places):
            pltpu.make_async_remote_copy(
                src_ref=out.at[i],
                dst_ref=everyone.at[mine_at],
                send_sem=send_sem.at[plan],
                recv_sem=recv_sem.at[plan],
                device_id=(j, tp),
                device_id_type=MESH,
            ).start()

    def send_a(low, high):
        places = [beside_xy(*offset) for offset in FAR_XY[low:high]]
        send(0, range(low, high), places, by_prompt_a, out_a, all_a, xy)

    def send_b(low, high):
        places = [beside_zx(*offset) for offset in FAR_ZX[low:high]]
        send(1, range(low, high), places, by_prompt_b, out_b, all_b, zx)

    regroup(own_a, got_a, NZ - 1, by_prompt_a)
    pl.semaphore_wait(lines.at[0], NX - 1)
    pl.semaphore_wait(lines.at[1], NZ - 1)

    for low in range(0, NXY // 2, 4):
        send_a(low, low + 4)
    first[4].wait_recv()
    first[5].wait_recv()
    for copy in second[2:]:
        copy.wait_recv()
    regroup(own_b, got_b, NY - 1, by_prompt_b)

    for low in range(0, NZX - 1, 5):
        send_b(low, low + 5)
    for low in range(NXY // 2, NXY - 1, 5):
        send_a(low, low + 5)

    mine = prompts[me]
    all_a[xy] = by_prompt_a[mine]
    all_b[zx] = by_prompt_b[mine]

    load_q.wait()
    load_kv.wait()
    responses, steps, width = q.shape
    scale2 = math.log2(math.e) / math.sqrt(SCALAR)
    kv_heads = kv.shape[3] // HEAD_DIM
    column = lax.broadcasted_iota(jnp.int32, (8, steps), 1)
    last_q = []
    for r in range(responses):
        pick = (column == lengths[r] - 1).astype(jnp.bfloat16)
        last_q.append(jnp.dot(pick, q[r], preferred_element_type=jnp.float32).astype(jnp.bfloat16))

    def keys_values(g):
        ref = (all_a, all_b)[g // 2]
        h = g % 2
        return (
            ref[:, h].reshape(-1, HEAD_DIM),
            ref[:, 2 + h].reshape(-1, HEAD_DIM),
        )

    def own_keys_values(r, g):
        columns = slice(g * HEAD_DIM, (g + 1) * HEAD_DIM)
        return kv[0, r, :, columns], kv[1, r, :, columns]

    def wait_bytes(ref, sem):
        pltpu.make_async_copy(ref, ref, sem).wait()

    partial = [jnp.zeros((8, HEAD_DIM), jnp.float32) for _ in range(responses)]

    def reward_of(g):
        k, v = keys_values(g)
        heads = (2 * g, 2 * g + 1)
        rows = [
            jnp.concatenate([last[:, h * HEAD_DIM : (h + 1) * HEAD_DIM] for h in heads], axis=0)
            for last in last_q
        ]
        own, own_v = [], []
        for r in range(responses):
            its_k, its_v = own_keys_values(r, g)
            scores = scores_of(rows[r], its_k)
            seen = lax.broadcasted_iota(jnp.int32, scores.shape, 1) < lengths[r]
            own.append(jnp.where(seen, scores, -1e30))
            own_v.append(its_v)
        shared = scores_of(jnp.concatenate(rows, axis=0), k)
        own = jnp.concatenate(own, axis=0)
        top = jnp.maximum(
            jnp.max(shared, axis=1, keepdims=True), jnp.max(own, axis=1, keepdims=True)
        )
        shared = jnp.exp2((shared - top) * scale2)
        own = jnp.exp2((own - top) * scale2)
        total = jnp.sum(shared, axis=1, keepdims=True) + jnp.sum(own, axis=1, keepdims=True)
        own = own.astype(jnp.bfloat16)
        mixed = jnp.dot(shared.astype(jnp.bfloat16), v, preferred_element_type=jnp.float32)
        for r in range(responses):
            low = 16 * r
            part = mixed[low : low + 16] + jnp.dot(
                own[low : low + 16], own_v[r], preferred_element_type=jnp.float32
            )
            part = part * (1.0 / total[low : low + 16])
            part = part.astype(jnp.bfloat16).astype(jnp.float32)
            for n, h in enumerate(heads):
                partial[r] = partial[r] + part[8 * n : 8 * n + 8] * probe[h : h + 1, :]

    def attend(r, g):
        k, v = keys_values(g)
        own_k, own_v = own_keys_values(r, g)
        low = 2 * g * HEAD_DIM
        rows = jnp.concatenate(
            [q[r, :, low : low + HEAD_DIM], q[r, :, low + HEAD_DIM : low + 2 * HEAD_DIM]], axis=0
        )
        own = scores_of(rows, own_k)
        t = lax.broadcasted_iota(jnp.int32, own.shape, 0)
        t = jnp.where(t >= steps, t - steps, t)
        u = lax.broadcasted_iota(jnp.int32, own.shape, 1)
        own = jnp.where(u <= t, own, -1e30)
        mixed = attention([scores_of(rows, k), own], [v, own_v], scale2)
        live = lax.broadcasted_iota(jnp.int32, (steps, HEAD_DIM), 0) < lengths[r]
        for n in range(2):
            part = jnp.where(live, mixed[n * steps : (n + 1) * steps], 0.0)
            context[r, :, low + n * HEAD_DIM : low + (n + 1) * HEAD_DIM] = part.astype(jnp.bfloat16)

    wait_bytes(all_a.at[pl.ds(0, NXY - 1)], recv_sem.at[0])
    for g in range(2):
        reward_of(g)

    wait_bytes(all_b.at[pl.ds(0, NZX - 1)], recv_sem.at[1])
    for g in range(2, kv_heads):
        reward_of(g)

    lane = lax.broadcasted_iota(jnp.int32, (1, HEAD_DIM), 1)
    sums = [jnp.sum(part[0:1], axis=1, keepdims=True) for part in partial]
    row = jnp.where(lane == mine, sums[0] + sums[1], 0.0)
    for r in range(responses):
        row = jnp.where(lane == PROMPTS + r, sums[r], row)

    zt = zh * NT + tp
    rounds = (
        (row_1, zt, [(at_z(dz), at_tp(dt)) for dz, dt in FAR_ZT]),
        (row_2, xy, [(beside_xy(*offset), tp) for offset in FAR_XY]),
    )

    def send_row(n, row):
        ref, slot, devices = rounds[n]
        ref[slot] = row
        for device in devices:
            pltpu.make_async_remote_copy(
                src_ref=ref.at[slot],
                dst_ref=ref.at[slot],
                send_sem=send_sem.at[2 + n],
                recv_sem=recv_sem.at[2 + n],
                device_id=device,
                device_id_type=MESH,
            ).start()

    def wait_rows(n):
        ref, _, devices = rounds[n]
        wait_bytes(ref.at[pl.ds(0, len(devices))], recv_sem.at[2 + n])

    send_row(0, row)
    for g in range(2):
        for r in range(responses):
            attend(r, g)
    wait_rows(0)
    rewards = jnp.sum(row_1[pl.ds(zh * NT, NT)], axis=0)
    send_row(1, jnp.sum(row_1[...], axis=0))
    for g in range(2, kv_heads):
        for r in range(responses):
            attend(r, g)
    wait_rows(1)
    table = jnp.sum(row_2[...], axis=0)
    group = jnp.sum(jnp.where(lane == mine, table, 0.0), axis=1, keepdims=True) / BEST
    result = rewards - group
    for r in range(responses):
        advantage[r] = jnp.sum(jnp.where(lane == PROMPTS + r, result, 0.0))

    for copy in first:
        copy.wait_send()
    for copy in second:
        copy.wait_send()
    wait_bytes(out_a.at[pl.ds(0, NXY - 1)], send_sem.at[0])
    wait_bytes(out_b.at[pl.ds(0, NZX - 1)], send_sem.at[1])
    for n, (ref, _, devices) in enumerate(rounds):
        wait_bytes(ref.at[pl.ds(0, len(devices))], send_sem.at[2 + n])


def shards(response_queries, response_kv, prompt_kv, response_lengths, device_prompt, probe_weight):
    bf16 = jnp.bfloat16
    smem = pl.BlockSpec(memory_space=pltpu.SMEM)
    vmem = pl.BlockSpec(memory_space=pltpu.VMEM)
    anywhere = pl.BlockSpec(memory_space=pl.ANY)
    in_hbm = functools.partial(pltpu.with_memory_space_constraint, memory_space=pltpu.HBM)
    block = (PROMPTS, ROWS, HEAD_DIM)
    context, advantage = pl.pallas_call(
        kernel,
        out_shape=(
            pltpu.VMEM(response_queries.shape, bf16),
            jax.ShapeDtypeStruct(response_lengths.shape, jnp.float32),
        ),
        in_specs=[smem, smem, vmem, anywhere, anywhere, anywhere],
        out_specs=(vmem, smem),
        scratch_shapes=[
            pltpu.VMEM(response_queries.shape, bf16),
            pltpu.VMEM(response_kv.shape, bf16),
            pltpu.VMEM(prompt_kv.shape, bf16),
            pltpu.VMEM(block, bf16),
            pltpu.VMEM(block, bf16),
            pltpu.VMEM((NZ - 1,) + block, bf16),
            pltpu.VMEM((NY - 1,) + block, bf16),
            pltpu.VMEM((PROMPTS, PIECES, NZ * TOKENS, HEAD_DIM), bf16),
            pltpu.VMEM((PROMPTS, PIECES, NY * TOKENS, HEAD_DIM), bf16),
            pltpu.VMEM((NXY, PIECES, NZ * TOKENS, HEAD_DIM), bf16),
            pltpu.VMEM((NZX, PIECES, NY * TOKENS, HEAD_DIM), bf16),
            pltpu.VMEM((NXY, PIECES, NZ * TOKENS, HEAD_DIM), bf16),
            pltpu.VMEM((NZX, PIECES, NY * TOKENS, HEAD_DIM), bf16),
            pltpu.VMEM((NZ * NT, 1, HEAD_DIM), jnp.float32),
            pltpu.VMEM((NXY, 1, HEAD_DIM), jnp.float32),
            pltpu.SemaphoreType.REGULAR((2,)),
            pltpu.SemaphoreType.DMA((3,)),
            pltpu.SemaphoreType.DMA((12,)),
            pltpu.SemaphoreType.DMA((12,)),
            pltpu.SemaphoreType.DMA((4,)),
            pltpu.SemaphoreType.DMA((4,)),
        ],
        compiler_params=pltpu.CompilerParams(
            collective_id=0, has_side_effects=True, vmem_limit_bytes=48 * 1024 * 1024
        ),
        cost_estimate=pl.CostEstimate(
            flops=700_000_000, bytes_accessed=2_000_000, transcendentals=1_400_000
        ),
    )(
        in_hbm(response_lengths),
        in_hbm(device_prompt),
        in_hbm(probe_weight.reshape(-1, HEAD_DIM)),
        in_hbm(response_queries),
        in_hbm(response_kv),
        in_hbm(prompt_kv),
    )
    return context, advantage


def solution(mesh):
    placed = (
        P("resp", None, "tp"),
        P(None, "resp", None, "tp"),
        P(None, None, "resp", "tp"),
        P("resp"),
        P(),
        P("tp"),
    )
    return jax.shard_map(
        shards,
        mesh=mesh,
        in_specs=placed,
        out_specs=(P("resp", None, "tp"), P("resp")),
        check_vma=False,
    )
```

```python
import functools
import math

import jax
import jax.numpy as jnp
from jax import lax
from jax.experimental import pallas as pl
from jax.experimental.pallas import tpu as pltpu
from jax.sharding import PartitionSpec as P

HEAD_DIM = 128
SCALAR = 144
BEST = 16
MESH = pl.DeviceIdType.MESH

NZ, NX, NY, NT = 4, 4, 8, 4
NXY, NZX = NX * NY, NZ * NX
PROMPTS = 16
TOKENS = 4
PIECES = 4
ROWS = PIECES * TOKENS


def far_first(first, second):
    places = [(a, b) for a in range(first[0]) for b in range(second[0]) if (a, b) != (0, 0)]
    hops = lambda n, step: min(n[0] - step, step) * n[1]
    return sorted(places, key=lambda p: (-hops(first, p[0]) - hops(second, p[1]), p))


FAR_XY = far_first((NX, 1), (NY, 1))
FAR_ZX = far_first((NZ, 2), (NX, 1))
FAR_ZT = far_first((NZ, 2), (NT, 1))


def attention(scores_parts, values, scale2):
    top = functools.reduce(jnp.maximum, [jnp.max(s, axis=1, keepdims=True) for s in scores_parts])
    weights = [jnp.exp2((s - top) * scale2) for s in scores_parts]
    total = functools.reduce(jnp.add, [jnp.sum(w, axis=1, keepdims=True) for w in weights])
    mixed = functools.reduce(
        jnp.add,
        [
            jnp.dot(w.astype(jnp.bfloat16), v, preferred_element_type=jnp.float32)
            for w, v in zip(weights, values)
        ],
    )
    return mixed * (1.0 / total)


def scores_of(q, k):
    return lax.dot_general(q, k, (((1,), (1,)), ((), ())), preferred_element_type=jnp.float32)


def kernel(
    lengths_hbm,
    prompts_hbm,
    probe_hbm,
    q_hbm,
    kv_hbm,
    raw_hbm,
    context,
    advantage,
    lengths,
    prompts,
    probe,
    q,
    kv,
    raw,
    own_a,
    own_b,
    got_a,
    got_b,
    by_prompt_a,
    by_prompt_b,
    out_a,
    out_b,
    all_a,
    all_b,
    row_1,
    row_2,
    lines,
    load_sem,
    ring_send,
    ring_recv,
    send_sem,
    recv_sem,
):
    me = lax.axis_index("resp")
    tp = lax.axis_index("tp")
    zh = lax.div(me, NXY)
    xy = lax.rem(me, NXY)
    x = lax.div(xy, NY)
    y = lax.rem(xy, NY)
    zx = zh * NX + x

    def at_z(step):
        return lax.rem(zh + step, NZ) * NXY + xy

    def at_y(step):
        return zh * NXY + x * NY + lax.rem(y + step, NY)

    def at_x(step):
        return zh * NXY + lax.rem(x + step, NX) * NY + y

    def at_tp(step):
        return lax.rem(tp + step, NT)

    barrier = pltpu.get_barrier_semaphore()

    def greet(device, tp_index):
        pl.semaphore_signal(barrier, inc=1, device_id=(device, tp_index), device_id_type=MESH)

    for i in (4, 3, 5, 2, 6, 1, 7):
        greet(at_y(i), tp)
    for i in (2, 1, 3):
        greet(at_z(i), tp)
    for i in (2, 1, 3):
        greet(at_x(i), tp)
    for i in (2, 3, 1):
        greet(me, at_tp(i))

    load_raw = pltpu.make_async_copy(raw_hbm, raw, load_sem.at[0])
    load_prompts = pltpu.make_async_copy(prompts_hbm, prompts, load_sem.at[1])
    load_rest = [
        pltpu.make_async_copy(src, dst, load_sem.at[2 + n])
        for n, (src, dst) in enumerate(
            ((q_hbm, q), (kv_hbm, kv), (lengths_hbm, lengths), (probe_hbm, probe))
        )
    ]
    load_raw.start()
    load_prompts.start()
    for load in load_rest:
        load.start()

    load_raw.wait()

    def split(p, c):
        k = raw[0, p].astype(jnp.float32)
        v = raw[1, p].astype(jnp.float32)
        for plan, dst in enumerate((own_a, own_b)):
            parts = [
                part[:, (2 * plan + h) * HEAD_DIM : (2 * plan + h + 1) * HEAD_DIM]
                for part in (k, v)
                for h in range(2)
            ]
            dst[p] = jnp.concatenate(parts, axis=0).astype(jnp.bfloat16)
        return c

    lax.fori_loop(0, PROMPTS, split, 0)

    pl.semaphore_wait(barrier, (NY - 1) + (NZ - 1) + (NX - 1) + (NT - 1))

    half = PROMPTS // 2
    lo, hi = pl.ds(0, half), pl.ds(half, half)

    def ring(index, src, dst, device):
        return pltpu.make_async_remote_copy(
            src_ref=src,
            dst_ref=dst,
            send_sem=ring_send.at[index],
            recv_sem=ring_recv.at[index],
            device_id=(device, tp),
            device_id_type=MESH,
        )

    first = [
        ring(0, own_a, got_a.at[0], at_z(1)),
        ring(1, own_a, got_a.at[1], at_z(NZ - 1)),
        ring(2, own_b, got_b.at[2], at_y(2)),
        ring(3, own_b, got_b.at[3], at_y(NY - 2)),
        ring(4, own_b, got_b.at[0], at_y(1)),
        ring(5, own_b, got_b.at[1], at_y(NY - 1)),
    ]
    second = [
        ring(6, got_a.at[0, lo], got_a.at[2, lo], at_z(1)),
        ring(7, got_a.at[1, hi], got_a.at[2, hi], at_z(NZ - 1)),
        ring(8, got_b.at[2, lo], got_b.at[6, lo], at_y(2)),
        ring(9, got_b.at[2], got_b.at[4], at_y(1)),
        ring(10, got_b.at[3, hi], got_b.at[6, hi], at_y(NY - 2)),
        ring(11, got_b.at[3], got_b.at[5], at_y(NY - 1)),
    ]
    for n in (2, 3, 0, 1, 4, 5):
        first[n].start()
    for i in range(1, NX):
        pl.semaphore_signal(lines.at[0], inc=1, device_id=(at_x(i), tp), device_id_type=MESH)
    for i in range(1, NZ):
        pl.semaphore_signal(lines.at[1], inc=1, device_id=(at_z(i), tp), device_id_type=MESH)
    first[2].wait_recv()
    second[2].start()
    second[3].start()
    first[3].wait_recv()
    second[4].start()
    second[5].start()
    first[0].wait_recv()
    second[0].start()
    first[1].wait_recv()
    second[1].start()
    second[0].wait_recv()
    second[1].wait_recv()

    def regroup(own, got, slots, dst):
        def one(p, c):
            tiles = [own[p]] + [got[s, p] for s in range(slots)]
            tiles = [t.astype(jnp.float32) for t in tiles]
            for g in range(PIECES):
                rows = [t[TOKENS * g : TOKENS * (g + 1)] for t in tiles]
                dst[p, g] = jnp.concatenate(rows, axis=0).astype(jnp.bfloat16)
            return c

        def four(i, c):
            for n in range(4):
                one(4 * i + n, c)
            return c

        lax.fori_loop(0, PROMPTS // 4, four, 0)

    def beside_xy(dx, dy):
        return zh * NXY + lax.rem(x + dx, NX) * NY + lax.rem(y + dy, NY)

    def beside_zx(dz, dx):
        return lax.rem(zh + dz, NZ) * NXY + lax.rem(x + dx, NX) * NY + y

    def send(plan, slots, places, by_prompt, out, everyone, mine_at):
        blocks = [by_prompt[prompts[j]] for j in places]
        for i, block in zip(slots, blocks):
            out[i] = block
        for i, j in zip(slots, places):
            pltpu.make_async_remote_copy(
                src_ref=out.at[i],
                dst_ref=everyone.at[mine_at],
                send_sem=send_sem.at[plan],
                recv_sem=recv_sem.at[plan],
                device_id=(j, tp),
                device_id_type=MESH,
            ).start()

    def send_a(low, high):
        places = [beside_xy(*offset) for offset in FAR_XY[low:high]]
        send(0, range(low, high), places, by_prompt_a, out_a, all_a, xy)

    def send_b(low, high):
        places = [beside_zx(*offset) for offset in FAR_ZX[low:high]]
        send(1, range(low, high), places, by_prompt_b, out_b, all_b, zx)

    regroup(own_a, got_a, NZ - 1, by_prompt_a)
    load_prompts.wait()
    pl.semaphore_wait(lines.at[0], NX - 1)
    pl.semaphore_wait(lines.at[1], NZ - 1)

    for low in range(0, NXY // 2, 4):
        send_a(low, low + 4)
    first[4].wait_recv()
    first[5].wait_recv()
    for copy in second[2:]:
        copy.wait_recv()
    regroup(own_b, got_b, NY - 1, by_prompt_b)

    for low in range(0, NZX - 1, 5):
        send_b(low, low + 5)
    for low in range(NXY // 2, NXY - 1, 5):
        send_a(low, low + 5)

    mine = prompts[me]
    all_a[xy] = by_prompt_a[mine]
    all_b[zx] = by_prompt_b[mine]

    for load in load_rest:
        load.wait()
    responses, steps, width = q.shape
    scale2 = math.log2(math.e) / math.sqrt(SCALAR)
    kv_heads = kv.shape[3] // HEAD_DIM
    column = lax.broadcasted_iota(jnp.int32, (8, steps), 1)
    last_q = []
    for r in range(responses):
        pick = (column == lengths[r] - 1).astype(jnp.bfloat16)
        last_q.append(jnp.dot(pick, q[r], preferred_element_type=jnp.float32).astype(jnp.bfloat16))

    def keys_values(g):
        ref = (all_a, all_b)[g // 2]
        h = g % 2
        return (
            ref[:, h].reshape(-1, HEAD_DIM),
            ref[:, 2 + h].reshape(-1, HEAD_DIM),
        )

    def own_keys_values(r, g):
        columns = slice(g * HEAD_DIM, (g + 1) * HEAD_DIM)
        return kv[0, r, :, columns], kv[1, r, :, columns]

    def wait_bytes(ref, sem):
        pltpu.make_async_copy(ref, ref, sem).wait()

    partial = [jnp.zeros((8, HEAD_DIM), jnp.float32) for _ in range(responses)]

    def reward_of(g):
        k, v = keys_values(g)
        heads = (2 * g, 2 * g + 1)
        rows = [
            jnp.concatenate([last[:, h * HEAD_DIM : (h + 1) * HEAD_DIM] for h in heads], axis=0)
            for last in last_q
        ]
        own, own_v = [], []
        for r in range(responses):
            its_k, its_v = own_keys_values(r, g)
            scores = scores_of(rows[r], its_k)
            seen = lax.broadcasted_iota(jnp.int32, scores.shape, 1) < lengths[r]
            own.append(jnp.where(seen, scores, -1e30))
            own_v.append(its_v)
        shared = scores_of(jnp.concatenate(rows, axis=0), k)
        own = jnp.concatenate(own, axis=0)
        top = jnp.maximum(
            jnp.max(shared, axis=1, keepdims=True), jnp.max(own, axis=1, keepdims=True)
        )
        shared = jnp.exp2((shared - top) * scale2)
        own = jnp.exp2((own - top) * scale2)
        total = jnp.sum(shared, axis=1, keepdims=True) + jnp.sum(own, axis=1, keepdims=True)
        own = own.astype(jnp.bfloat16)
        mixed = jnp.dot(shared.astype(jnp.bfloat16), v, preferred_element_type=jnp.float32)
        for r in range(responses):
            low = 16 * r
            part = mixed[low : low + 16] + jnp.dot(
                own[low : low + 16], own_v[r], preferred_element_type=jnp.float32
            )
            part = part * (1.0 / total[low : low + 16])
            part = part.astype(jnp.bfloat16).astype(jnp.float32)
            for n, h in enumerate(heads):
                partial[r] = partial[r] + part[8 * n : 8 * n + 8] * probe[h : h + 1, :]

    def attend(r, g):
        k, v = keys_values(g)
        own_k, own_v = own_keys_values(r, g)
        low = 2 * g * HEAD_DIM
        rows = jnp.concatenate(
            [q[r, :, low : low + HEAD_DIM], q[r, :, low + HEAD_DIM : low + 2 * HEAD_DIM]], axis=0
        )
        own = scores_of(rows, own_k)
        t = lax.broadcasted_iota(jnp.int32, own.shape, 0)
        t = jnp.where(t >= steps, t - steps, t)
        u = lax.broadcasted_iota(jnp.int32, own.shape, 1)
        own = jnp.where(u <= t, own, -1e30)
        mixed = attention([scores_of(rows, k), own], [v, own_v], scale2)
        live = lax.broadcasted_iota(jnp.int32, (steps, HEAD_DIM), 0) < lengths[r]
        for n in range(2):
            part = jnp.where(live, mixed[n * steps : (n + 1) * steps], 0.0)
            context[r, :, low + n * HEAD_DIM : low + (n + 1) * HEAD_DIM] = part.astype(jnp.bfloat16)

    wait_bytes(all_a.at[pl.ds(0, NXY - 1)], recv_sem.at[0])
    for g in range(2):
        reward_of(g)

    wait_bytes(all_b.at[pl.ds(0, NZX - 1)], recv_sem.at[1])
    for g in range(2, kv_heads):
        reward_of(g)

    lane = lax.broadcasted_iota(jnp.int32, (1, HEAD_DIM), 1)
    sums = [jnp.sum(part[0:1], axis=1, keepdims=True) for part in partial]
    row = jnp.where(lane == mine, sums[0] + sums[1], 0.0)
    for r in range(responses):
        row = jnp.where(lane == PROMPTS + r, sums[r], row)

    zt = zh * NT + tp
    rounds = (
        (row_1, zt, [(at_z(dz), at_tp(dt)) for dz, dt in FAR_ZT]),
        (row_2, xy, [(beside_xy(*offset), tp) for offset in FAR_XY]),
    )

    def send_row(n, row):
        ref, slot, devices = rounds[n]
        ref[slot] = row
        for device in devices:
            pltpu.make_async_remote_copy(
                src_ref=ref.at[slot],
                dst_ref=ref.at[slot],
                send_sem=send_sem.at[2 + n],
                recv_sem=recv_sem.at[2 + n],
                device_id=device,
                device_id_type=MESH,
            ).start()

    def wait_rows(n):
        ref, _, devices = rounds[n]
        wait_bytes(ref.at[pl.ds(0, len(devices))], recv_sem.at[2 + n])

    send_row(0, row)
    for g in range(2):
        for r in range(responses):
            attend(r, g)
    wait_rows(0)
    rewards = jnp.sum(row_1[pl.ds(zh * NT, NT)], axis=0)
    send_row(1, jnp.sum(row_1[...], axis=0))
    for g in range(2, kv_heads):
        for r in range(responses):
            attend(r, g)
    wait_rows(1)
    table = jnp.sum(row_2[...], axis=0)
    group = jnp.sum(jnp.where(lane == mine, table, 0.0), axis=1, keepdims=True) / BEST
    advantage[...] = rewards - group

    for copy in first:
        copy.wait_send()
    for copy in second:
        copy.wait_send()
    wait_bytes(out_a.at[pl.ds(0, NXY - 1)], send_sem.at[0])
    wait_bytes(out_b.at[pl.ds(0, NZX - 1)], send_sem.at[1])
    for n, (ref, _, devices) in enumerate(rounds):
        wait_bytes(ref.at[pl.ds(0, len(devices))], send_sem.at[2 + n])


def shards(response_queries, response_kv, prompt_kv, response_lengths, device_prompt, probe_weight):
    bf16 = jnp.bfloat16
    vmem = pl.BlockSpec(memory_space=pltpu.VMEM)
    anywhere = pl.BlockSpec(memory_space=pl.ANY)
    in_hbm = functools.partial(pltpu.with_memory_space_constraint, memory_space=pltpu.HBM)
    block = (PROMPTS, ROWS, HEAD_DIM)
    context, advantage = pl.pallas_call(
        kernel,
        out_shape=(
            pltpu.VMEM(response_queries.shape, bf16),
            pltpu.VMEM((1, HEAD_DIM), jnp.float32),
        ),
        in_specs=[anywhere] * 6,
        out_specs=(vmem, vmem),
        scratch_shapes=[
            pltpu.SMEM(response_lengths.shape, jnp.int32),
            pltpu.SMEM(device_prompt.shape, jnp.int32),
            pltpu.VMEM((probe_weight.shape[0] // HEAD_DIM, HEAD_DIM), jnp.float32),
            pltpu.VMEM(response_queries.shape, bf16),
            pltpu.VMEM(response_kv.shape, bf16),
            pltpu.VMEM(prompt_kv.shape, bf16),
            pltpu.VMEM(block, bf16),
            pltpu.VMEM(block, bf16),
            pltpu.VMEM((NZ - 1,) + block, bf16),
            pltpu.VMEM((NY - 1,) + block, bf16),
            pltpu.VMEM((PROMPTS, PIECES, NZ * TOKENS, HEAD_DIM), bf16),
            pltpu.VMEM((PROMPTS, PIECES, NY * TOKENS, HEAD_DIM), bf16),
            pltpu.VMEM((NXY, PIECES, NZ * TOKENS, HEAD_DIM), bf16),
            pltpu.VMEM((NZX, PIECES, NY * TOKENS, HEAD_DIM), bf16),
            pltpu.VMEM((NXY, PIECES, NZ * TOKENS, HEAD_DIM), bf16),
            pltpu.VMEM((NZX, PIECES, NY * TOKENS, HEAD_DIM), bf16),
            pltpu.VMEM((NZ * NT, 1, HEAD_DIM), jnp.float32),
            pltpu.VMEM((NXY, 1, HEAD_DIM), jnp.float32),
            pltpu.SemaphoreType.REGULAR((2,)),
            pltpu.SemaphoreType.DMA((6,)),
            pltpu.SemaphoreType.DMA((12,)),
            pltpu.SemaphoreType.DMA((12,)),
            pltpu.SemaphoreType.DMA((4,)),
            pltpu.SemaphoreType.DMA((4,)),
        ],
        compiler_params=pltpu.CompilerParams(
            collective_id=0, has_side_effects=True, vmem_limit_bytes=48 * 1024 * 1024
        ),
        cost_estimate=pl.CostEstimate(
            flops=700_000_000, bytes_accessed=2_000_000, transcendentals=1_400_000
        ),
    )(
        in_hbm(response_lengths),
        in_hbm(device_prompt),
        in_hbm(probe_weight.reshape(-1, HEAD_DIM)),
        in_hbm(response_queries),
        in_hbm(response_kv),
        in_hbm(prompt_kv),
    )
    return context, advantage[0, PROMPTS : PROMPTS + response_lengths.shape[0]]


def solution(mesh):
    placed = (
        P("resp", None, "tp"),
        P(None, "resp", None, "tp"),
        P(None, None, "resp", "tp"),
        P("resp"),
        P(),
        P("tp"),
    )
    return jax.shard_map(
        shards,
        mesh=mesh,
        in_specs=placed,
        out_specs=(P("resp", None, "tp"), P("resp")),
        check_vma=False,
    )
```

```python
import functools
import math

import jax
import jax.numpy as jnp
from jax import lax
from jax.experimental import pallas as pl
from jax.experimental.pallas import tpu as pltpu
from jax.sharding import PartitionSpec as P

HEAD_DIM = 128
SCALAR = 144
BEST = 16
MESH = pl.DeviceIdType.MESH

NZ, NX, NY, NT = 4, 4, 8, 4
NXY, NZX = NX * NY, NZ * NX
PROMPTS = 16
TOKENS = 4
PIECES = 4
ROWS = PIECES * TOKENS


def far_first(first, second):
    places = [(a, b) for a in range(first[0]) for b in range(second[0]) if (a, b) != (0, 0)]
    hops = lambda n, step: min(n[0] - step, step) * n[1]
    return sorted(places, key=lambda p: (-hops(first, p[0]) - hops(second, p[1]), p))


FAR_XY = far_first((NX, 1), (NY, 1))
FAR_ZX = far_first((NZ, 2), (NX, 1))
FAR_ZT = far_first((NZ, 2), (NT, 1))


def attention(scores_parts, values, scale2):
    top = functools.reduce(jnp.maximum, [jnp.max(s, axis=1, keepdims=True) for s in scores_parts])
    weights = [jnp.exp2((s - top) * scale2) for s in scores_parts]
    total = functools.reduce(jnp.add, [jnp.sum(w, axis=1, keepdims=True) for w in weights])
    mixed = functools.reduce(
        jnp.add,
        [
            jnp.dot(w.astype(jnp.bfloat16), v, preferred_element_type=jnp.float32)
            for w, v in zip(weights, values)
        ],
    )
    return mixed * (1.0 / total)


def scores_of(q, k):
    return lax.dot_general(q, k, (((1,), (1,)), ((), ())), preferred_element_type=jnp.float32)


def kernel(
    lengths_hbm,
    prompts_hbm,
    probe_hbm,
    q_hbm,
    kv_hbm,
    raw_hbm,
    context,
    advantage,
    lengths,
    prompts,
    probe,
    q,
    kv,
    raw,
    own_a,
    own_b,
    got_a,
    got_b,
    by_prompt_a,
    by_prompt_b,
    out_a,
    out_b,
    all_a,
    all_b,
    row_1,
    row_2,
    lines,
    load_sem,
    ring_send,
    ring_recv,
    send_sem,
    recv_sem,
):
    me = lax.axis_index("resp")
    tp = lax.axis_index("tp")
    zh = lax.div(me, NXY)
    xy = lax.rem(me, NXY)
    x = lax.div(xy, NY)
    y = lax.rem(xy, NY)
    zx = zh * NX + x

    def at_z(step):
        return lax.rem(zh + step, NZ) * NXY + xy

    def at_y(step):
        return zh * NXY + x * NY + lax.rem(y + step, NY)

    def at_x(step):
        return zh * NXY + lax.rem(x + step, NX) * NY + y

    def at_tp(step):
        return lax.rem(tp + step, NT)

    barrier = pltpu.get_barrier_semaphore()

    def greet(device, tp_index):
        pl.semaphore_signal(barrier, inc=1, device_id=(device, tp_index), device_id_type=MESH)

    for i in (2, 6, 1, 7):
        greet(at_y(i), tp)
    for i in (1, 3):
        greet(at_z(i), tp)
    for i in (2, 1, 3):
        greet(at_x(i), tp)
    for i in (2, 3, 1):
        greet(me, at_tp(i))

    load_raw = pltpu.make_async_copy(raw_hbm, raw, load_sem.at[0])
    load_prompts = pltpu.make_async_copy(prompts_hbm, prompts, load_sem.at[1])
    load_rest = [
        pltpu.make_async_copy(src, dst, load_sem.at[2 + n])
        for n, (src, dst) in enumerate(
            ((q_hbm, q), (kv_hbm, kv), (lengths_hbm, lengths), (probe_hbm, probe))
        )
    ]
    load_raw.start()
    load_prompts.start()
    for load in load_rest:
        load.start()

    load_raw.wait()

    def split(p, c):
        k = raw[0, p].astype(jnp.float32)
        v = raw[1, p].astype(jnp.float32)
        for plan, dst in enumerate((own_a, own_b)):
            parts = [
                part[:, (2 * plan + h) * HEAD_DIM : (2 * plan + h + 1) * HEAD_DIM]
                for part in (k, v)
                for h in range(2)
            ]
            dst[p] = jnp.concatenate(parts, axis=0).astype(jnp.bfloat16)
        return c

    lax.fori_loop(0, PROMPTS, split, 0)

    pl.semaphore_wait(barrier, 4 + 2 + (NX - 1) + (NT - 1))

    half = PROMPTS // 2
    lo, hi = pl.ds(0, half), pl.ds(half, half)

    def ring(index, src, dst, device):
        return pltpu.make_async_remote_copy(
            src_ref=src,
            dst_ref=dst,
            send_sem=ring_send.at[index],
            recv_sem=ring_recv.at[index],
            device_id=(device, tp),
            device_id_type=MESH,
        )

    first = [
        ring(0, own_a, got_a.at[0], at_z(1)),
        ring(1, own_a, got_a.at[1], at_z(NZ - 1)),
        ring(2, own_b, got_b.at[2], at_y(2)),
        ring(3, own_b, got_b.at[3], at_y(NY - 2)),
        ring(4, own_b, got_b.at[0], at_y(1)),
        ring(5, own_b, got_b.at[1], at_y(NY - 1)),
    ]
    second = [
        ring(6, got_a.at[0, lo], got_a.at[2, lo], at_z(1)),
        ring(7, got_a.at[1, hi], got_a.at[2, hi], at_z(NZ - 1)),
        ring(8, got_b.at[2, lo], got_b.at[6, lo], at_y(2)),
        ring(9, got_b.at[2], got_b.at[4], at_y(1)),
        ring(10, got_b.at[3, hi], got_b.at[6, hi], at_y(NY - 2)),
        ring(11, got_b.at[3], got_b.at[5], at_y(NY - 1)),
    ]
    for n in (2, 3, 0, 1, 4, 5):
        first[n].start()
    for device in (at_y(2), at_y(NY - 2), at_z(NZ - 1)):
        pl.semaphore_signal(lines.at[2], inc=1, device_id=(device, tp), device_id_type=MESH)
    pl.semaphore_wait(lines.at[2], 3)
    for i in range(1, NX):
        pl.semaphore_signal(lines.at[0], inc=1, device_id=(at_x(i), tp), device_id_type=MESH)
    for i in range(1, NZ):
        pl.semaphore_signal(lines.at[1], inc=1, device_id=(at_z(i), tp), device_id_type=MESH)
    first[2].wait_recv()
    second[2].start()
    second[3].start()
    first[3].wait_recv()
    second[4].start()
    second[5].start()
    first[0].wait_recv()
    second[0].start()
    first[1].wait_recv()
    second[1].start()
    second[0].wait_recv()
    second[1].wait_recv()

    def regroup(own, got, slots, dst):
        def one(p, c):
            tiles = [own[p]] + [got[s, p] for s in range(slots)]
            tiles = [t.astype(jnp.float32) for t in tiles]
            for g in range(PIECES):
                rows = [t[TOKENS * g : TOKENS * (g + 1)] for t in tiles]
                dst[p, g] = jnp.concatenate(rows, axis=0).astype(jnp.bfloat16)
            return c

        def four(i, c):
            for n in range(4):
                one(4 * i + n, c)
            return c

        lax.fori_loop(0, PROMPTS // 4, four, 0)

    def beside_xy(dx, dy):
        return zh * NXY + lax.rem(x + dx, NX) * NY + lax.rem(y + dy, NY)

    def beside_zx(dz, dx):
        return lax.rem(zh + dz, NZ) * NXY + lax.rem(x + dx, NX) * NY + y

    def send(plan, slots, places, by_prompt, out, everyone, mine_at):
        blocks = [by_prompt[prompts[j]] for j in places]
        for i, block in zip(slots, blocks):
            out[i] = block
        for i, j in zip(slots, places):
            pltpu.make_async_remote_copy(
                src_ref=out.at[i],
                dst_ref=everyone.at[mine_at],
                send_sem=send_sem.at[plan],
                recv_sem=recv_sem.at[plan],
                device_id=(j, tp),
                device_id_type=MESH,
            ).start()

    def send_a(low, high):
        places = [beside_xy(*offset) for offset in FAR_XY[low:high]]
        send(0, range(low, high), places, by_prompt_a, out_a, all_a, xy)

    def send_b(low, high):
        places = [beside_zx(*offset) for offset in FAR_ZX[low:high]]
        send(1, range(low, high), places, by_prompt_b, out_b, all_b, zx)

    regroup(own_a, got_a, NZ - 1, by_prompt_a)
    load_prompts.wait()
    pl.semaphore_wait(lines.at[0], NX - 1)
    pl.semaphore_wait(lines.at[1], NZ - 1)

    for low in range(0, NXY // 2, 4):
        send_a(low, low + 4)
    first[4].wait_recv()
    first[5].wait_recv()
    for copy in second[2:]:
        copy.wait_recv()
    regroup(own_b, got_b, NY - 1, by_prompt_b)

    for low in range(0, NZX - 1, 5):
        send_b(low, low + 5)
    for low in range(NXY // 2, NXY - 1, 5):
        send_a(low, low + 5)

    mine = prompts[me]
    all_a[xy] = by_prompt_a[mine]
    all_b[zx] = by_prompt_b[mine]

    for load in load_rest:
        load.wait()
    responses, steps, width = q.shape
    scale2 = math.log2(math.e) / math.sqrt(SCALAR)
    kv_heads = kv.shape[3] // HEAD_DIM
    column = lax.broadcasted_iota(jnp.int32, (8, steps), 1)
    last_q = []
    for r in range(responses):
        pick = (column == lengths[r] - 1).astype(jnp.bfloat16)
        last_q.append(jnp.dot(pick, q[r], preferred_element_type=jnp.float32).astype(jnp.bfloat16))

    def keys_values(g):
        ref = (all_a, all_b)[g // 2]
        h = g % 2
        return (
            ref[:, h].reshape(-1, HEAD_DIM),
            ref[:, 2 + h].reshape(-1, HEAD_DIM),
        )

    def own_keys_values(r, g):
        columns = slice(g * HEAD_DIM, (g + 1) * HEAD_DIM)
        return kv[0, r, :, columns], kv[1, r, :, columns]

    def wait_bytes(ref, sem):
        pltpu.make_async_copy(ref, ref, sem).wait()

    partial = [jnp.zeros((8, HEAD_DIM), jnp.float32) for _ in range(responses)]

    def reward_of(g):
        k, v = keys_values(g)
        heads = (2 * g, 2 * g + 1)
        rows = [
            jnp.concatenate([last[:, h * HEAD_DIM : (h + 1) * HEAD_DIM] for h in heads], axis=0)
            for last in last_q
        ]
        own, own_v = [], []
        for r in range(responses):
            its_k, its_v = own_keys_values(r, g)
            scores = scores_of(rows[r], its_k)
            seen = lax.broadcasted_iota(jnp.int32, scores.shape, 1) < lengths[r]
            own.append(jnp.where(seen, scores, -1e30))
            own_v.append(its_v)
        shared = scores_of(jnp.concatenate(rows, axis=0), k)
        own = jnp.concatenate(own, axis=0)
        top = jnp.maximum(
            jnp.max(shared, axis=1, keepdims=True), jnp.max(own, axis=1, keepdims=True)
        )
        shared = jnp.exp2((shared - top) * scale2)
        own = jnp.exp2((own - top) * scale2)
        total = jnp.sum(shared, axis=1, keepdims=True) + jnp.sum(own, axis=1, keepdims=True)
        own = own.astype(jnp.bfloat16)
        mixed = jnp.dot(shared.astype(jnp.bfloat16), v, preferred_element_type=jnp.float32)
        for r in range(responses):
            low = 16 * r
            part = mixed[low : low + 16] + jnp.dot(
                own[low : low + 16], own_v[r], preferred_element_type=jnp.float32
            )
            part = part * (1.0 / total[low : low + 16])
            part = part.astype(jnp.bfloat16).astype(jnp.float32)
            for n, h in enumerate(heads):
                partial[r] = partial[r] + part[8 * n : 8 * n + 8] * probe[h : h + 1, :]

    def attend(r, g):
        k, v = keys_values(g)
        own_k, own_v = own_keys_values(r, g)
        low = 2 * g * HEAD_DIM
        rows = jnp.concatenate(
            [q[r, :, low : low + HEAD_DIM], q[r, :, low + HEAD_DIM : low + 2 * HEAD_DIM]], axis=0
        )
        own = scores_of(rows, own_k)
        t = lax.broadcasted_iota(jnp.int32, own.shape, 0)
        t = jnp.where(t >= steps, t - steps, t)
        u = lax.broadcasted_iota(jnp.int32, own.shape, 1)
        own = jnp.where(u <= t, own, -1e30)
        mixed = attention([scores_of(rows, k), own], [v, own_v], scale2)
        live = lax.broadcasted_iota(jnp.int32, (steps, HEAD_DIM), 0) < lengths[r]
        for n in range(2):
            part = jnp.where(live, mixed[n * steps : (n + 1) * steps], 0.0)
            context[r, :, low + n * HEAD_DIM : low + (n + 1) * HEAD_DIM] = part.astype(jnp.bfloat16)

    wait_bytes(all_a.at[pl.ds(0, NXY - 1)], recv_sem.at[0])
    for g in range(2):
        reward_of(g)

    wait_bytes(all_b.at[pl.ds(0, NZX - 1)], recv_sem.at[1])
    for g in range(2, kv_heads):
        reward_of(g)

    lane = lax.broadcasted_iota(jnp.int32, (1, HEAD_DIM), 1)
    sums = [jnp.sum(part[0:1], axis=1, keepdims=True) for part in partial]
    row = jnp.where(lane == mine, sums[0] + sums[1], 0.0)
    for r in range(responses):
        row = jnp.where(lane == PROMPTS + r, sums[r], row)

    zt = zh * NT + tp
    rounds = (
        (row_1, zt, [(at_z(dz), at_tp(dt)) for dz, dt in FAR_ZT]),
        (row_2, xy, [(beside_xy(*offset), tp) for offset in FAR_XY]),
    )

    def send_row(n, row):
        ref, slot, devices = rounds[n]
        ref[slot] = row
        for device in devices:
            pltpu.make_async_remote_copy(
                src_ref=ref.at[slot],
                dst_ref=ref.at[slot],
                send_sem=send_sem.at[2 + n],
                recv_sem=recv_sem.at[2 + n],
                device_id=device,
                device_id_type=MESH,
            ).start()

    def wait_rows(n):
        ref, _, devices = rounds[n]
        wait_bytes(ref.at[pl.ds(0, len(devices))], recv_sem.at[2 + n])

    send_row(0, row)
    for g in range(2):
        for r in range(responses):
            attend(r, g)
    wait_rows(0)
    rewards = jnp.sum(row_1[pl.ds(zh * NT, NT)], axis=0)
    send_row(1, jnp.sum(row_1[...], axis=0))
    for g in range(2, kv_heads):
        for r in range(responses):
            attend(r, g)
    wait_rows(1)
    table = jnp.sum(row_2[...], axis=0)
    group = jnp.sum(jnp.where(lane == mine, table, 0.0), axis=1, keepdims=True) / BEST
    advantage[...] = rewards - group

    for copy in first:
        copy.wait_send()
    for copy in second:
        copy.wait_send()
    wait_bytes(out_a.at[pl.ds(0, NXY - 1)], send_sem.at[0])
    wait_bytes(out_b.at[pl.ds(0, NZX - 1)], send_sem.at[1])
    for n, (ref, _, devices) in enumerate(rounds):
        wait_bytes(ref.at[pl.ds(0, len(devices))], send_sem.at[2 + n])


def shards(response_queries, response_kv, prompt_kv, response_lengths, device_prompt, probe_weight):
    bf16 = jnp.bfloat16
    vmem = pl.BlockSpec(memory_space=pltpu.VMEM)
    anywhere = pl.BlockSpec(memory_space=pl.ANY)
    in_hbm = functools.partial(pltpu.with_memory_space_constraint, memory_space=pltpu.HBM)
    block = (PROMPTS, ROWS, HEAD_DIM)
    context, advantage = pl.pallas_call(
        kernel,
        out_shape=(
            pltpu.VMEM(response_queries.shape, bf16),
            pltpu.VMEM((1, HEAD_DIM), jnp.float32),
        ),
        in_specs=[anywhere] * 6,
        out_specs=(vmem, vmem),
        scratch_shapes=[
            pltpu.SMEM(response_lengths.shape, jnp.int32),
            pltpu.SMEM(device_prompt.shape, jnp.int32),
            pltpu.VMEM((probe_weight.shape[0] // HEAD_DIM, HEAD_DIM), jnp.float32),
            pltpu.VMEM(response_queries.shape, bf16),
            pltpu.VMEM(response_kv.shape, bf16),
            pltpu.VMEM(prompt_kv.shape, bf16),
            pltpu.VMEM(block, bf16),
            pltpu.VMEM(block, bf16),
            pltpu.VMEM((NZ - 1,) + block, bf16),
            pltpu.VMEM((NY - 1,) + block, bf16),
            pltpu.VMEM((PROMPTS, PIECES, NZ * TOKENS, HEAD_DIM), bf16),
            pltpu.VMEM((PROMPTS, PIECES, NY * TOKENS, HEAD_DIM), bf16),
            pltpu.VMEM((NXY, PIECES, NZ * TOKENS, HEAD_DIM), bf16),
            pltpu.VMEM((NZX, PIECES, NY * TOKENS, HEAD_DIM), bf16),
            pltpu.VMEM((NXY, PIECES, NZ * TOKENS, HEAD_DIM), bf16),
            pltpu.VMEM((NZX, PIECES, NY * TOKENS, HEAD_DIM), bf16),
            pltpu.VMEM((NZ * NT, 1, HEAD_DIM), jnp.float32),
            pltpu.VMEM((NXY, 1, HEAD_DIM), jnp.float32),
            pltpu.SemaphoreType.REGULAR((3,)),
            pltpu.SemaphoreType.DMA((6,)),
            pltpu.SemaphoreType.DMA((12,)),
            pltpu.SemaphoreType.DMA((12,)),
            pltpu.SemaphoreType.DMA((4,)),
            pltpu.SemaphoreType.DMA((4,)),
        ],
        compiler_params=pltpu.CompilerParams(
            collective_id=0, has_side_effects=True, vmem_limit_bytes=48 * 1024 * 1024
        ),
        cost_estimate=pl.CostEstimate(
            flops=700_000_000, bytes_accessed=2_000_000, transcendentals=1_400_000
        ),
    )(
        in_hbm(response_lengths),
        in_hbm(device_prompt),
        in_hbm(probe_weight.reshape(-1, HEAD_DIM)),
        in_hbm(response_queries),
        in_hbm(response_kv),
        in_hbm(prompt_kv),
    )
    return context, advantage[0, PROMPTS : PROMPTS + response_lengths.shape[0]]


def solution(mesh):
    placed = (
        P("resp", None, "tp"),
        P(None, "resp", None, "tp"),
        P(None, None, "resp", "tp"),
        P("resp"),
        P(),
        P("tp"),
    )
    return jax.shard_map(
        shards,
        mesh=mesh,
        in_specs=placed,
        out_specs=(P("resp", None, "tp"), P("resp")),
        check_vma=False,
    )
```

```python
import functools
import math

import jax
import jax.numpy as jnp
from jax import lax
from jax.experimental import pallas as pl
from jax.experimental.pallas import tpu as pltpu
from jax.sharding import PartitionSpec as P

HEAD_DIM = 128
SCALAR = 144
BEST = 16
MESH = pl.DeviceIdType.MESH

NZ, NX, NY, NT = 4, 4, 8, 4
NXY, NZX = NX * NY, NZ * NX
PROMPTS = 16
TOKENS = 4
PIECES = 4
ROWS = PIECES * TOKENS


def far_first(first, second):
    places = [(a, b) for a in range(first[0]) for b in range(second[0]) if (a, b) != (0, 0)]
    hops = lambda n, step: min(n[0] - step, step) * n[1]
    return sorted(places, key=lambda p: (-hops(first, p[0]) - hops(second, p[1]), p))


FAR_XY = far_first((NX, 1), (NY, 1))
FAR_ZX = [p for p in far_first((NZ, 2), (NX, 1)) if p[0] != 2]
FAR_ZT = far_first((NZ, 2), (NT, 1))


def attention(scores_parts, values, scale2):
    top = functools.reduce(jnp.maximum, [jnp.max(s, axis=1, keepdims=True) for s in scores_parts])
    weights = [jnp.exp2((s - top) * scale2) for s in scores_parts]
    total = functools.reduce(jnp.add, [jnp.sum(w, axis=1, keepdims=True) for w in weights])
    mixed = functools.reduce(
        jnp.add,
        [
            jnp.dot(w.astype(jnp.bfloat16), v, preferred_element_type=jnp.float32)
            for w, v in zip(weights, values)
        ],
    )
    return mixed * (1.0 / total)


def scores_of(q, k):
    return lax.dot_general(q, k, (((1,), (1,)), ((), ())), preferred_element_type=jnp.float32)


def kernel(
    lengths_hbm,
    prompts_hbm,
    probe_hbm,
    q_hbm,
    kv_hbm,
    raw_hbm,
    context,
    advantage,
    lengths,
    prompts,
    probe,
    q,
    kv,
    raw,
    own_a,
    own_b,
    got_a,
    got_b,
    by_prompt_a,
    by_prompt_b,
    out_a,
    out_b,
    out_relay,
    got_relay,
    all_a,
    all_b,
    row_1,
    row_2,
    lines,
    relay_send,
    relay_recv,
    load_sem,
    ring_send,
    ring_recv,
    send_sem,
    recv_sem,
):
    me = lax.axis_index("resp")
    tp = lax.axis_index("tp")
    zh = lax.div(me, NXY)
    xy = lax.rem(me, NXY)
    x = lax.div(xy, NY)
    y = lax.rem(xy, NY)
    zx = zh * NX + x

    def at_z(step):
        return lax.rem(zh + step, NZ) * NXY + xy

    def at_y(step):
        return zh * NXY + x * NY + lax.rem(y + step, NY)

    def at_x(step):
        return zh * NXY + lax.rem(x + step, NX) * NY + y

    def at_tp(step):
        return lax.rem(tp + step, NT)

    barrier = pltpu.get_barrier_semaphore()

    def greet(device, tp_index):
        pl.semaphore_signal(barrier, inc=1, device_id=(device, tp_index), device_id_type=MESH)

    for i in (2, 6, 1, 7):
        greet(at_y(i), tp)
    for i in (1, 3):
        greet(at_z(i), tp)
    for i in (2, 1, 3):
        greet(at_x(i), tp)
    for i in (2, 3, 1):
        greet(me, at_tp(i))

    load_raw = pltpu.make_async_copy(raw_hbm, raw, load_sem.at[0])
    load_prompts = pltpu.make_async_copy(prompts_hbm, prompts, load_sem.at[1])
    load_rest = [
        pltpu.make_async_copy(src, dst, load_sem.at[2 + n])
        for n, (src, dst) in enumerate(
            ((q_hbm, q), (kv_hbm, kv), (lengths_hbm, lengths), (probe_hbm, probe))
        )
    ]
    load_raw.start()
    load_prompts.start()
    for load in load_rest:
        load.start()

    load_raw.wait()

    def split(p, c):
        k = raw[0, p].astype(jnp.float32)
        v = raw[1, p].astype(jnp.float32)
        for plan, dst in enumerate((own_a, own_b)):
            parts = [
                part[:, (2 * plan + h) * HEAD_DIM : (2 * plan + h + 1) * HEAD_DIM]
                for part in (k, v)
                for h in range(2)
            ]
            dst[p] = jnp.concatenate(parts, axis=0).astype(jnp.bfloat16)
        return c

    lax.fori_loop(0, PROMPTS, split, 0)

    pl.semaphore_wait(barrier, 4 + 2 + (NX - 1) + (NT - 1))

    half = PROMPTS // 2
    lo, hi = pl.ds(0, half), pl.ds(half, half)

    def ring(index, src, dst, device):
        return pltpu.make_async_remote_copy(
            src_ref=src,
            dst_ref=dst,
            send_sem=ring_send.at[index],
            recv_sem=ring_recv.at[index],
            device_id=(device, tp),
            device_id_type=MESH,
        )

    first = [
        ring(0, own_a, got_a.at[0], at_z(1)),
        ring(1, own_a, got_a.at[1], at_z(NZ - 1)),
        ring(2, own_b, got_b.at[2], at_y(2)),
        ring(3, own_b, got_b.at[3], at_y(NY - 2)),
        ring(4, own_b, got_b.at[0], at_y(1)),
        ring(5, own_b, got_b.at[1], at_y(NY - 1)),
    ]
    second = [
        ring(6, got_a.at[0, lo], got_a.at[2, lo], at_z(1)),
        ring(7, got_a.at[1, hi], got_a.at[2, hi], at_z(NZ - 1)),
        ring(8, got_b.at[2, lo], got_b.at[6, lo], at_y(2)),
        ring(9, got_b.at[2], got_b.at[4], at_y(1)),
        ring(10, got_b.at[3, hi], got_b.at[6, hi], at_y(NY - 2)),
        ring(11, got_b.at[3], got_b.at[5], at_y(NY - 1)),
    ]
    for n in (2, 3, 0, 1, 4, 5):
        first[n].start()
    for device in (at_y(2), at_y(NY - 2), at_z(NZ - 1)):
        pl.semaphore_signal(lines.at[2], inc=1, device_id=(device, tp), device_id_type=MESH)
    pl.semaphore_wait(lines.at[2], 3)
    for i in range(1, NX):
        pl.semaphore_signal(lines.at[0], inc=1, device_id=(at_x(i), tp), device_id_type=MESH)
    for i in range(1, NZ):
        pl.semaphore_signal(lines.at[1], inc=1, device_id=(at_z(i), tp), device_id_type=MESH)
    first[2].wait_recv()
    second[2].start()
    second[3].start()
    first[3].wait_recv()
    second[4].start()
    second[5].start()
    first[0].wait_recv()
    second[0].start()
    first[1].wait_recv()
    second[1].start()

    def regroup(tiles_of, dst, low):
        def one(p, c):
            tiles = [t.astype(jnp.float32) for t in tiles_of(p)]
            for g in range(PIECES):
                rows = [t[TOKENS * g : TOKENS * (g + 1)] for t in tiles]
                dst[p, g, low : low + ROWS] = jnp.concatenate(rows, axis=0).astype(jnp.bfloat16)
            return c

        def four(i, c):
            for n in range(4):
                one(4 * i + n, c)
            return c

        lax.fori_loop(0, PROMPTS // 4, four, 0)

    def beside_xy(dx, dy):
        return zh * NXY + lax.rem(x + dx, NX) * NY + lax.rem(y + dy, NY)

    def beside_zx(dz, dx):
        return lax.rem(zh + dz, NZ) * NXY + lax.rem(x + dx, NX) * NY + y

    def send(plan, slots, places, by_prompt, out, everyone, mine_at):
        blocks = [by_prompt[prompts[j]] for j in places]
        for i, block in zip(slots, blocks):
            out[i] = block
        for i, j in zip(slots, places):
            pltpu.make_async_remote_copy(
                src_ref=out.at[i],
                dst_ref=everyone.at[mine_at],
                send_sem=send_sem.at[plan],
                recv_sem=recv_sem.at[plan],
                device_id=(j, tp),
                device_id_type=MESH,
            ).start()

    def send_a(low, high):
        places = [beside_xy(*offset) for offset in FAR_XY[low:high]]
        send(0, range(low, high), places, by_prompt_a, out_a, all_a, xy)

    def send_b(low, high):
        places = [beside_zx(*offset) for offset in FAR_ZX[low:high]]
        send(1, range(low, high), places, by_prompt_b, out_b, all_b, zx)

    first[4].wait_recv()
    first[5].wait_recv()
    regroup(lambda p: [own_b[p], got_b[0, p], got_b[1, p], got_b[2, p]], by_prompt_b, 0)
    second[0].wait_recv()
    second[1].wait_recv()
    regroup(lambda p: [own_a[p], got_a[0, p], got_a[1, p], got_a[2, p]], by_prompt_a, 0)
    load_prompts.wait()
    pl.semaphore_wait(lines.at[0], NX - 1)
    pl.semaphore_wait(lines.at[1], NZ - 1)

    for low in range(0, NXY // 2, 4):
        send_a(low, low + 4)
    for copy in second[2:]:
        copy.wait_recv()
    regroup(lambda p: [got_b[s, p] for s in (3, 4, 5, 6)], by_prompt_b, ROWS)

    for dx in range(NX):
        block = by_prompt_b[prompts[beside_zx(2, dx)]]
        out_relay[0, dx] = block[:2]
        out_relay[1, dx] = block[2:]
    relays = [
        pltpu.make_async_remote_copy(
            src_ref=out_relay.at[way],
            dst_ref=got_relay.at[way],
            send_sem=relay_send.at[way],
            recv_sem=relay_recv.at[way],
            device_id=(at_z(step), tp),
            device_id_type=MESH,
        )
        for way, step in ((0, 1), (1, NZ - 1))
    ]
    for copy in relays:
        copy.start()
    send_b(0, 6)
    send_b(6, len(FAR_ZX))
    for low in range(NXY // 2, NXY - 1, 5):
        send_a(low, low + 5)

    for way, step in ((0, 1), (1, NZ - 1)):
        relays[way].wait_recv()
        origin = lax.rem(zh + NZ - step, NZ) * NX + x
        for dx in (2, 1, 3, 0):
            pltpu.make_async_remote_copy(
                src_ref=got_relay.at[way, dx],
                dst_ref=all_b.at[origin, pl.ds(2 * way, 2)],
                send_sem=send_sem.at[1],
                recv_sem=recv_sem.at[1],
                device_id=(beside_zx(step, dx), tp),
                device_id_type=MESH,
            ).start()

    mine = prompts[me]
    all_a[xy] = by_prompt_a[mine]
    all_b[zx] = by_prompt_b[mine]

    for load in load_rest:
        load.wait()
    responses, steps, width = q.shape
    scale2 = math.log2(math.e) / math.sqrt(SCALAR)
    kv_heads = kv.shape[3] // HEAD_DIM
    column = lax.broadcasted_iota(jnp.int32, (8, steps), 1)
    last_q = []
    for r in range(responses):
        pick = (column == lengths[r] - 1).astype(jnp.bfloat16)
        last_q.append(jnp.dot(pick, q[r], preferred_element_type=jnp.float32).astype(jnp.bfloat16))

    def keys_values(g):
        ref = (all_a, all_b)[g // 2]
        h = g % 2
        return (
            ref[:, h].reshape(-1, HEAD_DIM),
            ref[:, 2 + h].reshape(-1, HEAD_DIM),
        )

    def own_keys_values(r, g):
        columns = slice(g * HEAD_DIM, (g + 1) * HEAD_DIM)
        return kv[0, r, :, columns], kv[1, r, :, columns]

    def wait_bytes(ref, sem):
        pltpu.make_async_copy(ref, ref, sem).wait()

    partial = [jnp.zeros((8, HEAD_DIM), jnp.float32) for _ in range(responses)]

    def reward_of(g):
        k, v = keys_values(g)
        heads = (2 * g, 2 * g + 1)
        rows = [
            jnp.concatenate([last[:, h * HEAD_DIM : (h + 1) * HEAD_DIM] for h in heads], axis=0)
            for last in last_q
        ]
        own, own_v = [], []
        for r in range(responses):
            its_k, its_v = own_keys_values(r, g)
            scores = scores_of(rows[r], its_k)
            seen = lax.broadcasted_iota(jnp.int32, scores.shape, 1) < lengths[r]
            own.append(jnp.where(seen, scores, -1e30))
            own_v.append(its_v)
        shared = scores_of(jnp.concatenate(rows, axis=0), k)
        own = jnp.concatenate(own, axis=0)
        top = jnp.maximum(
            jnp.max(shared, axis=1, keepdims=True), jnp.max(own, axis=1, keepdims=True)
        )
        shared = jnp.exp2((shared - top) * scale2)
        own = jnp.exp2((own - top) * scale2)
        total = jnp.sum(shared, axis=1, keepdims=True) + jnp.sum(own, axis=1, keepdims=True)
        own = own.astype(jnp.bfloat16)
        mixed = jnp.dot(shared.astype(jnp.bfloat16), v, preferred_element_type=jnp.float32)
        for r in range(responses):
            low = 16 * r
            part = mixed[low : low + 16] + jnp.dot(
                own[low : low + 16], own_v[r], preferred_element_type=jnp.float32
            )
            part = part * (1.0 / total[low : low + 16])
            part = part.astype(jnp.bfloat16).astype(jnp.float32)
            for n, h in enumerate(heads):
                partial[r] = partial[r] + part[8 * n : 8 * n + 8] * probe[h : h + 1, :]

    def attend(r, g):
        k, v = keys_values(g)
        own_k, own_v = own_keys_values(r, g)
        low = 2 * g * HEAD_DIM
        rows = jnp.concatenate(
            [q[r, :, low : low + HEAD_DIM], q[r, :, low + HEAD_DIM : low + 2 * HEAD_DIM]], axis=0
        )
        own = scores_of(rows, own_k)
        t = lax.broadcasted_iota(jnp.int32, own.shape, 0)
        t = jnp.where(t >= steps, t - steps, t)
        u = lax.broadcasted_iota(jnp.int32, own.shape, 1)
        own = jnp.where(u <= t, own, -1e30)
        mixed = attention([scores_of(rows, k), own], [v, own_v], scale2)
        live = lax.broadcasted_iota(jnp.int32, (steps, HEAD_DIM), 0) < lengths[r]
        for n in range(2):
            part = jnp.where(live, mixed[n * steps : (n + 1) * steps], 0.0)
            context[r, :, low + n * HEAD_DIM : low + (n + 1) * HEAD_DIM] = part.astype(jnp.bfloat16)

    wait_bytes(all_a.at[pl.ds(0, NXY - 1)], recv_sem.at[0])
    for g in range(2):
        reward_of(g)

    wait_bytes(all_b.at[pl.ds(0, NZX - 1)], recv_sem.at[1])
    for g in range(2, kv_heads):
        reward_of(g)

    lane = lax.broadcasted_iota(jnp.int32, (1, HEAD_DIM), 1)
    sums = [jnp.sum(part[0:1], axis=1, keepdims=True) for part in partial]
    row = jnp.where(lane == mine, sums[0] + sums[1], 0.0)
    for r in range(responses):
        row = jnp.where(lane == PROMPTS + r, sums[r], row)

    zt = zh * NT + tp
    rounds = (
        (row_1, zt, [(at_z(dz), at_tp(dt)) for dz, dt in FAR_ZT]),
        (row_2, xy, [(beside_xy(*offset), tp) for offset in FAR_XY]),
    )

    def send_row(n, row):
        ref, slot, devices = rounds[n]
        ref[slot] = row
        for device in devices:
            pltpu.make_async_remote_copy(
                src_ref=ref.at[slot],
                dst_ref=ref.at[slot],
                send_sem=send_sem.at[2 + n],
                recv_sem=recv_sem.at[2 + n],
                device_id=device,
                device_id_type=MESH,
            ).start()

    def wait_rows(n):
        ref, _, devices = rounds[n]
        wait_bytes(ref.at[pl.ds(0, len(devices))], recv_sem.at[2 + n])

    send_row(0, row)
    order = [(r, g) for g in range(kv_heads) for r in range(responses)]
    for r, g in order[:3]:
        attend(r, g)
    wait_rows(0)
    rewards = jnp.sum(row_1[pl.ds(zh * NT, NT)], axis=0)
    send_row(1, jnp.sum(row_1[...], axis=0))
    for r, g in order[3:]:
        attend(r, g)
    wait_rows(1)
    table = jnp.sum(row_2[...], axis=0)
    group = jnp.sum(jnp.where(lane == mine, table, 0.0), axis=1, keepdims=True) / BEST
    advantage[...] = rewards - group

    for copy in first:
        copy.wait_send()
    for copy in second + relays:
        copy.wait_send()
    wait_bytes(out_a.at[pl.ds(0, NXY - 1)], send_sem.at[0])
    wait_bytes(out_b.at[pl.ds(0, NZX - 1)], send_sem.at[1])
    for n, (ref, _, devices) in enumerate(rounds):
        wait_bytes(ref.at[pl.ds(0, len(devices))], send_sem.at[2 + n])


def shards(response_queries, response_kv, prompt_kv, response_lengths, device_prompt, probe_weight):
    bf16 = jnp.bfloat16
    vmem = pl.BlockSpec(memory_space=pltpu.VMEM)
    anywhere = pl.BlockSpec(memory_space=pl.ANY)
    in_hbm = functools.partial(pltpu.with_memory_space_constraint, memory_space=pltpu.HBM)
    block = (PROMPTS, ROWS, HEAD_DIM)
    context, advantage = pl.pallas_call(
        kernel,
        out_shape=(
            pltpu.VMEM(response_queries.shape, bf16),
            pltpu.VMEM((1, HEAD_DIM), jnp.float32),
        ),
        in_specs=[anywhere] * 6,
        out_specs=(vmem, vmem),
        scratch_shapes=[
            pltpu.SMEM(response_lengths.shape, jnp.int32),
            pltpu.SMEM(device_prompt.shape, jnp.int32),
            pltpu.VMEM((probe_weight.shape[0] // HEAD_DIM, HEAD_DIM), jnp.float32),
            pltpu.VMEM(response_queries.shape, bf16),
            pltpu.VMEM(response_kv.shape, bf16),
            pltpu.VMEM(prompt_kv.shape, bf16),
            pltpu.VMEM(block, bf16),
            pltpu.VMEM(block, bf16),
            pltpu.VMEM((NZ - 1,) + block, bf16),
            pltpu.VMEM((NY - 1,) + block, bf16),
            pltpu.VMEM((PROMPTS, PIECES, NZ * TOKENS, HEAD_DIM), bf16),
            pltpu.VMEM((PROMPTS, PIECES, NY * TOKENS, HEAD_DIM), bf16),
            pltpu.VMEM((NXY, PIECES, NZ * TOKENS, HEAD_DIM), bf16),
            pltpu.VMEM((NZX, PIECES, NY * TOKENS, HEAD_DIM), bf16),
            pltpu.VMEM((2, NX, PIECES // 2, NY * TOKENS, HEAD_DIM), bf16),
            pltpu.VMEM((2, NX, PIECES // 2, NY * TOKENS, HEAD_DIM), bf16),
            pltpu.VMEM((NXY, PIECES, NZ * TOKENS, HEAD_DIM), bf16),
            pltpu.VMEM((NZX, PIECES, NY * TOKENS, HEAD_DIM), bf16),
            pltpu.VMEM((NZ * NT, 1, HEAD_DIM), jnp.float32),
            pltpu.VMEM((NXY, 1, HEAD_DIM), jnp.float32),
            pltpu.SemaphoreType.REGULAR((3,)),
            pltpu.SemaphoreType.DMA((2,)),
            pltpu.SemaphoreType.DMA((2,)),
            pltpu.SemaphoreType.DMA((6,)),
            pltpu.SemaphoreType.DMA((12,)),
            pltpu.SemaphoreType.DMA((12,)),
            pltpu.SemaphoreType.DMA((4,)),
            pltpu.SemaphoreType.DMA((4,)),
        ],
        compiler_params=pltpu.CompilerParams(
            collective_id=0, has_side_effects=True, vmem_limit_bytes=48 * 1024 * 1024
        ),
        cost_estimate=pl.CostEstimate(
            flops=700_000_000, bytes_accessed=2_000_000, transcendentals=1_400_000
        ),
    )(
        in_hbm(response_lengths),
        in_hbm(device_prompt),
        in_hbm(probe_weight.reshape(-1, HEAD_DIM)),
        in_hbm(response_queries),
        in_hbm(response_kv),
        in_hbm(prompt_kv),
    )
    return context, advantage[0, PROMPTS : PROMPTS + response_lengths.shape[0]]


def solution(mesh):
    placed = (
        P("resp", None, "tp"),
        P(None, "resp", None, "tp"),
        P(None, None, "resp", "tp"),
        P("resp"),
        P(),
        P("tp"),
    )
    return jax.shard_map(
        shards,
        mesh=mesh,
        in_specs=placed,
        out_specs=(P("resp", None, "tp"), P("resp")),
        check_vma=False,
    )
```

```python
import functools
import math

import jax
import jax.numpy as jnp
from jax import lax
from jax.experimental import pallas as pl
from jax.experimental.pallas import tpu as pltpu
from jax.sharding import PartitionSpec as P

HEAD_DIM = 128
SCALAR = 144
BEST = 16
MESH = pl.DeviceIdType.MESH

NZ, NX, NY, NT = 4, 4, 8, 4
NXY, NZX = NX * NY, NZ * NX
PROMPTS = 16
TOKENS = 4
PIECES = 4
ROWS = PIECES * TOKENS


def far_first(first, second):
    places = [(a, b) for a in range(first[0]) for b in range(second[0]) if (a, b) != (0, 0)]
    hops = lambda n, step: min(n[0] - step, step) * n[1]
    return sorted(places, key=lambda p: (-hops(first, p[0]) - hops(second, p[1]), p))


FAR_XY = far_first((NX, 1), (NY, 1))
FAR_ZX = far_first((NZ, 2), (NX, 1))
FAR_ZT = far_first((NZ, 2), (NT, 1))


def attention(scores_parts, values, scale2):
    top = functools.reduce(jnp.maximum, [jnp.max(s, axis=1, keepdims=True) for s in scores_parts])
    weights = [jnp.exp2((s - top) * scale2) for s in scores_parts]
    total = functools.reduce(jnp.add, [jnp.sum(w, axis=1, keepdims=True) for w in weights])
    mixed = functools.reduce(
        jnp.add,
        [
            jnp.dot(w.astype(jnp.bfloat16), v, preferred_element_type=jnp.float32)
            for w, v in zip(weights, values)
        ],
    )
    return mixed * (1.0 / total)


def scores_of(q, k):
    return lax.dot_general(q, k, (((1,), (1,)), ((), ())), preferred_element_type=jnp.float32)


def kernel(
    lengths_hbm,
    prompts_hbm,
    probe_hbm,
    q_hbm,
    kv_hbm,
    raw_hbm,
    context,
    advantage,
    lengths,
    prompts,
    probe,
    q,
    kv,
    raw,
    own_a,
    own_b,
    got_a,
    got_b,
    by_prompt_a,
    by_prompt_b,
    out_a,
    out_b,
    all_a,
    all_b,
    row_1,
    row_2,
    lines,
    load_sem,
    ring_send,
    ring_recv,
    send_sem,
    recv_sem,
):
    me = lax.axis_index("resp")
    tp = lax.axis_index("tp")
    zh = lax.div(me, NXY)
    xy = lax.rem(me, NXY)
    x = lax.div(xy, NY)
    y = lax.rem(xy, NY)
    zx = zh * NX + x

    def at_z(step):
        return lax.rem(zh + step, NZ) * NXY + xy

    def at_y(step):
        return zh * NXY + x * NY + lax.rem(y + step, NY)

    def at_x(step):
        return zh * NXY + lax.rem(x + step, NX) * NY + y

    def at_tp(step):
        return lax.rem(tp + step, NT)

    barrier = pltpu.get_barrier_semaphore()

    def greet(device, tp_index):
        pl.semaphore_signal(barrier, inc=1, device_id=(device, tp_index), device_id_type=MESH)

    for i in (2, 6, 1, 7):
        greet(at_y(i), tp)
    for i in (1, 3):
        greet(at_z(i), tp)
    for i in (2, 1, 3):
        greet(at_x(i), tp)
    for i in (2, 3, 1):
        greet(me, at_tp(i))

    load_raw = pltpu.make_async_copy(raw_hbm, raw, load_sem.at[0])
    load_prompts = pltpu.make_async_copy(prompts_hbm, prompts, load_sem.at[1])
    load_rest = [
        pltpu.make_async_copy(src, dst, load_sem.at[2 + n])
        for n, (src, dst) in enumerate(
            ((q_hbm, q), (kv_hbm, kv), (lengths_hbm, lengths), (probe_hbm, probe))
        )
    ]
    load_raw.start()
    load_prompts.start()
    for load in load_rest:
        load.start()

    load_raw.wait()

    def split(p, c):
        k = raw[0, p].astype(jnp.float32)
        v = raw[1, p].astype(jnp.float32)
        for plan, dst in enumerate((own_a, own_b)):
            parts = [
                part[:, (2 * plan + h) * HEAD_DIM : (2 * plan + h + 1) * HEAD_DIM]
                for part in (k, v)
                for h in range(2)
            ]
            dst[p] = jnp.concatenate(parts, axis=0).astype(jnp.bfloat16)
        return c

    lax.fori_loop(0, PROMPTS, split, 0)

    pl.semaphore_wait(barrier, 4 + 2 + (NX - 1) + (NT - 1))

    half = PROMPTS // 2
    lo, hi = pl.ds(0, half), pl.ds(half, half)

    def ring(index, src, dst, device):
        return pltpu.make_async_remote_copy(
            src_ref=src,
            dst_ref=dst,
            send_sem=ring_send.at[index],
            recv_sem=ring_recv.at[index],
            device_id=(device, tp),
            device_id_type=MESH,
        )

    first = [
        ring(0, own_a, got_a.at[0], at_z(1)),
        ring(1, own_a, got_a.at[1], at_z(NZ - 1)),
        ring(2, own_b, got_b.at[2], at_y(2)),
        ring(3, own_b, got_b.at[3], at_y(NY - 2)),
        ring(4, own_b, got_b.at[0], at_y(1)),
        ring(5, own_b, got_b.at[1], at_y(NY - 1)),
    ]
    second = [
        ring(6, got_a.at[0, lo], got_a.at[2, lo], at_z(1)),
        ring(7, got_a.at[1, hi], got_a.at[2, hi], at_z(NZ - 1)),
        ring(8, got_b.at[2, lo], got_b.at[6, lo], at_y(2)),
        ring(9, got_b.at[2], got_b.at[4], at_y(1)),
        ring(10, got_b.at[3, hi], got_b.at[6, hi], at_y(NY - 2)),
        ring(11, got_b.at[3], got_b.at[5], at_y(NY - 1)),
    ]
    for n in (2, 3, 0, 1, 4, 5):
        first[n].start()
    for device in (at_y(2), at_y(NY - 2), at_z(NZ - 1)):
        pl.semaphore_signal(lines.at[2], inc=1, device_id=(device, tp), device_id_type=MESH)
    pl.semaphore_wait(lines.at[2], 3)
    for i in range(1, NX):
        pl.semaphore_signal(lines.at[0], inc=1, device_id=(at_x(i), tp), device_id_type=MESH)
    for i in range(1, NZ):
        pl.semaphore_signal(lines.at[1], inc=1, device_id=(at_z(i), tp), device_id_type=MESH)
    first[2].wait_recv()
    second[2].start()
    second[3].start()
    first[3].wait_recv()
    second[4].start()
    second[5].start()
    first[0].wait_recv()
    second[0].start()
    first[1].wait_recv()
    second[1].start()

    def regroup(tiles_of, dst, low):
        def one(p, c):
            tiles = [t.astype(jnp.float32) for t in tiles_of(p)]
            for g in range(PIECES):
                rows = [t[TOKENS * g : TOKENS * (g + 1)] for t in tiles]
                dst[p, g, low : low + ROWS] = jnp.concatenate(rows, axis=0).astype(jnp.bfloat16)
            return c

        def four(i, c):
            for n in range(4):
                one(4 * i + n, c)
            return c

        lax.fori_loop(0, PROMPTS // 4, four, 0)

    def beside_xy(dx, dy):
        return zh * NXY + lax.rem(x + dx, NX) * NY + lax.rem(y + dy, NY)

    def beside_zx(dz, dx):
        return lax.rem(zh + dz, NZ) * NXY + lax.rem(x + dx, NX) * NY + y

    def send(plan, slots, places, by_prompt, out, everyone, mine_at):
        blocks = [by_prompt[prompts[j]] for j in places]
        for i, block in zip(slots, blocks):
            out[i] = block
        for i, j in zip(slots, places):
            pltpu.make_async_remote_copy(
                src_ref=out.at[i],
                dst_ref=everyone.at[mine_at],
                send_sem=send_sem.at[plan],
                recv_sem=recv_sem.at[plan],
                device_id=(j, tp),
                device_id_type=MESH,
            ).start()

    def send_a(low, high):
        places = [beside_xy(*offset) for offset in FAR_XY[low:high]]
        send(0, range(low, high), places, by_prompt_a, out_a, all_a, xy)

    def send_b(low, high):
        places = [beside_zx(*offset) for offset in FAR_ZX[low:high]]
        send(1, range(low, high), places, by_prompt_b, out_b, all_b, zx)

    first[4].wait_recv()
    first[5].wait_recv()
    regroup(lambda p: [own_b[p], got_b[0, p], got_b[1, p], got_b[2, p]], by_prompt_b, 0)
    load_prompts.wait()
    pl.semaphore_wait(lines.at[0], NX - 1)
    pl.semaphore_wait(lines.at[1], NZ - 1)
    second[0].wait_recv()
    second[1].wait_recv()
    regroup(lambda p: [own_a[p], got_a[0, p], got_a[1, p], got_a[2, p]], by_prompt_a, 0)

    for low in range(0, NXY // 2, 4):
        send_a(low, low + 4)
    for copy in second[2:]:
        copy.wait_recv()
    regroup(lambda p: [got_b[s, p] for s in (3, 4, 5, 6)], by_prompt_b, ROWS)

    for low in range(0, NZX - 1, 5):
        send_b(low, low + 5)
    for low in range(NXY // 2, NXY - 1, 5):
        send_a(low, low + 5)

    mine = prompts[me]
    all_a[xy] = by_prompt_a[mine]
    all_b[zx] = by_prompt_b[mine]

    for load in load_rest:
        load.wait()
    responses, steps, width = q.shape
    scale2 = math.log2(math.e) / math.sqrt(SCALAR)
    kv_heads = kv.shape[3] // HEAD_DIM
    column = lax.broadcasted_iota(jnp.int32, (8, steps), 1)
    last_q = []
    for r in range(responses):
        pick = (column == lengths[r] - 1).astype(jnp.bfloat16)
        last_q.append(jnp.dot(pick, q[r], preferred_element_type=jnp.float32).astype(jnp.bfloat16))

    def keys_values(g):
        ref = (all_a, all_b)[g // 2]
        h = g % 2
        return (
            ref[:, h].reshape(-1, HEAD_DIM),
            ref[:, 2 + h].reshape(-1, HEAD_DIM),
        )

    def own_keys_values(r, g):
        columns = slice(g * HEAD_DIM, (g + 1) * HEAD_DIM)
        return kv[0, r, :, columns], kv[1, r, :, columns]

    def wait_bytes(ref, sem):
        pltpu.make_async_copy(ref, ref, sem).wait()

    partial = [jnp.zeros((8, HEAD_DIM), jnp.float32) for _ in range(responses)]

    def reward_of(g):
        k, v = keys_values(g)
        heads = (2 * g, 2 * g + 1)
        rows = [
            jnp.concatenate([last[:, h * HEAD_DIM : (h + 1) * HEAD_DIM] for h in heads], axis=0)
            for last in last_q
        ]
        own, own_v = [], []
        for r in range(responses):
            its_k, its_v = own_keys_values(r, g)
            scores = scores_of(rows[r], its_k)
            seen = lax.broadcasted_iota(jnp.int32, scores.shape, 1) < lengths[r]
            own.append(jnp.where(seen, scores, -1e30))
            own_v.append(its_v)
        shared = scores_of(jnp.concatenate(rows, axis=0), k)
        own = jnp.concatenate(own, axis=0)
        top = jnp.maximum(
            jnp.max(shared, axis=1, keepdims=True), jnp.max(own, axis=1, keepdims=True)
        )
        shared = jnp.exp2((shared - top) * scale2)
        own = jnp.exp2((own - top) * scale2)
        total = jnp.sum(shared, axis=1, keepdims=True) + jnp.sum(own, axis=1, keepdims=True)
        own = own.astype(jnp.bfloat16)
        mixed = jnp.dot(shared.astype(jnp.bfloat16), v, preferred_element_type=jnp.float32)
        for r in range(responses):
            low = 16 * r
            part = mixed[low : low + 16] + jnp.dot(
                own[low : low + 16], own_v[r], preferred_element_type=jnp.float32
            )
            part = part * (1.0 / total[low : low + 16])
            part = part.astype(jnp.bfloat16).astype(jnp.float32)
            for n, h in enumerate(heads):
                partial[r] = partial[r] + part[8 * n : 8 * n + 8] * probe[h : h + 1, :]

    def attend(r, g):
        k, v = keys_values(g)
        own_k, own_v = own_keys_values(r, g)
        low = 2 * g * HEAD_DIM
        rows = jnp.concatenate(
            [q[r, :, low : low + HEAD_DIM], q[r, :, low + HEAD_DIM : low + 2 * HEAD_DIM]], axis=0
        )
        own = scores_of(rows, own_k)
        t = lax.broadcasted_iota(jnp.int32, own.shape, 0)
        t = jnp.where(t >= steps, t - steps, t)
        u = lax.broadcasted_iota(jnp.int32, own.shape, 1)
        own = jnp.where(u <= t, own, -1e30)
        mixed = attention([scores_of(rows, k), own], [v, own_v], scale2)
        live = lax.broadcasted_iota(jnp.int32, (steps, HEAD_DIM), 0) < lengths[r]
        for n in range(2):
            part = jnp.where(live, mixed[n * steps : (n + 1) * steps], 0.0)
            context[r, :, low + n * HEAD_DIM : low + (n + 1) * HEAD_DIM] = part.astype(jnp.bfloat16)

    wait_bytes(all_a.at[pl.ds(0, NXY - 1)], recv_sem.at[0])
    for g in range(2):
        reward_of(g)

    wait_bytes(all_b.at[pl.ds(0, NZX - 1)], recv_sem.at[1])
    for g in range(2, kv_heads):
        reward_of(g)

    lane = lax.broadcasted_iota(jnp.int32, (1, HEAD_DIM), 1)
    sums = [jnp.sum(part[0:1], axis=1, keepdims=True) for part in partial]
    row = jnp.where(lane == mine, sums[0] + sums[1], 0.0)
    for r in range(responses):
        row = jnp.where(lane == PROMPTS + r, sums[r], row)

    zt = zh * NT + tp
    rounds = (
        (row_1, zt, [(at_z(dz), at_tp(dt)) for dz, dt in FAR_ZT]),
        (row_2, xy, [(beside_xy(*offset), tp) for offset in FAR_XY]),
    )

    def send_row(n, row):
        ref, slot, devices = rounds[n]
        ref[slot] = row
        for device in devices:
            pltpu.make_async_remote_copy(
                src_ref=ref.at[slot],
                dst_ref=ref.at[slot],
                send_sem=send_sem.at[2 + n],
                recv_sem=recv_sem.at[2 + n],
                device_id=device,
                device_id_type=MESH,
            ).start()

    def wait_rows(n):
        ref, _, devices = rounds[n]
        wait_bytes(ref.at[pl.ds(0, len(devices))], recv_sem.at[2 + n])

    send_row(0, row)
    order = [(r, g) for g in range(kv_heads) for r in range(responses)]
    for r, g in order[:3]:
        attend(r, g)
    wait_rows(0)
    rewards = jnp.sum(row_1[pl.ds(zh * NT, NT)], axis=0)
    send_row(1, jnp.sum(row_1[...], axis=0))
    for r, g in order[3:]:
        attend(r, g)
    wait_rows(1)
    table = jnp.sum(row_2[...], axis=0)
    group = jnp.sum(jnp.where(lane == mine, table, 0.0), axis=1, keepdims=True) / BEST
    advantage[...] = rewards - group

    for copy in first:
        copy.wait_send()
    for copy in second:
        copy.wait_send()
    wait_bytes(out_a.at[pl.ds(0, NXY - 1)], send_sem.at[0])
    wait_bytes(out_b.at[pl.ds(0, NZX - 1)], send_sem.at[1])
    for n, (ref, _, devices) in enumerate(rounds):
        wait_bytes(ref.at[pl.ds(0, len(devices))], send_sem.at[2 + n])


def shards(response_queries, response_kv, prompt_kv, response_lengths, device_prompt, probe_weight):
    bf16 = jnp.bfloat16
    vmem = pl.BlockSpec(memory_space=pltpu.VMEM)
    anywhere = pl.BlockSpec(memory_space=pl.ANY)
    in_hbm = functools.partial(pltpu.with_memory_space_constraint, memory_space=pltpu.HBM)
    block = (PROMPTS, ROWS, HEAD_DIM)
    context, advantage = pl.pallas_call(
        kernel,
        out_shape=(
            pltpu.VMEM(response_queries.shape, bf16),
            pltpu.VMEM((1, HEAD_DIM), jnp.float32),
        ),
        in_specs=[anywhere] * 6,
        out_specs=(vmem, vmem),
        scratch_shapes=[
            pltpu.SMEM(response_lengths.shape, jnp.int32),
            pltpu.SMEM(device_prompt.shape, jnp.int32),
            pltpu.VMEM((probe_weight.shape[0] // HEAD_DIM, HEAD_DIM), jnp.float32),
            pltpu.VMEM(response_queries.shape, bf16),
            pltpu.VMEM(response_kv.shape, bf16),
            pltpu.VMEM(prompt_kv.shape, bf16),
            pltpu.VMEM(block, bf16),
            pltpu.VMEM(block, bf16),
            pltpu.VMEM((NZ - 1,) + block, bf16),
            pltpu.VMEM((NY - 1,) + block, bf16),
            pltpu.VMEM((PROMPTS, PIECES, NZ * TOKENS, HEAD_DIM), bf16),
            pltpu.VMEM((PROMPTS, PIECES, NY * TOKENS, HEAD_DIM), bf16),
            pltpu.VMEM((NXY, PIECES, NZ * TOKENS, HEAD_DIM), bf16),
            pltpu.VMEM((NZX, PIECES, NY * TOKENS, HEAD_DIM), bf16),
            pltpu.VMEM((NXY, PIECES, NZ * TOKENS, HEAD_DIM), bf16),
            pltpu.VMEM((NZX, PIECES, NY * TOKENS, HEAD_DIM), bf16),
            pltpu.VMEM((NZ * NT, 1, HEAD_DIM), jnp.float32),
            pltpu.VMEM((NXY, 1, HEAD_DIM), jnp.float32),
            pltpu.SemaphoreType.REGULAR((3,)),
            pltpu.SemaphoreType.DMA((6,)),
            pltpu.SemaphoreType.DMA((12,)),
            pltpu.SemaphoreType.DMA((12,)),
            pltpu.SemaphoreType.DMA((4,)),
            pltpu.SemaphoreType.DMA((4,)),
        ],
        compiler_params=pltpu.CompilerParams(
            collective_id=0, has_side_effects=True, vmem_limit_bytes=48 * 1024 * 1024
        ),
        cost_estimate=pl.CostEstimate(
            flops=700_000_000, bytes_accessed=2_000_000, transcendentals=1_400_000
        ),
    )(
        in_hbm(response_lengths),
        in_hbm(device_prompt),
        in_hbm(probe_weight.reshape(-1, HEAD_DIM)),
        in_hbm(response_queries),
        in_hbm(response_kv),
        in_hbm(prompt_kv),
    )
    return context, advantage[0, PROMPTS : PROMPTS + response_lengths.shape[0]]


def solution(mesh):
    placed = (
        P("resp", None, "tp"),
        P(None, "resp", None, "tp"),
        P(None, None, "resp", "tp"),
        P("resp"),
        P(),
        P("tp"),
    )
    return jax.shard_map(
        shards,
        mesh=mesh,
        in_specs=placed,
        out_specs=(P("resp", None, "tp"), P("resp")),
        check_vma=False,
    )
```

```python
import functools
import math

import jax
import jax.numpy as jnp
from jax import lax
from jax.experimental import pallas as pl
from jax.experimental.pallas import tpu as pltpu
from jax.sharding import PartitionSpec as P

HEAD_DIM = 128
SCALAR = 144
BEST = 16
MESH = pl.DeviceIdType.MESH

NZ, NX, NY, NT = 4, 4, 8, 4
NXY, NZX = NX * NY, NZ * NX
PROMPTS = 16
TOKENS = 4
PIECES = 4
ROWS = PIECES * TOKENS


def far_first(first, second):
    places = [(a, b) for a in range(first[0]) for b in range(second[0]) if (a, b) != (0, 0)]
    hops = lambda n, step: min(n[0] - step, step) * n[1]
    return sorted(places, key=lambda p: (-hops(first, p[0]) - hops(second, p[1]), p))


FAR_XY = far_first((NX, 1), (NY, 1))
FAR_ZX = far_first((NZ, 2), (NX, 1))
FAR_ZT = far_first((NZ, 2), (NT, 1))


def attention(scores_parts, values, scale2):
    top = functools.reduce(jnp.maximum, [jnp.max(s, axis=1, keepdims=True) for s in scores_parts])
    weights = [jnp.exp2((s - top) * scale2) for s in scores_parts]
    total = functools.reduce(jnp.add, [jnp.sum(w, axis=1, keepdims=True) for w in weights])
    mixed = functools.reduce(
        jnp.add,
        [
            jnp.dot(w.astype(jnp.bfloat16), v, preferred_element_type=jnp.float32)
            for w, v in zip(weights, values)
        ],
    )
    return mixed * (1.0 / total)


def scores_of(q, k):
    return lax.dot_general(q, k, (((1,), (1,)), ((), ())), preferred_element_type=jnp.float32)


def kernel(
    lengths_hbm,
    prompts_hbm,
    probe_hbm,
    q_hbm,
    kv_hbm,
    raw_hbm,
    context,
    advantage,
    lengths,
    prompts,
    probe,
    q,
    kv,
    raw,
    own_a,
    own_b,
    got_a,
    got_b,
    by_prompt_a,
    by_prompt_b,
    out_a,
    out_b,
    all_a,
    all_b,
    row_1,
    row_2,
    lines,
    load_sem,
    ring_send,
    ring_recv,
    send_sem,
    recv_sem,
):
    me = lax.axis_index("resp")
    tp = lax.axis_index("tp")
    zh = lax.div(me, NXY)
    xy = lax.rem(me, NXY)
    x = lax.div(xy, NY)
    y = lax.rem(xy, NY)
    zx = zh * NX + x

    def at_z(step):
        return lax.rem(zh + step, NZ) * NXY + xy

    def at_y(step):
        return zh * NXY + x * NY + lax.rem(y + step, NY)

    def at_x(step):
        return zh * NXY + lax.rem(x + step, NX) * NY + y

    def at_tp(step):
        return lax.rem(tp + step, NT)

    barrier = pltpu.get_barrier_semaphore()

    def greet(device, tp_index):
        pl.semaphore_signal(barrier, inc=1, device_id=(device, tp_index), device_id_type=MESH)

    for i in (2, 6, 1, 7):
        greet(at_y(i), tp)
    for i in (1, 3):
        greet(at_z(i), tp)
    for i in (2, 1, 3):
        greet(at_x(i), tp)
    for i in (2, 3, 1):
        greet(me, at_tp(i))

    load_raw = pltpu.make_async_copy(raw_hbm, raw, load_sem.at[0])
    load_prompts = pltpu.make_async_copy(prompts_hbm, prompts, load_sem.at[1])
    load_rest = [
        pltpu.make_async_copy(src, dst, load_sem.at[2 + n])
        for n, (src, dst) in enumerate(
            ((q_hbm, q), (kv_hbm, kv), (lengths_hbm, lengths), (probe_hbm, probe))
        )
    ]
    load_raw.start()
    load_prompts.start()
    for load in load_rest:
        load.start()

    load_raw.wait()

    def split(p, c):
        k = raw[0, p].astype(jnp.float32)
        v = raw[1, p].astype(jnp.float32)
        for plan, dst in enumerate((own_a, own_b)):
            parts = [
                part[:, (2 * plan + h) * HEAD_DIM : (2 * plan + h + 1) * HEAD_DIM]
                for part in (k, v)
                for h in range(2)
            ]
            dst[p] = jnp.concatenate(parts, axis=0).astype(jnp.bfloat16)
        return c

    lax.fori_loop(0, PROMPTS, split, 0)

    pl.semaphore_wait(barrier, 4 + 2 + (NX - 1) + (NT - 1))

    half = PROMPTS // 2
    lo, hi = pl.ds(0, half), pl.ds(half, half)

    def ring(index, src, dst, device):
        return pltpu.make_async_remote_copy(
            src_ref=src,
            dst_ref=dst,
            send_sem=ring_send.at[index],
            recv_sem=ring_recv.at[index],
            device_id=(device, tp),
            device_id_type=MESH,
        )

    first = [
        ring(0, own_a, got_a.at[0], at_z(1)),
        ring(1, own_a, got_a.at[1], at_z(NZ - 1)),
        ring(2, own_b, got_b.at[2], at_y(2)),
        ring(3, own_b, got_b.at[3], at_y(NY - 2)),
        ring(4, own_b, got_b.at[0], at_y(1)),
        ring(5, own_b, got_b.at[1], at_y(NY - 1)),
    ]
    second = [
        ring(6, got_a.at[0, lo], got_a.at[2, lo], at_z(1)),
        ring(7, got_a.at[1, hi], got_a.at[2, hi], at_z(NZ - 1)),
        ring(8, got_b.at[2, lo], got_b.at[6, lo], at_y(2)),
        ring(9, got_b.at[2], got_b.at[4], at_y(1)),
        ring(10, got_b.at[3, hi], got_b.at[6, hi], at_y(NY - 2)),
        ring(11, got_b.at[3], got_b.at[5], at_y(NY - 1)),
    ]
    for n in (2, 3, 0, 1, 4, 5):
        first[n].start()
    for device in (at_y(2), at_y(NY - 2), at_z(NZ - 1)):
        pl.semaphore_signal(lines.at[2], inc=1, device_id=(device, tp), device_id_type=MESH)
    pl.semaphore_wait(lines.at[2], 3)
    for i in range(1, NX):
        pl.semaphore_signal(lines.at[0], inc=1, device_id=(at_x(i), tp), device_id_type=MESH)
    for i in range(1, NZ):
        pl.semaphore_signal(lines.at[1], inc=1, device_id=(at_z(i), tp), device_id_type=MESH)
    first[2].wait_recv()
    second[2].start()
    second[3].start()
    first[3].wait_recv()
    second[4].start()
    second[5].start()
    first[0].wait_recv()
    second[0].start()
    first[1].wait_recv()
    second[1].start()
    second[0].wait_recv()
    second[1].wait_recv()

    def regroup(own, got, slots, dst):
        def one(p, c):
            tiles = [own[p]] + [got[s, p] for s in range(slots)]
            tiles = [t.astype(jnp.float32) for t in tiles]
            for g in range(PIECES):
                rows = [t[TOKENS * g : TOKENS * (g + 1)] for t in tiles]
                dst[p, g] = jnp.concatenate(rows, axis=0).astype(jnp.bfloat16)
            return c

        def four(i, c):
            for n in range(4):
                one(4 * i + n, c)
            return c

        lax.fori_loop(0, PROMPTS // 4, four, 0)

    def beside_xy(dx, dy):
        return zh * NXY + lax.rem(x + dx, NX) * NY + lax.rem(y + dy, NY)

    def beside_zx(dz, dx):
        return lax.rem(zh + dz, NZ) * NXY + lax.rem(x + dx, NX) * NY + y

    def send(plan, slots, places, by_prompt, out, everyone, mine_at):
        blocks = [by_prompt[prompts[j]] for j in places]
        for i, block in zip(slots, blocks):
            out[i] = block
        for i, j in zip(slots, places):
            pltpu.make_async_remote_copy(
                src_ref=out.at[i],
                dst_ref=everyone.at[mine_at],
                send_sem=send_sem.at[plan],
                recv_sem=recv_sem.at[plan],
                device_id=(j, tp),
                device_id_type=MESH,
            ).start()

    def send_a(low, high):
        places = [beside_xy(*offset) for offset in FAR_XY[low:high]]
        send(0, range(low, high), places, by_prompt_a, out_a, all_a, xy)

    def send_b(low, high):
        places = [beside_zx(*offset) for offset in FAR_ZX[low:high]]
        send(1, range(low, high), places, by_prompt_b, out_b, all_b, zx)

    regroup(own_a, got_a, NZ - 1, by_prompt_a)
    load_prompts.wait()
    pl.semaphore_wait(lines.at[0], NX - 1)
    pl.semaphore_wait(lines.at[1], NZ - 1)

    for low in range(0, NXY // 2, 4):
        send_a(low, low + 4)
    for low in range(NXY // 2, NXY - 1, 5):
        send_a(low, low + 5)
    first[4].wait_recv()
    first[5].wait_recv()
    for copy in second[2:]:
        copy.wait_recv()
    regroup(own_b, got_b, NY - 1, by_prompt_b)

    for low in range(0, NZX - 1, 5):
        send_b(low, low + 5)

    mine = prompts[me]
    all_a[xy] = by_prompt_a[mine]
    all_b[zx] = by_prompt_b[mine]

    for load in load_rest:
        load.wait()
    responses, steps, width = q.shape
    scale2 = math.log2(math.e) / math.sqrt(SCALAR)
    kv_heads = kv.shape[3] // HEAD_DIM
    column = lax.broadcasted_iota(jnp.int32, (8, steps), 1)
    last_q = []
    for r in range(responses):
        pick = (column == lengths[r] - 1).astype(jnp.bfloat16)
        last_q.append(jnp.dot(pick, q[r], preferred_element_type=jnp.float32).astype(jnp.bfloat16))

    def keys_values(g):
        ref = (all_a, all_b)[g // 2]
        h = g % 2
        return (
            ref[:, h].reshape(-1, HEAD_DIM),
            ref[:, 2 + h].reshape(-1, HEAD_DIM),
        )

    def own_keys_values(r, g):
        columns = slice(g * HEAD_DIM, (g + 1) * HEAD_DIM)
        return kv[0, r, :, columns], kv[1, r, :, columns]

    def wait_bytes(ref, sem):
        pltpu.make_async_copy(ref, ref, sem).wait()

    partial = [jnp.zeros((8, HEAD_DIM), jnp.float32) for _ in range(responses)]

    def reward_of(g):
        k, v = keys_values(g)
        heads = (2 * g, 2 * g + 1)
        rows = [
            jnp.concatenate([last[:, h * HEAD_DIM : (h + 1) * HEAD_DIM] for h in heads], axis=0)
            for last in last_q
        ]
        own, own_v = [], []
        for r in range(responses):
            its_k, its_v = own_keys_values(r, g)
            scores = scores_of(rows[r], its_k)
            seen = lax.broadcasted_iota(jnp.int32, scores.shape, 1) < lengths[r]
            own.append(jnp.where(seen, scores, -1e30))
            own_v.append(its_v)
        shared = scores_of(jnp.concatenate(rows, axis=0), k)
        own = jnp.concatenate(own, axis=0)
        top = jnp.maximum(
            jnp.max(shared, axis=1, keepdims=True), jnp.max(own, axis=1, keepdims=True)
        )
        shared = jnp.exp2((shared - top) * scale2)
        own = jnp.exp2((own - top) * scale2)
        total = jnp.sum(shared, axis=1, keepdims=True) + jnp.sum(own, axis=1, keepdims=True)
        own = own.astype(jnp.bfloat16)
        mixed = jnp.dot(shared.astype(jnp.bfloat16), v, preferred_element_type=jnp.float32)
        for r in range(responses):
            low = 16 * r
            part = mixed[low : low + 16] + jnp.dot(
                own[low : low + 16], own_v[r], preferred_element_type=jnp.float32
            )
            part = part * (1.0 / total[low : low + 16])
            part = part.astype(jnp.bfloat16).astype(jnp.float32)
            for n, h in enumerate(heads):
                partial[r] = partial[r] + part[8 * n : 8 * n + 8] * probe[h : h + 1, :]

    def attend(r, g):
        k, v = keys_values(g)
        own_k, own_v = own_keys_values(r, g)
        low = 2 * g * HEAD_DIM
        rows = jnp.concatenate(
            [q[r, :, low : low + HEAD_DIM], q[r, :, low + HEAD_DIM : low + 2 * HEAD_DIM]], axis=0
        )
        own = scores_of(rows, own_k)
        t = lax.broadcasted_iota(jnp.int32, own.shape, 0)
        t = jnp.where(t >= steps, t - steps, t)
        u = lax.broadcasted_iota(jnp.int32, own.shape, 1)
        own = jnp.where(u <= t, own, -1e30)
        mixed = attention([scores_of(rows, k), own], [v, own_v], scale2)
        live = lax.broadcasted_iota(jnp.int32, (steps, HEAD_DIM), 0) < lengths[r]
        for n in range(2):
            part = jnp.where(live, mixed[n * steps : (n + 1) * steps], 0.0)
            context[r, :, low + n * HEAD_DIM : low + (n + 1) * HEAD_DIM] = part.astype(jnp.bfloat16)

    wait_bytes(all_a.at[pl.ds(0, NXY - 1)], recv_sem.at[0])
    for g in range(2):
        reward_of(g)

    wait_bytes(all_b.at[pl.ds(0, NZX - 1)], recv_sem.at[1])
    for g in range(2, kv_heads):
        reward_of(g)

    lane = lax.broadcasted_iota(jnp.int32, (1, HEAD_DIM), 1)
    sums = [jnp.sum(part[0:1], axis=1, keepdims=True) for part in partial]
    row = jnp.where(lane == mine, sums[0] + sums[1], 0.0)
    for r in range(responses):
        row = jnp.where(lane == PROMPTS + r, sums[r], row)

    zt = zh * NT + tp
    rounds = (
        (row_1, zt, [(at_z(dz), at_tp(dt)) for dz, dt in FAR_ZT]),
        (row_2, xy, [(beside_xy(*offset), tp) for offset in FAR_XY]),
    )

    def send_row(n, row):
        ref, slot, devices = rounds[n]
        ref[slot] = row
        for device in devices:
            pltpu.make_async_remote_copy(
                src_ref=ref.at[slot],
                dst_ref=ref.at[slot],
                send_sem=send_sem.at[2 + n],
                recv_sem=recv_sem.at[2 + n],
                device_id=device,
                device_id_type=MESH,
            ).start()

    def wait_rows(n):
        ref, _, devices = rounds[n]
        wait_bytes(ref.at[pl.ds(0, len(devices))], recv_sem.at[2 + n])

    send_row(0, row)
    for g in range(2):
        for r in range(responses):
            attend(r, g)
    wait_rows(0)
    rewards = jnp.sum(row_1[pl.ds(zh * NT, NT)], axis=0)
    send_row(1, jnp.sum(row_1[...], axis=0))
    for g in range(2, kv_heads):
        for r in range(responses):
            attend(r, g)
    wait_rows(1)
    table = jnp.sum(row_2[...], axis=0)
    group = jnp.sum(jnp.where(lane == mine, table, 0.0), axis=1, keepdims=True) / BEST
    advantage[...] = rewards - group

    for copy in first:
        copy.wait_send()
    for copy in second:
        copy.wait_send()
    wait_bytes(out_a.at[pl.ds(0, NXY - 1)], send_sem.at[0])
    wait_bytes(out_b.at[pl.ds(0, NZX - 1)], send_sem.at[1])
    for n, (ref, _, devices) in enumerate(rounds):
        wait_bytes(ref.at[pl.ds(0, len(devices))], send_sem.at[2 + n])


def shards(response_queries, response_kv, prompt_kv, response_lengths, device_prompt, probe_weight):
    bf16 = jnp.bfloat16
    vmem = pl.BlockSpec(memory_space=pltpu.VMEM)
    anywhere = pl.BlockSpec(memory_space=pl.ANY)
    in_hbm = functools.partial(pltpu.with_memory_space_constraint, memory_space=pltpu.HBM)
    block = (PROMPTS, ROWS, HEAD_DIM)
    context, advantage = pl.pallas_call(
        kernel,
        out_shape=(
            pltpu.VMEM(response_queries.shape, bf16),
            pltpu.VMEM((1, HEAD_DIM), jnp.float32),
        ),
        in_specs=[anywhere] * 6,
        out_specs=(vmem, vmem),
        scratch_shapes=[
            pltpu.SMEM(response_lengths.shape, jnp.int32),
            pltpu.SMEM(device_prompt.shape, jnp.int32),
            pltpu.VMEM((probe_weight.shape[0] // HEAD_DIM, HEAD_DIM), jnp.float32),
            pltpu.VMEM(response_queries.shape, bf16),
            pltpu.VMEM(response_kv.shape, bf16),
            pltpu.VMEM(prompt_kv.shape, bf16),
            pltpu.VMEM(block, bf16),
            pltpu.VMEM(block, bf16),
            pltpu.VMEM((NZ - 1,) + block, bf16),
            pltpu.VMEM((NY - 1,) + block, bf16),
            pltpu.VMEM((PROMPTS, PIECES, NZ * TOKENS, HEAD_DIM), bf16),
            pltpu.VMEM((PROMPTS, PIECES, NY * TOKENS, HEAD_DIM), bf16),
            pltpu.VMEM((NXY, PIECES, NZ * TOKENS, HEAD_DIM), bf16),
            pltpu.VMEM((NZX, PIECES, NY * TOKENS, HEAD_DIM), bf16),
            pltpu.VMEM((NXY, PIECES, NZ * TOKENS, HEAD_DIM), bf16),
            pltpu.VMEM((NZX, PIECES, NY * TOKENS, HEAD_DIM), bf16),
            pltpu.VMEM((NZ * NT, 1, HEAD_DIM), jnp.float32),
            pltpu.VMEM((NXY, 1, HEAD_DIM), jnp.float32),
            pltpu.SemaphoreType.REGULAR((3,)),
            pltpu.SemaphoreType.DMA((6,)),
            pltpu.SemaphoreType.DMA((12,)),
            pltpu.SemaphoreType.DMA((12,)),
            pltpu.SemaphoreType.DMA((4,)),
            pltpu.SemaphoreType.DMA((4,)),
        ],
        compiler_params=pltpu.CompilerParams(
            collective_id=0, has_side_effects=True, vmem_limit_bytes=48 * 1024 * 1024
        ),
        cost_estimate=pl.CostEstimate(
            flops=700_000_000, bytes_accessed=2_000_000, transcendentals=1_400_000
        ),
    )(
        in_hbm(response_lengths),
        in_hbm(device_prompt),
        in_hbm(probe_weight.reshape(-1, HEAD_DIM)),
        in_hbm(response_queries),
        in_hbm(response_kv),
        in_hbm(prompt_kv),
    )
    return context, advantage[0, PROMPTS : PROMPTS + response_lengths.shape[0]]


def solution(mesh):
    placed = (
        P("resp", None, "tp"),
        P(None, "resp", None, "tp"),
        P(None, None, "resp", "tp"),
        P("resp"),
        P(),
        P("tp"),
    )
    return jax.shard_map(
        shards,
        mesh=mesh,
        in_specs=placed,
        out_specs=(P("resp", None, "tp"), P("resp")),
        check_vma=False,
    )
```

```python
import functools
import math

import jax
import jax.numpy as jnp
from jax import lax
from jax.experimental import pallas as pl
from jax.experimental.pallas import tpu as pltpu
from jax.sharding import PartitionSpec as P

HEAD_DIM = 128
SCALAR = 144
BEST = 16
MESH = pl.DeviceIdType.MESH

NZ, NX, NY, NT = 4, 4, 8, 4
NXY, NZX = NX * NY, NZ * NX
PROMPTS = 16
TOKENS = 4
PIECES = 4
ROWS = PIECES * TOKENS


def far_first(first, second):
    places = [(a, b) for a in range(first[0]) for b in range(second[0]) if (a, b) != (0, 0)]
    hops = lambda n, step: min(n[0] - step, step) * n[1]
    return sorted(places, key=lambda p: (-hops(first, p[0]) - hops(second, p[1]), p))


FAR_XY = far_first((NX, 1), (NY, 1))
FAR_ZX = far_first((NZ, 2), (NX, 1))
FAR_ZT = far_first((NZ, 2), (NT, 1))


def attention(scores_parts, values, scale2):
    top = functools.reduce(jnp.maximum, [jnp.max(s, axis=1, keepdims=True) for s in scores_parts])
    weights = [jnp.exp2((s - top) * scale2) for s in scores_parts]
    total = functools.reduce(jnp.add, [jnp.sum(w, axis=1, keepdims=True) for w in weights])
    mixed = functools.reduce(
        jnp.add,
        [
            jnp.dot(w.astype(jnp.bfloat16), v, preferred_element_type=jnp.float32)
            for w, v in zip(weights, values)
        ],
    )
    return mixed * (1.0 / total)


def scores_of(q, k):
    return lax.dot_general(q, k, (((1,), (1,)), ((), ())), preferred_element_type=jnp.float32)


def kernel(
    lengths_hbm,
    prompts_hbm,
    probe_hbm,
    q_hbm,
    kv_hbm,
    raw_hbm,
    context,
    advantage,
    lengths,
    prompts,
    probe,
    q,
    kv,
    raw,
    own_a,
    own_b,
    got_a,
    got_b,
    by_prompt_a,
    by_prompt_b,
    out_a,
    out_b,
    all_a,
    all_b,
    row_1,
    row_2,
    lines,
    load_sem,
    ring_send,
    ring_recv,
    send_sem,
    recv_sem,
):
    me = lax.axis_index("resp")
    tp = lax.axis_index("tp")
    zh = lax.div(me, NXY)
    xy = lax.rem(me, NXY)
    x = lax.div(xy, NY)
    y = lax.rem(xy, NY)
    zx = zh * NX + x

    def at_z(step):
        return lax.rem(zh + step, NZ) * NXY + xy

    def at_y(step):
        return zh * NXY + x * NY + lax.rem(y + step, NY)

    def at_x(step):
        return zh * NXY + lax.rem(x + step, NX) * NY + y

    def at_tp(step):
        return lax.rem(tp + step, NT)

    barrier = pltpu.get_barrier_semaphore()

    def greet(device, tp_index):
        pl.semaphore_signal(barrier, inc=1, device_id=(device, tp_index), device_id_type=MESH)

    for i in (2, 6, 1, 7):
        greet(at_y(i), tp)
    for i in (1, 3):
        greet(at_z(i), tp)
    for i in (2, 1, 3):
        greet(at_x(i), tp)
    for i in (2, 3, 1):
        greet(me, at_tp(i))

    load_raw = pltpu.make_async_copy(raw_hbm, raw, load_sem.at[0])
    load_prompts = pltpu.make_async_copy(prompts_hbm, prompts, load_sem.at[1])
    load_rest = [
        pltpu.make_async_copy(src, dst, load_sem.at[2 + n])
        for n, (src, dst) in enumerate(
            ((q_hbm, q), (kv_hbm, kv), (lengths_hbm, lengths), (probe_hbm, probe))
        )
    ]
    load_raw.start()
    load_prompts.start()
    for load in load_rest:
        load.start()

    load_raw.wait()

    def split(p, c):
        k = raw[0, p].astype(jnp.float32)
        v = raw[1, p].astype(jnp.float32)
        for plan, dst in enumerate((own_a, own_b)):
            parts = [
                part[:, (2 * plan + h) * HEAD_DIM : (2 * plan + h + 1) * HEAD_DIM]
                for part in (k, v)
                for h in range(2)
            ]
            dst[p] = jnp.concatenate(parts, axis=0).astype(jnp.bfloat16)
        return c

    def split_four(i, c):
        for n in range(4):
            split(4 * i + n, c)
        return c

    lax.fori_loop(0, PROMPTS // 4, split_four, 0)

    pl.semaphore_wait(barrier, 4 + 2 + (NX - 1) + (NT - 1))

    half = PROMPTS // 2
    lo, hi = pl.ds(0, half), pl.ds(half, half)

    def ring(index, src, dst, device):
        return pltpu.make_async_remote_copy(
            src_ref=src,
            dst_ref=dst,
            send_sem=ring_send.at[index],
            recv_sem=ring_recv.at[index],
            device_id=(device, tp),
            device_id_type=MESH,
        )

    first = [
        ring(0, own_a, got_a.at[0], at_z(1)),
        ring(1, own_a, got_a.at[1], at_z(NZ - 1)),
        ring(2, own_b, got_b.at[2], at_y(2)),
        ring(3, own_b, got_b.at[3], at_y(NY - 2)),
        ring(4, own_b, got_b.at[0], at_y(1)),
        ring(5, own_b, got_b.at[1], at_y(NY - 1)),
    ]
    second = [
        ring(6, got_a.at[0, lo], got_a.at[2, lo], at_z(1)),
        ring(7, got_a.at[1, hi], got_a.at[2, hi], at_z(NZ - 1)),
        ring(8, got_b.at[2, lo], got_b.at[6, lo], at_y(2)),
        ring(9, got_b.at[2], got_b.at[4], at_y(1)),
        ring(10, got_b.at[3, hi], got_b.at[6, hi], at_y(NY - 2)),
        ring(11, got_b.at[3], got_b.at[5], at_y(NY - 1)),
    ]
    for n in (2, 3, 0, 1, 4, 5):
        first[n].start()
    for device in (at_y(2), at_y(NY - 2), at_z(NZ - 1)):
        pl.semaphore_signal(lines.at[2], inc=1, device_id=(device, tp), device_id_type=MESH)
    pl.semaphore_wait(lines.at[2], 3)
    for i in range(1, NX):
        pl.semaphore_signal(lines.at[0], inc=1, device_id=(at_x(i), tp), device_id_type=MESH)
    for i in range(1, NZ):
        pl.semaphore_signal(lines.at[1], inc=1, device_id=(at_z(i), tp), device_id_type=MESH)
    first[2].wait_recv()
    second[2].start()
    second[3].start()
    first[3].wait_recv()
    second[4].start()
    second[5].start()
    first[0].wait_recv()
    second[0].start()
    first[1].wait_recv()
    second[1].start()
    second[0].wait_recv()
    second[1].wait_recv()

    def regroup(own, got, slots, dst):
        def one(p, c):
            tiles = [own[p]] + [got[s, p] for s in range(slots)]
            tiles = [t.astype(jnp.float32) for t in tiles]
            for g in range(PIECES):
                rows = [t[TOKENS * g : TOKENS * (g + 1)] for t in tiles]
                dst[p, g] = jnp.concatenate(rows, axis=0).astype(jnp.bfloat16)
            return c

        def four(i, c):
            for n in range(4):
                one(4 * i + n, c)
            return c

        lax.fori_loop(0, PROMPTS // 4, four, 0)

    def beside_xy(dx, dy):
        return zh * NXY + lax.rem(x + dx, NX) * NY + lax.rem(y + dy, NY)

    def beside_zx(dz, dx):
        return lax.rem(zh + dz, NZ) * NXY + lax.rem(x + dx, NX) * NY + y

    def send(plan, slots, places, by_prompt, out, everyone, mine_at):
        blocks = [by_prompt[prompts[j]] for j in places]
        for i, block in zip(slots, blocks):
            out[i] = block
        for i, j in zip(slots, places):
            pltpu.make_async_remote_copy(
                src_ref=out.at[i],
                dst_ref=everyone.at[mine_at],
                send_sem=send_sem.at[plan],
                recv_sem=recv_sem.at[plan],
                device_id=(j, tp),
                device_id_type=MESH,
            ).start()

    def send_a(low, high):
        places = [beside_xy(*offset) for offset in FAR_XY[low:high]]
        send(0, range(low, high), places, by_prompt_a, out_a, all_a, xy)

    def send_b(low, high):
        places = [beside_zx(*offset) for offset in FAR_ZX[low:high]]
        send(1, range(low, high), places, by_prompt_b, out_b, all_b, zx)

    regroup(own_a, got_a, NZ - 1, by_prompt_a)
    load_prompts.wait()
    pl.semaphore_wait(lines.at[0], NX - 1)
    pl.semaphore_wait(lines.at[1], NZ - 1)

    for low in range(0, NXY // 2, 4):
        send_a(low, low + 4)
    for low in range(NXY // 2, NXY - 1, 5):
        send_a(low, low + 5)
    first[4].wait_recv()
    first[5].wait_recv()
    for copy in second[2:]:
        copy.wait_recv()
    regroup(own_b, got_b, NY - 1, by_prompt_b)

    for low in range(0, NZX - 1, 5):
        send_b(low, low + 5)

    mine = prompts[me]
    all_a[xy] = by_prompt_a[mine]
    all_b[zx] = by_prompt_b[mine]

    for load in load_rest:
        load.wait()
    responses, steps, width = q.shape
    scale2 = math.log2(math.e) / math.sqrt(SCALAR)
    kv_heads = kv.shape[3] // HEAD_DIM
    column = lax.broadcasted_iota(jnp.int32, (8, steps), 1)
    last_q = []
    for r in range(responses):
        pick = (column == lengths[r] - 1).astype(jnp.bfloat16)
        last_q.append(jnp.dot(pick, q[r], preferred_element_type=jnp.float32).astype(jnp.bfloat16))

    def keys_values(g):
        ref = (all_a, all_b)[g // 2]
        h = g % 2
        return (
            ref[:, h].reshape(-1, HEAD_DIM),
            ref[:, 2 + h].reshape(-1, HEAD_DIM),
        )

    def own_keys_values(r, g):
        columns = slice(g * HEAD_DIM, (g + 1) * HEAD_DIM)
        return kv[0, r, :, columns], kv[1, r, :, columns]

    def wait_bytes(ref, sem):
        pltpu.make_async_copy(ref, ref, sem).wait()

    partial = [jnp.zeros((8, HEAD_DIM), jnp.float32) for _ in range(responses)]

    def reward_of(g):
        k, v = keys_values(g)
        heads = (2 * g, 2 * g + 1)
        rows = [
            jnp.concatenate([last[:, h * HEAD_DIM : (h + 1) * HEAD_DIM] for h in heads], axis=0)
            for last in last_q
        ]
        own, own_v = [], []
        for r in range(responses):
            its_k, its_v = own_keys_values(r, g)
            scores = scores_of(rows[r], its_k)
            seen = lax.broadcasted_iota(jnp.int32, scores.shape, 1) < lengths[r]
            own.append(jnp.where(seen, scores, -1e30))
            own_v.append(its_v)
        shared = scores_of(jnp.concatenate(rows, axis=0), k)
        own = jnp.concatenate(own, axis=0)
        top = jnp.maximum(
            jnp.max(shared, axis=1, keepdims=True), jnp.max(own, axis=1, keepdims=True)
        )
        shared = jnp.exp2((shared - top) * scale2)
        own = jnp.exp2((own - top) * scale2)
        total = jnp.sum(shared, axis=1, keepdims=True) + jnp.sum(own, axis=1, keepdims=True)
        own = own.astype(jnp.bfloat16)
        mixed = jnp.dot(shared.astype(jnp.bfloat16), v, preferred_element_type=jnp.float32)
        for r in range(responses):
            low = 16 * r
            part = mixed[low : low + 16] + jnp.dot(
                own[low : low + 16], own_v[r], preferred_element_type=jnp.float32
            )
            part = part * (1.0 / total[low : low + 16])
            part = part.astype(jnp.bfloat16).astype(jnp.float32)
            for n, h in enumerate(heads):
                partial[r] = partial[r] + part[8 * n : 8 * n + 8] * probe[h : h + 1, :]

    def attend(r, g):
        k, v = keys_values(g)
        own_k, own_v = own_keys_values(r, g)
        low = 2 * g * HEAD_DIM
        rows = jnp.concatenate(
            [q[r, :, low : low + HEAD_DIM], q[r, :, low + HEAD_DIM : low + 2 * HEAD_DIM]], axis=0
        )
        own = scores_of(rows, own_k)
        t = lax.broadcasted_iota(jnp.int32, own.shape, 0)
        t = jnp.where(t >= steps, t - steps, t)
        u = lax.broadcasted_iota(jnp.int32, own.shape, 1)
        own = jnp.where(u <= t, own, -1e30)
        mixed = attention([scores_of(rows, k), own], [v, own_v], scale2)
        live = lax.broadcasted_iota(jnp.int32, (steps, HEAD_DIM), 0) < lengths[r]
        for n in range(2):
            part = jnp.where(live, mixed[n * steps : (n + 1) * steps], 0.0)
            context[r, :, low + n * HEAD_DIM : low + (n + 1) * HEAD_DIM] = part.astype(jnp.bfloat16)

    wait_bytes(all_a.at[pl.ds(0, NXY - 1)], recv_sem.at[0])
    for g in range(2):
        reward_of(g)

    wait_bytes(all_b.at[pl.ds(0, NZX - 1)], recv_sem.at[1])
    for g in range(2, kv_heads):
        reward_of(g)

    lane = lax.broadcasted_iota(jnp.int32, (1, HEAD_DIM), 1)
    sums = [jnp.sum(part[0:1], axis=1, keepdims=True) for part in partial]
    row = jnp.where(lane == mine, sums[0] + sums[1], 0.0)
    for r in range(responses):
        row = jnp.where(lane == PROMPTS + r, sums[r], row)

    zt = zh * NT + tp
    rounds = (
        (row_1, zt, [(at_z(dz), at_tp(dt)) for dz, dt in FAR_ZT]),
        (row_2, xy, [(beside_xy(*offset), tp) for offset in FAR_XY]),
    )

    def send_row(n, row):
        ref, slot, devices = rounds[n]
        ref[slot] = row
        for device in devices:
            pltpu.make_async_remote_copy(
                src_ref=ref.at[slot],
                dst_ref=ref.at[slot],
                send_sem=send_sem.at[2 + n],
                recv_sem=recv_sem.at[2 + n],
                device_id=device,
                device_id_type=MESH,
            ).start()

    def wait_rows(n):
        ref, _, devices = rounds[n]
        wait_bytes(ref.at[pl.ds(0, len(devices))], recv_sem.at[2 + n])

    send_row(0, row)
    for g in range(2):
        for r in range(responses):
            attend(r, g)
    wait_rows(0)
    rewards = jnp.sum(row_1[pl.ds(zh * NT, NT)], axis=0)
    send_row(1, jnp.sum(row_1[...], axis=0))
    for g in range(2, kv_heads):
        for r in range(responses):
            attend(r, g)
    wait_rows(1)
    table = jnp.sum(row_2[...], axis=0)
    group = jnp.sum(jnp.where(lane == mine, table, 0.0), axis=1, keepdims=True) / BEST
    advantage[...] = rewards - group

    for copy in first:
        copy.wait_send()
    for copy in second:
        copy.wait_send()
    wait_bytes(out_a.at[pl.ds(0, NXY - 1)], send_sem.at[0])
    wait_bytes(out_b.at[pl.ds(0, NZX - 1)], send_sem.at[1])
    for n, (ref, _, devices) in enumerate(rounds):
        wait_bytes(ref.at[pl.ds(0, len(devices))], send_sem.at[2 + n])


def shards(response_queries, response_kv, prompt_kv, response_lengths, device_prompt, probe_weight):
    bf16 = jnp.bfloat16
    vmem = pl.BlockSpec(memory_space=pltpu.VMEM)
    anywhere = pl.BlockSpec(memory_space=pl.ANY)
    in_hbm = functools.partial(pltpu.with_memory_space_constraint, memory_space=pltpu.HBM)
    block = (PROMPTS, ROWS, HEAD_DIM)
    context, advantage = pl.pallas_call(
        kernel,
        out_shape=(
            pltpu.VMEM(response_queries.shape, bf16),
            pltpu.VMEM((1, HEAD_DIM), jnp.float32),
        ),
        in_specs=[anywhere] * 6,
        out_specs=(vmem, vmem),
        scratch_shapes=[
            pltpu.SMEM(response_lengths.shape, jnp.int32),
            pltpu.SMEM(device_prompt.shape, jnp.int32),
            pltpu.VMEM((probe_weight.shape[0] // HEAD_DIM, HEAD_DIM), jnp.float32),
            pltpu.VMEM(response_queries.shape, bf16),
            pltpu.VMEM(response_kv.shape, bf16),
            pltpu.VMEM(prompt_kv.shape, bf16),
            pltpu.VMEM(block, bf16),
            pltpu.VMEM(block, bf16),
            pltpu.VMEM((NZ - 1,) + block, bf16),
            pltpu.VMEM((NY - 1,) + block, bf16),
            pltpu.VMEM((PROMPTS, PIECES, NZ * TOKENS, HEAD_DIM), bf16),
            pltpu.VMEM((PROMPTS, PIECES, NY * TOKENS, HEAD_DIM), bf16),
            pltpu.VMEM((NXY, PIECES, NZ * TOKENS, HEAD_DIM), bf16),
            pltpu.VMEM((NZX, PIECES, NY * TOKENS, HEAD_DIM), bf16),
            pltpu.VMEM((NXY, PIECES, NZ * TOKENS, HEAD_DIM), bf16),
            pltpu.VMEM((NZX, PIECES, NY * TOKENS, HEAD_DIM), bf16),
            pltpu.VMEM((NZ * NT, 1, HEAD_DIM), jnp.float32),
            pltpu.VMEM((NXY, 1, HEAD_DIM), jnp.float32),
            pltpu.SemaphoreType.REGULAR((3,)),
            pltpu.SemaphoreType.DMA((6,)),
            pltpu.SemaphoreType.DMA((12,)),
            pltpu.SemaphoreType.DMA((12,)),
            pltpu.SemaphoreType.DMA((4,)),
            pltpu.SemaphoreType.DMA((4,)),
        ],
        compiler_params=pltpu.CompilerParams(
            collective_id=0, has_side_effects=True, vmem_limit_bytes=48 * 1024 * 1024
        ),
        cost_estimate=pl.CostEstimate(
            flops=700_000_000, bytes_accessed=2_000_000, transcendentals=1_400_000
        ),
    )(
        in_hbm(response_lengths),
        in_hbm(device_prompt),
        in_hbm(probe_weight.reshape(-1, HEAD_DIM)),
        in_hbm(response_queries),
        in_hbm(response_kv),
        in_hbm(prompt_kv),
    )
    return context, advantage[0, PROMPTS : PROMPTS + response_lengths.shape[0]]


def solution(mesh):
    placed = (
        P("resp", None, "tp"),
        P(None, "resp", None, "tp"),
        P(None, None, "resp", "tp"),
        P("resp"),
        P(),
        P("tp"),
    )
    return jax.shard_map(
        shards,
        mesh=mesh,
        in_specs=placed,
        out_specs=(P("resp", None, "tp"), P("resp")),
        check_vma=False,
    )
```
